32 devices in a mesh: body: 4 (over y, core), blk: 8 (over z, x).
Axes of the slice: x: 2, y: 2, z: 4, core: 2. Of those that a mesh axis runs over, the one named last changes fastest.
Arguments:
- psi_init: float32 [16384, 320], P(('body', 'blk')), may hold values from -6 to 6
- source: float32 [16384, 320], P(('body', 'blk'))
- coupling: bfloat16 [16384, 6, 5, 320], P(('body', 'blk')), may hold values from -0.59765625 to 0.59765625
- diag_inv: bfloat16 [16384, 5, 320], P(('body', 'blk')), as said below
- neighbours: int32 [16384, 6], P(('body', 'blk')), may hold values from 0 to 527, as said below
- seam_perm: int32 [4, 8], P('body'), may hold values from 0 to 7, each once within a row
- fringe_src: int32 [32, 256], P(('body', 'blk')), may hold values from 0 to 511
- fringe_dst: int32 [32, 256], P(('body', 'blk')), may hold values from 0 to 511, as said below
- fringe_weight: float32 [32, 256], P(('body', 'blk')), may hold values from 0.2 to 1
Outputs:
- adjoint: float32 [16384, 320], P(('body', 'blk'))
- residual: float32 [16384, 320], P(('body', 'blk'))
The draws below stay inside these ranges and needn't reach their ends.
Inputs may be any that keep to these rules, and one draw needn't show every extreme that they name: neighbours[i, m] - 8 - (i mod 512) lies in -8 .. 8. `fringe_dst`: every slot names a receiver block. `diag_inv`: each per-cell 5 x 5 matrix has a positive diagonal.
All inputs are finite; a program needn't handle non-finite values.
Results may differ from the reference program's by a relative error of at most 0.0003.
Values sent between devices are 32-bit elements; how exact they have to be, the bound alone decides.
No kernel may reach another device: no remote copies, remote signals or barrier semaphores. Data moves between devices by JAX's collectives and lax.ppermute only.
A program may use at most 128 MiB of HBM per device.

```python
import math
import jax
import jax.numpy as jnp
from jax import lax

CELLS = 64
VARS = 5
BW = 320
NB = 512
K = 6
HB = 8
CAP = 8
STEPS = 2
NBT = 16384
N_BODY = 4
N_BLK = 8
DEVICES = 32


def draw_source(key, part):
    rows = jnp.arange(NBT, dtype=jnp.int32)[:, None]
    device = (rows // NB).astype(jnp.float32)
    scale = 1.5 * (1.0 + 2.0 * device / max(DEVICES - 1, 1))
    base = jnp.clip(jax.random.normal(jax.random.fold_in(key, 1), (NBT, BW), jnp.float32), -6.0, 6.0)
    return base * scale


def draw_diag_inv(key, part):
    upper = jnp.arange(VARS, dtype=jnp.int32)[None, :, None]
    lower = (jnp.arange(BW, dtype=jnp.int32) // CELLS)[None, None, :]
    diag = jnp.exp(jax.random.uniform(jax.random.fold_in(key, 1), (NBT, VARS, BW), jnp.float32, math.log(0.6), math.log(1.2)))
    off = jnp.clip(0.15 * jax.random.normal(jax.random.fold_in(key, 2), (NBT, VARS, BW), jnp.float32), -0.6, 0.6)
    return jnp.where(upper == lower, diag, off).astype(jnp.bfloat16)


def draw_neighbours(key, part):
    offset = jax.random.randint(jax.random.fold_in(key, 1), (NBT, K), -HB, HB + 1)
    local = (jnp.arange(NBT, dtype=jnp.int32) % NB)[:, None]
    slot = jnp.arange(K, dtype=jnp.int32)[None, :]
    offset = jnp.where((local == NB - 1) & (slot == 0), HB, offset)
    offset = jnp.where((local == 0) & (slot == 0), -HB, offset)
    return (local + HB + offset).astype(jnp.int32)


def draw_fringe_dst(key, part):
    cols = jnp.arange(DEVICES * CAP, dtype=jnp.int32)[None, :]
    values = jax.random.randint(jax.random.fold_in(key, 1), (DEVICES, DEVICES * CAP), 0, NB)
    values = jnp.where(cols == 0, NB - 1, values)
    return values.astype(jnp.int32)


def plant(drawn, own_key, smallest, largest):
    spot = [jax.random.randint(jax.random.fold_in(own_key, axis), (), 0, length) for axis, length in enumerate(drawn.shape)]
    main_axis = drawn.shape.index(max(drawn.shape))
    beside = spot[:main_axis] + [(spot[main_axis] + 1) % drawn.shape[main_axis]] + spot[main_axis + 1:]
    return drawn.at[tuple(spot)].set(smallest).at[tuple(beside)].set(largest)


def levels(key, extent, shards, smallest, top_value):
    def one(axis_at, parts):
        steps = jax.random.uniform(jax.random.fold_in(jax.random.fold_in(key, 6), axis_at), (parts,), jnp.float32, smallest / len(shards), top_value / len(shards))
        return jnp.repeat(jnp.exp(steps), extent[axis_at] // parts).reshape((-1,) + (1,) * (len(extent) - axis_at - 1))

    gain = one(*shards[0])
    for cut in shards[1:]:
        gain = gain * one(*cut)
    return gain


def bell_draw(key, shape, deviation, limit, shards=(), kind=jnp.bfloat16):
    factor_of = levels(key, shape, shards, -0.22, 0.18) if shards else 1.0
    array = jax.random.normal(key, shape, jnp.float32) * deviation * factor_of
    return jnp.minimum(jnp.maximum(array, -limit), limit).astype(kind)


def setup_inputs(seed: int = 0) -> dict:
    key_of = jax.random.split(jax.random.key(seed), 10)
    return {
        "psi_init": bell_draw(key_of[0], (NBT, BW), 1.0, 6.0, ((0, 32),), jnp.float32),
        "source": draw_source(jax.random.fold_in(key_of[9], 71), 0),
        "coupling": bell_draw(key_of[2], (NBT, K, VARS, BW), 0.12, 0.59765625, ((0, 32),)),
        "diag_inv": draw_diag_inv(jax.random.fold_in(key_of[9], 71), 0),
        "neighbours": draw_neighbours(jax.random.fold_in(key_of[9], 71), 0),
        "seam_perm": jax.vmap(lambda own: jax.random.permutation(own, HB))(jax.random.split(key_of[5], N_BODY)).reshape((N_BODY, HB)).astype(jnp.int32),
        "fringe_src": plant(jax.random.randint(key_of[6], (DEVICES, DEVICES * CAP), 0, NB), jax.random.fold_in(key_of[6], 1), 0, NB - 1).astype(jnp.int32),
        "fringe_dst": draw_fringe_dst(jax.random.fold_in(key_of[9], 71), 0),
        "fringe_weight": jnp.clip(0.2 + 0.8 * jax.random.uniform(key_of[8], (DEVICES, DEVICES * CAP), jnp.float32) ** levels(key_of[8], (DEVICES, DEVICES * CAP), ((0, 32),), -0.2, 0.2), 0.2, 1.0),
    }


step_cfl = 0.5

def rotate(block, sign):
    first = block[:, 2 * CELLS:3 * CELLS]
    second = block[:, 3 * CELLS:4 * CELLS]
    cosine = math.cos(2.0 * math.pi / 3.0)
    sine = sign * math.sin(2.0 * math.pi / 3.0)
    return jnp.concatenate([block[:, :2 * CELLS], cosine * first - sine * second, sine * first + cosine * second, block[:, 4 * CELLS:]], axis=1)

def couple(args):
    extended, nbr, coup = args
    near = extended[nbr]
    prod = coup.astype(jnp.float32) * near[:, :, None, :]
    prod = lax.optimization_barrier(jnp.sum(prod, axis=1)).reshape(NB, VARS, VARS, CELLS)
    return lax.optimization_barrier(jnp.sum(prod, axis=2)).reshape(NB, BW)

def precondition(args):
    dinv, resid = args
    prod = (dinv.astype(jnp.float32) * resid[:, None, :]).reshape(NB, VARS, VARS, CELLS)
    return lax.optimization_barrier(jnp.sum(prod, axis=2)).reshape(NB, BW)

def fringe_add(args):
    dst, weight, received = args
    table = (dst[None, :] == jnp.arange(NB, dtype=jnp.int32)[:, None]).astype(jnp.float32) * weight[None, :]
    return jnp.dot(table, received, precision=lax.Precision.HIGHEST)

def operator(psi, source, coupling, neighbours, seam_perm, fringe_src, fringe_dst, fringe_weight):
    grid = psi.reshape(N_BODY, N_BLK, NB, BW)
    lower = jnp.roll(grid[:, :, NB - HB:], 1, axis=1)
    upper = jnp.roll(grid[:, :, :HB], -1, axis=1)
    onehot = (seam_perm[:, :, None] == jnp.arange(HB, dtype=jnp.int32)[None, None, :]).astype(jnp.float32)
    seam_lo = jnp.einsum('bji,bic->bjc', onehot, lower[:, 0], precision=lax.Precision.HIGHEST)
    seam_hi = jnp.einsum('bji,bjc->bic', onehot, upper[:, N_BLK - 1], precision=lax.Precision.HIGHEST)
    seam_lo = rotate(seam_lo.reshape(N_BODY * HB, BW), 1.0).reshape(N_BODY, HB, BW)
    seam_hi = rotate(seam_hi.reshape(N_BODY * HB, BW), -1.0).reshape(N_BODY, HB, BW)
    lower = lower.at[:, 0].set(seam_lo)
    upper = upper.at[:, N_BLK - 1].set(seam_hi)
    extended = jnp.concatenate([lower, grid, upper], axis=2).reshape(DEVICES, NB + 2 * HB, BW)
    coupled = lax.map(couple, (extended, neighbours.reshape(DEVICES, NB, K), coupling.reshape(DEVICES, NB, K, VARS, BW)))
    psi_dev = psi.reshape(DEVICES, NB, BW)
    sent = jnp.take_along_axis(psi_dev, fringe_src[:, :, None], axis=1)
    received = sent.reshape(DEVICES, DEVICES, CAP, BW).transpose(1, 0, 2, 3).reshape(DEVICES, DEVICES * CAP, BW)
    fringe = lax.map(fringe_add, (fringe_dst, fringe_weight, received))
    return source - psi + coupled.reshape(NBT, BW) + fringe.reshape(NBT, BW)

def reference(psi_init, source, coupling, diag_inv, neighbours, seam_perm, fringe_src, fringe_dst, fringe_weight):
    psi = psi_init
    first_norm = None
    resid = psi
    for step in range(STEPS):
        resid = operator(psi, source, coupling, neighbours, seam_perm, fringe_src, fringe_dst, fringe_weight)
        norm_now = jnp.sum(resid * resid) / (NBT * BW) + 1e-06
        if first_norm is None:
            first_norm = norm_now
        cfl = step_cfl * jnp.sqrt(first_norm / norm_now)
        update = lax.map(precondition, (diag_inv.reshape(DEVICES, NB, VARS, BW), resid.reshape(DEVICES, NB, BW)))
        psi = psi + cfl * update.reshape(NBT, BW)
    return (psi, resid)
```

```python
import functools
import math

import jax
import jax.numpy as jnp
from jax import lax
from jax.experimental import pallas as pl
from jax.experimental.pallas import tpu as pltpu
from jax.sharding import PartitionSpec as P

CELLS = 64
VARS = 5
BW = 320
STEP_CFL = 0.5
LANES = 128
PACK = 16
VMEM_LIMIT = 40 * 1024 * 1024


def split(x):
    high = x.astype(jnp.bfloat16)
    return high, (x - high.astype(jnp.float32)).astype(jnp.bfloat16)


def onehot(mask):
    return jnp.where(mask, 1.0, 0.0).astype(jnp.bfloat16)


def pick(x, table):
    high, low = split(x)
    return jnp.dot(high, table, preferred_element_type=jnp.float32) + jnp.dot(
        low, table, preferred_element_type=jnp.float32
    )


def send_blocks(x, src, perm_ref, out_ref, up_ref, down_ref):
    blocks = x.shape[1]
    slots = src.shape[1]
    rim = up_ref.shape[0]
    index = lax.axis_index("blk")
    at_last = index == lax.axis_size("blk") - 1
    at_first = index == 0
    rows = lax.broadcasted_iota(jnp.int32, (blocks, slots), 0)
    out_ref[...] = pick(x, onehot(rows == src)).T
    sub = lax.broadcasted_iota(jnp.int32, (LANES, LANES), 0)
    lane = lax.broadcasted_iota(jnp.int32, (LANES, LANES), 1)
    lane_row = lane[:1]
    sub_col = sub[:, :1]
    wanted = lane_row
    target = sub_col
    for j in range(rim):
        partner = perm_ref[0, j]
        wanted = jnp.where((lane_row == j) & at_last, partner, wanted)
        target = jnp.where((sub_col == j) & at_first, partner, target)
    to_up = (sub == wanted + (LANES - rim)) & (lane < rim)
    to_down = (target + rim == lane) & (sub < rim)
    rims = pick(x[:, blocks - LANES :], onehot(to_up)) + pick(x[:, :LANES], onehot(to_down))
    turn_up = (lane_row < rim) & at_last
    turn_down = (lane_row >= rim) & at_first
    angle = 2.0 * math.pi / 3.0
    cosine = jnp.where(turn_up | turn_down, math.cos(angle), 1.0)
    sine = jnp.where(turn_up, math.sin(angle), jnp.where(turn_down, -math.sin(angle), 0.0))
    first = rims[2 * CELLS : 3 * CELLS]
    second = rims[3 * CELLS : 4 * CELLS]
    rims = jnp.concatenate(
        [
            rims[: 2 * CELLS],
            cosine * first - sine * second,
            sine * first + cosine * second,
            rims[4 * CELLS :],
        ],
        axis=0,
    ).T
    up_ref[...] = rims[:rim]
    down_ref[...] = rims[rim : 2 * rim]


def donors_kernel(x_ref, src_ref, perm_ref, out_ref, up_ref, down_ref):
    send_blocks(x_ref[...], src_ref[...], perm_ref, out_ref, up_ref, down_ref)


def local_kernel(x_ref, lower_ref, upper_ref, nbr_ref, coup_ref, source_ref, out_ref, high, low, near):
    step = pl.program_id(0)
    blocks = x_ref.shape[1]
    rim = lower_ref.shape[0]
    slots = nbr_ref.shape[0]

    @pl.when(step == 0)
    def _():
        rims = jnp.concatenate(
            [lower_ref[...], upper_ref[...], jnp.zeros((LANES - 2 * rim, BW), jnp.float32)], axis=0
        ).T
        lane = lax.broadcasted_iota(jnp.int32, (BW, LANES), 1)
        moved = pltpu.roll(x_ref[...], rim, 1)
        head = jnp.where(lane < rim, rims, moved[:, :LANES])
        tail = jnp.where(lane < rim, moved[:, :LANES], jnp.where(lane < 2 * rim, rims, 0.0))
        ext = jnp.concatenate([head, moved[:, LANES:], tail], axis=1)
        high[...], low[...] = split(ext)

    start = pl.multiple_of(step * LANES, LANES)
    here = pl.ds(start, LANES)
    window = pl.ds(start, 2 * LANES)
    rows = lax.broadcasted_iota(jnp.int32, (2 * LANES, LANES), 0)
    table = jnp.concatenate(
        [onehot(rows == nbr_ref[m : m + 1, :] - start) for m in range(slots)], axis=1
    )
    near[...] = jnp.dot(high[:, window], table, preferred_element_type=jnp.float32) + jnp.dot(
        low[:, window], table, preferred_element_type=jnp.float32
    )

    def cells(part, carry):
        at = pl.multiple_of(part * PACK, PACK)
        total = [None] * VARS
        for m in range(slots):
            for v in range(VARS):
                value = near[pl.ds(v * CELLS + at, PACK), m * LANES : (m + 1) * LANES]
                for u in range(VARS):
                    term = coup_ref[m, u, pl.ds(v * CELLS + at, PACK), :].astype(jnp.float32) * value
                    total[u] = term if total[u] is None else total[u] + term
        for u in range(VARS):
            span = pl.ds(u * CELLS + at, PACK)
            out_ref[span, :] = source_ref[span, :] - x_ref[span, here] + total[u]
        return carry

    lax.fori_loop(0, CELLS // PACK, cells, 0)


def fringe_residual(local_ref, inc_ref, dst_ref, weight_ref):
    blocks = local_ref.shape[1]
    slots = inc_ref.shape[0]
    rows = lax.broadcasted_iota(jnp.int32, (blocks, slots), 0)
    table = onehot(rows == dst_ref[...])
    high, low = split(inc_ref[...].T * weight_ref[...])
    contract = (((1,), (1,)), ((), ()))
    return (
        local_ref[...]
        + lax.dot_general(high, table, contract, preferred_element_type=jnp.float32)
        + lax.dot_general(low, table, contract, preferred_element_type=jnp.float32)
    )


def precondition(diag_ref, resid_ref, u, at):
    total = None
    for v in range(VARS):
        span = pl.ds(v * CELLS + at, PACK)
        term = diag_ref[u, span, :].astype(jnp.float32) * resid_ref[span, :]
        total = term if total is None else total + term
    return total


def lane_sums(resid):
    square = jnp.sum(resid * resid, axis=0, keepdims=True)
    return sum(square[:, i : i + LANES] for i in range(0, square.shape[1], LANES))


def advance_kernel(
    local_ref, inc_ref, dst_ref, weight_ref, diag_ref, x_ref, src_ref, perm_ref,
    next_ref, norm_ref, out_ref, up_ref, down_ref, resid,
):
    resid[...] = fringe_residual(local_ref, inc_ref, dst_ref, weight_ref)
    norm_ref[...] = lane_sums(resid[...])

    def cells(part, carry):
        at = pl.multiple_of(part * PACK, PACK)
        for u in range(VARS):
            span = pl.ds(u * CELLS + at, PACK)
            next_ref[span, :] = x_ref[span, :] + STEP_CFL * precondition(diag_ref, resid, u, at)
        return carry

    lax.fori_loop(0, CELLS // PACK, cells, 0)
    send_blocks(next_ref[...], src_ref[...], perm_ref, out_ref, up_ref, down_ref)


def residual_kernel(local_ref, inc_ref, dst_ref, weight_ref, norm_ref, resid_ref, sums_ref):
    resid = fringe_residual(local_ref, inc_ref, dst_ref, weight_ref)
    resid_ref[...] = resid
    both = jnp.concatenate([norm_ref[...], lane_sums(resid)], axis=0)
    sums_ref[...] = jnp.broadcast_to(both[None], sums_ref.shape)


def direction_kernel(diag_ref, resid_ref, out_ref):
    def cells(part, carry):
        at = pl.multiple_of(part * PACK, PACK)
        for u in range(VARS):
            out_ref[pl.ds(u * CELLS + at, PACK), :] = precondition(diag_ref, resid_ref, u, at)
        return carry

    lax.fori_loop(0, CELLS // PACK, cells, 0)


def finish_kernel(entries, sums_ref, x_ref, update_ref, out_ref):
    sums = jnp.sum(jnp.sum(sums_ref[...], axis=0), axis=1, keepdims=True) / entries + 1e-06
    cfl = STEP_CFL * jnp.sqrt(sums[0:1] / sums[1:2])
    out_ref[...] = x_ref[...] + cfl * update_ref[...]


VMEM = pl.BlockSpec(memory_space=pltpu.VMEM)
SMEM = pl.BlockSpec(memory_space=pltpu.SMEM)


def f32(*shape):
    return jax.ShapeDtypeStruct(shape, jnp.float32)


def call(kernel, in_specs, out_shape, flops, moved, **more):
    many = isinstance(out_shape, (list, tuple))
    return pl.pallas_call(
        kernel,
        in_specs=in_specs,
        out_specs=more.pop("out_specs", [VMEM] * len(out_shape) if many else VMEM),
        out_shape=out_shape,
        compiler_params=pltpu.CompilerParams(vmem_limit_bytes=VMEM_LIMIT),
        cost_estimate=pl.CostEstimate(flops=flops, bytes_accessed=moved, transcendentals=0),
        **more,
    )


def shards(
    psi_init, source, coupling, diag_inv, neighbours, seam_perm, fringe_src, fringe_dst, fringe_weight
):
    blocks = psi_init.shape[0]
    slots = neighbours.shape[1]
    rim = seam_perm.shape[1]
    fringe = fringe_src.shape[1]
    peers = lax.axis_size("blk")
    devices = lax.axis_size("body") * peers
    up = [(i, (i + 1) % peers) for i in range(peers)]
    down = [(j, i) for i, j in up]
    x = psi_init.T
    source_t = source.T
    coup = coupling.transpose(1, 2, 3, 0)
    diag = diag_inv.transpose(1, 2, 0)
    nbr = neighbours.T
    state = f32(BW, blocks)
    sent = [f32(fringe, BW), f32(rim, BW), f32(rim, BW)]
    size = 4 * BW * blocks

    donors = call(donors_kernel, [VMEM, VMEM, SMEM], sent, 4 * BW * blocks * fringe, 2 * size)
    local = call(
        local_kernel,
        [
            pl.BlockSpec((BW, blocks), lambda i: (0, 0)),
            pl.BlockSpec((rim, BW), lambda i: (0, 0)),
            pl.BlockSpec((rim, BW), lambda i: (0, 0)),
            pl.BlockSpec((slots, LANES), lambda i: (0, i)),
            pl.BlockSpec((slots, VARS, BW, LANES), lambda i: (0, 0, 0, i)),
            pl.BlockSpec((BW, LANES), lambda i: (0, i)),
        ],
        state,
        4 * BW * 2 * LANES * slots * blocks,
        coup.size * 2 + 4 * size,
        grid=(blocks // LANES,),
        out_specs=pl.BlockSpec((BW, LANES), lambda i: (0, i)),
        scratch_shapes=[
            pltpu.VMEM((BW, blocks + LANES), jnp.bfloat16),
            pltpu.VMEM((BW, blocks + LANES), jnp.bfloat16),
            pltpu.VMEM((BW, slots * LANES), jnp.float32),
        ],
    )
    advance = call(
        advance_kernel,
        [VMEM] * 7 + [SMEM],
        [state, f32(1, LANES)] + sent,
        8 * BW * blocks * fringe,
        diag.size * 2 + 4 * size,
        scratch_shapes=[pltpu.VMEM((BW, blocks), jnp.float32)],
    )
    residual = call(
        residual_kernel,
        [VMEM] * 5,
        [state, f32(devices, 2, LANES)],
        4 * BW * blocks * fringe,
        3 * size,
    )
    direction = call(direction_kernel, [VMEM] * 2, state, diag.size * 2, diag.size * 2 + 2 * size)
    finish = call(
        functools.partial(finish_kernel, float(blocks * devices * BW)),
        [VMEM] * 3,
        state,
        2 * BW * blocks,
        3 * size,
    )

    def exchange(rows, to_up, to_down):
        rows = lax.all_to_all(rows, ("body", "blk"), split_axis=0, concat_axis=0, tiled=True)
        return rows, lax.ppermute(to_up, "blk", up), lax.ppermute(to_down, "blk", down)

    incoming, lower, upper = exchange(*donors(x, fringe_src, seam_perm))
    part = local(x, lower, upper, nbr, coup, source_t)
    x, norm, *out = advance(part, incoming, fringe_dst, fringe_weight, diag, x, fringe_src, seam_perm)
    incoming, lower, upper = exchange(*out)
    part = local(x, lower, upper, nbr, coup, source_t)
    resid, sums = residual(part, incoming, fringe_dst, fringe_weight, norm)
    sums = lax.all_to_all(sums, ("body", "blk"), split_axis=0, concat_axis=0, tiled=True)
    x = finish(sums, x, direction(diag, resid))
    return (x.T, resid.T)


def solution(mesh):
    return jax.shard_map(
        shards,
        mesh=mesh,
        in_specs=(
            P(("body", "blk"), None),
            P(("body", "blk"), None),
            P(("body", "blk"), None, None, None),
            P(("body", "blk"), None, None),
            P(("body", "blk"), None),
            P("body", None),
            P(("body", "blk"), None),
            P(("body", "blk"), None),
            P(("body", "blk"), None),
        ),
        out_specs=(P(("body", "blk"), None), P(("body", "blk"), None)),
        check_vma=False,
    )
```

```python
import functools
import math

import jax
import jax.numpy as jnp
from jax import lax
from jax.experimental import pallas as pl
from jax.experimental.pallas import tpu as pltpu
from jax.sharding import PartitionSpec as P

CELLS = 64
VARS = 5
BW = 320
STEP_CFL = 0.5
LANES = 128
PACK = 16
VMEM_LIMIT = 40 * 1024 * 1024


def split(x):
    high = x.astype(jnp.bfloat16)
    return high, (x - high.astype(jnp.float32)).astype(jnp.bfloat16)


def onehot(mask):
    return jnp.where(mask, 1.0, 0.0).astype(jnp.bfloat16)


def pick(x, table):
    high, low = split(x)
    return jnp.dot(high, table, preferred_element_type=jnp.float32) + jnp.dot(
        low, table, preferred_element_type=jnp.float32
    )


def send_blocks(x, table, sel_up, sel_down, out_ref, up_ref, down_ref):
    rim = up_ref.shape[0]
    index = lax.axis_index("blk")
    at_last = index == lax.axis_size("blk") - 1
    at_first = index == 0
    out_ref[...] = pick(x, table).T
    rims = pick(x[:, x.shape[1] - LANES :], sel_up) + pick(x[:, :LANES], sel_down)
    lane = lax.broadcasted_iota(jnp.int32, (1, LANES), 1)
    turn_up = (lane < rim) & at_last
    turn_down = (lane >= rim) & at_first
    angle = 2.0 * math.pi / 3.0
    cosine = jnp.where(turn_up | turn_down, math.cos(angle), 1.0)
    sine = jnp.where(turn_up, math.sin(angle), jnp.where(turn_down, -math.sin(angle), 0.0))
    first = rims[2 * CELLS : 3 * CELLS]
    second = rims[3 * CELLS : 4 * CELLS]
    rims = jnp.concatenate(
        [
            rims[: 2 * CELLS],
            cosine * first - sine * second,
            sine * first + cosine * second,
            rims[4 * CELLS :],
        ],
        axis=0,
    ).T
    up_ref[...] = rims[:rim]
    down_ref[...] = rims[rim : 2 * rim]


def donors_kernel(x_ref, src_ref, perm_ref, out_ref, up_ref, down_ref, table_ref, sel_up_ref, sel_down_ref):
    rim = up_ref.shape[0]
    index = lax.axis_index("blk")
    at_last = index == lax.axis_size("blk") - 1
    at_first = index == 0
    sub = lax.broadcasted_iota(jnp.int32, (LANES, LANES), 0)
    lane = lax.broadcasted_iota(jnp.int32, (LANES, LANES), 1)
    wanted = lane[:1]
    target = sub[:, :1]
    for j in range(rim):
        partner = perm_ref[0, j]
        wanted = jnp.where((lane[:1] == j) & at_last, partner, wanted)
        target = jnp.where((sub[:, :1] == j) & at_first, partner, target)
    sel_up = onehot((sub == wanted + (LANES - rim)) & (lane < rim))
    sel_down = onehot((target + rim == lane) & (sub < rim))
    rows = lax.broadcasted_iota(jnp.int32, table_ref.shape, 0)
    table = onehot(rows == src_ref[...])
    send_blocks(x_ref[...], table, sel_up, sel_down, out_ref, up_ref, down_ref)
    table_ref[...] = table
    sel_up_ref[...] = sel_up
    sel_down_ref[...] = sel_down


def local_kernel(rim, x_ref, nbr_ref, coup_ref, source_ref, out_ref, high, low, near):
    step = pl.program_id(0)
    slots = nbr_ref.shape[0]

    @pl.when(step == 0)
    def _():
        lane = lax.broadcasted_iota(jnp.int32, (BW, LANES), 1)
        moved = pltpu.roll(x_ref[...], rim, 1)
        head = jnp.where(lane < rim, 0.0, moved[:, :LANES])
        tail = jnp.where(lane < rim, moved[:, :LANES], 0.0)
        ext = jnp.concatenate([head, moved[:, LANES:], tail], axis=1)
        high[...], low[...] = split(ext)

    start = pl.multiple_of(step * LANES, LANES)
    here = pl.ds(start, LANES)
    window = pl.ds(start, 2 * LANES)
    rows = lax.broadcasted_iota(jnp.int32, (2 * LANES, LANES), 0)
    table = jnp.concatenate(
        [onehot(rows == nbr_ref[m : m + 1, :] - start) for m in range(slots)], axis=1
    )
    near[...] = jnp.dot(high[:, window], table, preferred_element_type=jnp.float32) + jnp.dot(
        low[:, window], table, preferred_element_type=jnp.float32
    )

    def cells(part, carry):
        at = pl.multiple_of(part * PACK, PACK)
        total = [None] * VARS
        for m in range(slots):
            for v in range(VARS):
                value = near[pl.ds(v * CELLS + at, PACK), m * LANES : (m + 1) * LANES]
                for u in range(VARS):
                    term = coup_ref[m, u, pl.ds(v * CELLS + at, PACK), :].astype(jnp.float32) * value
                    total[u] = term if total[u] is None else total[u] + term
        for u in range(VARS):
            span = pl.ds(u * CELLS + at, PACK)
            out_ref[span, :] = source_ref[span, :] - x_ref[span, here] + total[u]
        return carry

    lax.fori_loop(0, CELLS // PACK, cells, 0)


def first_local_kernel(
    rim, x_ref, nbr_ref, coup_ref, source_ref, diag_ref, dst_ref, weight_ref,
    out_ref, rimcoup_ref, rimrow_ref, x_out, diag_out, dst_out, weight_out, high, low, near,
):
    step = pl.program_id(0)
    last = pl.num_programs(0) - 1
    slots = nbr_ref.shape[0]
    blocks = x_ref.shape[1]
    local_kernel(rim, x_ref, nbr_ref, coup_ref, source_ref, out_ref, high, low, near)
    x_out[...] = x_ref[:, pl.ds(pl.multiple_of(step * LANES, LANES), LANES)]
    diag_out[...] = diag_ref[...]
    dst_out[...] = dst_ref[...]
    weight_out[...] = weight_ref[...]

    @pl.when((step == 0) | (step == last))
    def _():
        sub = lax.broadcasted_iota(jnp.int32, (LANES, LANES), 0)
        lane = lax.broadcasted_iota(jnp.int32, (LANES, LANES), 1)
        base = jnp.where(step == 0, 0, rim)
        at = sub - jnp.where(step == 0, 0, LANES - 2 * rim)
        inside = (at >= base) & (at < base + rim)
        place = jnp.concatenate(
            [onehot((lane == at + m * 2 * rim) & inside) for m in range(slots)], axis=0
        )
        reads = []
        for m in range(slots):
            row = nbr_ref[m : m + 1, :]
            lower = jnp.where(row < rim, row + 1, 0)
            upper = jnp.where(row >= blocks + rim, row - blocks + 1, 0)
            reads.append(jnp.where(step == 0, lower, upper))
        reads = jnp.broadcast_to(jnp.concatenate(reads, axis=1), (PACK, slots * LANES))
        reads = reads.astype(jnp.float32).astype(jnp.bfloat16)
        kept = jnp.where(step == 0, 0.0, rimrow_ref[...])
        rimrow_ref[...] = kept + jnp.dot(reads, place, preferred_element_type=jnp.float32)
        for u in range(VARS):
            rows = jnp.concatenate([coup_ref[m, u] for m in range(slots)], axis=1)
            moved = jnp.dot(rows, place, preferred_element_type=jnp.float32)
            kept = jnp.where(step == 0, 0.0, rimcoup_ref[u].astype(jnp.float32))
            rimcoup_ref[u] = (kept + moved).astype(jnp.bfloat16)


def full_residual(local_ref, inc_ref, lower_ref, upper_ref, dst_ref, weight_ref, rimcoup_ref, rimrow_ref):
    blocks = local_ref.shape[1]
    slots = inc_ref.shape[0]
    rim = lower_ref.shape[0]
    rims = jnp.concatenate(
        [lower_ref[...], upper_ref[...], jnp.zeros((LANES - 2 * rim, BW), jnp.float32)], axis=0
    ).T
    sub = lax.broadcasted_iota(jnp.int32, (LANES, LANES), 0)
    near = pick(rims, onehot(sub + 1 == rimrow_ref[:1].astype(jnp.int32)))
    edge = []
    for u in range(VARS):
        total = None
        for v in range(VARS):
            span = slice(v * CELLS, (v + 1) * CELLS)
            term = rimcoup_ref[u, span, :].astype(jnp.float32) * near[span]
            total = term if total is None else total + term
        edge.append(total)
    edge = jnp.concatenate(edge, axis=0)
    rows = lax.broadcasted_iota(jnp.int32, (blocks, slots), 0)
    edge_rows = lax.broadcasted_iota(jnp.int32, (blocks, LANES), 0)
    place = lax.rem(lax.broadcasted_iota(jnp.int32, (1, LANES), 1), 2 * rim)
    place = jnp.where(place < rim, place, place + (blocks - 2 * rim))
    table = jnp.concatenate([onehot(rows == dst_ref[...]), onehot(edge_rows == place)], axis=1)
    high, low = split(jnp.concatenate([inc_ref[...].T * weight_ref[...], edge], axis=1))
    contract = (((1,), (1,)), ((), ()))
    return (
        local_ref[...]
        + lax.dot_general(high, table, contract, preferred_element_type=jnp.float32)
        + lax.dot_general(low, table, contract, preferred_element_type=jnp.float32)
    )


def precondition(diag_ref, resid_ref, u, at):
    total = None
    for v in range(VARS):
        span = pl.ds(v * CELLS + at, PACK)
        term = diag_ref[u, span, :].astype(jnp.float32) * resid_ref[span, :]
        total = term if total is None else total + term
    return total


def lane_sums(resid):
    square = jnp.sum(resid * resid, axis=0, keepdims=True)
    return sum(square[:, i : i + LANES] for i in range(0, square.shape[1], LANES))


def advance_kernel(
    local_ref, inc_ref, lower_ref, upper_ref, dst_ref, weight_ref, rimcoup_ref, rimrow_ref,
    diag_ref, x_ref, table_ref, sel_up_ref, sel_down_ref,
    next_ref, norm_ref, out_ref, up_ref, down_ref, resid,
):
    resid[...] = full_residual(
        local_ref, inc_ref, lower_ref, upper_ref, dst_ref, weight_ref, rimcoup_ref, rimrow_ref
    )

    def cells(part, carry):
        at = pl.multiple_of(part * PACK, PACK)
        for u in range(VARS):
            span = pl.ds(u * CELLS + at, PACK)
            next_ref[span, :] = x_ref[span, :] + STEP_CFL * precondition(diag_ref, resid, u, at)
        return carry

    lax.fori_loop(0, CELLS // PACK, cells, 0)
    send_blocks(
        next_ref[...], table_ref[...], sel_up_ref[...], sel_down_ref[...], out_ref, up_ref, down_ref
    )
    norm_ref[...] = lane_sums(resid[...])


def residual_kernel(
    local_ref, inc_ref, lower_ref, upper_ref, dst_ref, weight_ref, rimcoup_ref, rimrow_ref, norm_ref,
    resid_ref, sums_ref,
):
    resid = full_residual(
        local_ref, inc_ref, lower_ref, upper_ref, dst_ref, weight_ref, rimcoup_ref, rimrow_ref
    )
    resid_ref[...] = resid
    both = jnp.concatenate([norm_ref[...], lane_sums(resid)], axis=0)
    sums_ref[...] = jnp.broadcast_to(both[None], sums_ref.shape)


def direction_kernel(diag_ref, resid_ref, out_ref, resid_out):
    resid_out[...] = resid_ref[...]

    def cells(part, carry):
        at = pl.multiple_of(part * PACK, PACK)
        for u in range(VARS):
            out_ref[pl.ds(u * CELLS + at, PACK), :] = precondition(diag_ref, resid_ref, u, at)
        return carry

    lax.fori_loop(0, CELLS // PACK, cells, 0)


def finish_kernel(entries, sums_ref, x_ref, update_ref, out_ref):
    sums = jnp.sum(jnp.sum(sums_ref[...], axis=0), axis=1, keepdims=True) / entries + 1e-06
    cfl = STEP_CFL * jnp.sqrt(sums[0:1] / sums[1:2])
    out_ref[...] = x_ref[...] + cfl * update_ref[...]


VMEM = pl.BlockSpec(memory_space=pltpu.VMEM)
SMEM = pl.BlockSpec(memory_space=pltpu.SMEM)


def f32(*shape):
    return jax.ShapeDtypeStruct(shape, jnp.float32)


def bf16(*shape):
    return jax.ShapeDtypeStruct(shape, jnp.bfloat16)


def call(kernel, in_specs, out_shape, flops, moved, **more):
    many = isinstance(out_shape, (list, tuple))
    return pl.pallas_call(
        kernel,
        in_specs=in_specs,
        out_specs=more.pop("out_specs", [VMEM] * len(out_shape) if many else VMEM),
        out_shape=out_shape,
        compiler_params=pltpu.CompilerParams(vmem_limit_bytes=VMEM_LIMIT),
        cost_estimate=pl.CostEstimate(flops=flops, bytes_accessed=moved, transcendentals=0),
        **more,
    )


def shards(
    psi_init, source, coupling, diag_inv, neighbours, seam_perm, fringe_src, fringe_dst, fringe_weight
):
    blocks = psi_init.shape[0]
    slots = neighbours.shape[1]
    rim = seam_perm.shape[1]
    fringe = fringe_src.shape[1]
    peers = lax.axis_size("blk")
    devices = lax.axis_size("body") * peers
    up = [(i, (i + 1) % peers) for i in range(peers)]
    down = [(j, i) for i, j in up]
    here = functools.partial(pltpu.with_memory_space_constraint, memory_space=pltpu.HBM)
    x = here(psi_init.T)
    source_t = here(source.T)
    coup = here(coupling.transpose(1, 2, 3, 0))
    diag = here(diag_inv.transpose(1, 2, 0))
    nbr = here(neighbours.T)
    state = f32(BW, blocks)
    sent = [f32(fringe, BW), f32(rim, BW), f32(rim, BW)]
    size = 4 * BW * blocks
    square = bf16(LANES, LANES)

    donors = call(
        donors_kernel,
        [VMEM, VMEM, SMEM],
        sent + [bf16(blocks, fringe), square, square],
        4 * BW * blocks * fringe,
        2 * size,
    )
    column = pl.BlockSpec((BW, LANES), lambda i: (0, i))
    diag_column = pl.BlockSpec((VARS, BW, LANES), lambda i: (0, 0, i))
    whole_row = pl.BlockSpec((1, fringe), lambda i: (0, 0))
    local_in = [
        pl.BlockSpec((BW, blocks), lambda i: (0, 0)),
        pl.BlockSpec((slots, LANES), lambda i: (0, i)),
        pl.BlockSpec((slots, VARS, BW, LANES), lambda i: (0, 0, 0, i)),
        column,
    ]
    local_more = dict(
        flops=4 * BW * 2 * LANES * slots * blocks,
        moved=coup.size * 2 + 4 * size,
        grid=(blocks // LANES,),
        scratch_shapes=[
            pltpu.VMEM((BW, blocks + LANES), jnp.bfloat16),
            pltpu.VMEM((BW, blocks + LANES), jnp.bfloat16),
            pltpu.VMEM((BW, slots * LANES), jnp.float32),
        ],
    )
    first_local = call(
        functools.partial(first_local_kernel, rim),
        local_in + [diag_column, whole_row, whole_row],
        [
            state,
            bf16(VARS, BW, LANES),
            f32(PACK, LANES),
            state,
            bf16(VARS, BW, blocks),
            jax.ShapeDtypeStruct((1, fringe), jnp.int32),
            f32(1, fringe),
        ],
        out_specs=[
            column,
            pl.BlockSpec((VARS, BW, LANES), lambda i: (0, 0, 0)),
            pl.BlockSpec((PACK, LANES), lambda i: (0, 0)),
            column,
            diag_column,
            whole_row,
            whole_row,
        ],
        **local_more,
    )
    local = call(functools.partial(local_kernel, rim), local_in, state, out_specs=column, **local_more)
    advance = call(
        advance_kernel,
        [VMEM] * 13,
        [state, f32(1, LANES)] + sent,
        8 * BW * blocks * fringe,
        diag.size * 2 + 4 * size,
        scratch_shapes=[pltpu.VMEM((BW, blocks), jnp.float32)],
    )
    residual = call(
        residual_kernel,
        [VMEM] * 9,
        [state, f32(devices, 2, LANES)],
        4 * BW * blocks * fringe,
        3 * size,
    )
    direction = call(
        direction_kernel, [VMEM] * 2, [state, state], diag.size * 2, diag.size * 2 + 2 * size
    )
    finish = call(
        functools.partial(finish_kernel, float(blocks * devices * BW)),
        [VMEM] * 3,
        state,
        2 * BW * blocks,
        3 * size,
    )

    def exchange(rows, to_up, to_down):
        rows = lax.all_to_all(rows, ("body", "blk"), split_axis=0, concat_axis=0, tiled=True)
        return rows, lax.ppermute(to_up, "blk", up), lax.ppermute(to_down, "blk", down)

    *out, table, sel_up, sel_down = donors(x, here(fringe_src), here(seam_perm))
    arrived = exchange(*out)
    part, rimcoup, rimrow, x, diag, dst, weight = first_local(
        x, nbr, coup, source_t, diag, here(fringe_dst), here(fringe_weight)
    )
    across = (dst, weight, rimcoup, rimrow)
    x, norm, *out = advance(part, *arrived, *across, diag, x, table, sel_up, sel_down)
    arrived = exchange(*out)
    part = local(x, nbr, coup, source_t)
    resid, sums = residual(part, *arrived, *across, norm)
    sums = lax.all_to_all(sums, ("body", "blk"), split_axis=0, concat_axis=0, tiled=True)
    update, resid = direction(diag, resid)
    x = finish(sums, x, update)
    return (x.T, resid.T)


def solution(mesh):
    return jax.shard_map(
        shards,
        mesh=mesh,
        in_specs=(
            P(("body", "blk"), None),
            P(("body", "blk"), None),
            P(("body", "blk"), None, None, None),
            P(("body", "blk"), None, None),
            P(("body", "blk"), None),
            P("body", None),
            P(("body", "blk"), None),
            P(("body", "blk"), None),
            P(("body", "blk"), None),
        ),
        out_specs=(P(("body", "blk"), None), P(("body", "blk"), None)),
        check_vma=False,
    )
```

```python
import functools
import math

import jax
import jax.numpy as jnp
from jax import lax
from jax.experimental import pallas as pl
from jax.experimental.pallas import tpu as pltpu
from jax.sharding import PartitionSpec as P

CELLS = 64
VARS = 5
BW = 320
STEP_CFL = 0.5
LANES = 128
PACK = 16
VMEM_LIMIT = 32 * 1024 * 1024


def split(x):
    high = x.astype(jnp.bfloat16)
    return high, (x - high.astype(jnp.float32)).astype(jnp.bfloat16)


def onehot(mask):
    return jnp.where(mask, 1.0, 0.0).astype(jnp.bfloat16)


def pick(x, table):
    high, low = split(x)
    return jnp.dot(high, table, preferred_element_type=jnp.float32) + jnp.dot(
        low, table, preferred_element_type=jnp.float32
    )


def send_blocks(x, table, sel_up, sel_down, out_ref, up_ref, down_ref):
    rim = up_ref.shape[0]
    index = lax.axis_index("blk")
    at_last = index == lax.axis_size("blk") - 1
    at_first = index == 0
    out_ref[...] = pick(x, table).T
    rims = pick(x[:, x.shape[1] - LANES :], sel_up) + pick(x[:, :LANES], sel_down)
    lane = lax.broadcasted_iota(jnp.int32, (1, LANES), 1)
    turn_up = (lane < rim) & at_last
    turn_down = (lane >= rim) & at_first
    angle = 2.0 * math.pi / 3.0
    cosine = jnp.where(turn_up | turn_down, math.cos(angle), 1.0)
    sine = jnp.where(turn_up, math.sin(angle), jnp.where(turn_down, -math.sin(angle), 0.0))
    first = rims[2 * CELLS : 3 * CELLS]
    second = rims[3 * CELLS : 4 * CELLS]
    rims = jnp.concatenate(
        [
            rims[: 2 * CELLS],
            cosine * first - sine * second,
            sine * first + cosine * second,
            rims[4 * CELLS :],
        ],
        axis=0,
    ).T
    up_ref[...] = rims[:rim]
    down_ref[...] = rims[rim : 2 * rim]


def donors_kernel(x_ref, src_ref, perm_ref, out_ref, up_ref, down_ref, table_ref, sel_up_ref, sel_down_ref):
    rim = up_ref.shape[0]
    index = lax.axis_index("blk")
    at_last = index == lax.axis_size("blk") - 1
    at_first = index == 0
    sub = lax.broadcasted_iota(jnp.int32, (LANES, LANES), 0)
    lane = lax.broadcasted_iota(jnp.int32, (LANES, LANES), 1)
    wanted = lane[:1]
    target = sub[:, :1]
    for j in range(rim):
        partner = perm_ref[0, j]
        wanted = jnp.where((lane[:1] == j) & at_last, partner, wanted)
        target = jnp.where((sub[:, :1] == j) & at_first, partner, target)
    sel_up = onehot((sub == wanted + (LANES - rim)) & (lane < rim))
    sel_down = onehot((target + rim == lane) & (sub < rim))
    rows = lax.broadcasted_iota(jnp.int32, table_ref.shape, 0)
    table = onehot(rows == src_ref[...])
    send_blocks(x_ref[...], table, sel_up, sel_down, out_ref, up_ref, down_ref)
    table_ref[...] = table
    sel_up_ref[...] = sel_up
    sel_down_ref[...] = sel_down


def local_kernel(rim, x_ref, nbr_ref, coup_ref, source_ref, out_ref, high, low, near):
    step = pl.program_id(0)
    slots = nbr_ref.shape[0]

    @pl.when(step == 0)
    def _():
        lane = lax.broadcasted_iota(jnp.int32, (BW, LANES), 1)
        moved = pltpu.roll(x_ref[...], rim, 1)
        head = jnp.where(lane < rim, 0.0, moved[:, :LANES])
        tail = jnp.where(lane < rim, moved[:, :LANES], 0.0)
        ext = jnp.concatenate([head, moved[:, LANES:], tail], axis=1)
        high[...], low[...] = split(ext)

    start = pl.multiple_of(step * LANES, LANES)
    here = pl.ds(start, LANES)
    window = pl.ds(start, 2 * LANES)
    rows = lax.broadcasted_iota(jnp.int32, (2 * LANES, LANES), 0)
    table = jnp.concatenate(
        [onehot(rows == nbr_ref[m : m + 1, :] - start) for m in range(slots)], axis=1
    )
    near[...] = jnp.dot(high[:, window], table, preferred_element_type=jnp.float32) + jnp.dot(
        low[:, window], table, preferred_element_type=jnp.float32
    )

    def cells(part, carry):
        at = pl.multiple_of(part * PACK, PACK)
        total = [None] * VARS
        for m in range(slots):
            for v in range(VARS):
                value = near[pl.ds(v * CELLS + at, PACK), m * LANES : (m + 1) * LANES]
                for u in range(VARS):
                    term = coup_ref[m, u, pl.ds(v * CELLS + at, PACK), :].astype(jnp.float32) * value
                    total[u] = term if total[u] is None else total[u] + term
        for u in range(VARS):
            span = pl.ds(u * CELLS + at, PACK)
            out_ref[span, :] = source_ref[span, :] - x_ref[span, here] + total[u]
        return carry

    lax.fori_loop(0, CELLS // PACK, cells, 0)


def first_local_kernel(
    rim, x_ref, nbr_ref, coup_ref, source_ref, dst_ref, weight_ref,
    out_ref, rimcoup_ref, rimrow_ref, x_out, dst_out, weight_out, high, low, near,
):
    step = pl.program_id(0)
    last = pl.num_programs(0) - 1
    slots = nbr_ref.shape[0]
    blocks = x_ref.shape[1]
    local_kernel(rim, x_ref, nbr_ref, coup_ref, source_ref, out_ref, high, low, near)
    x_out[...] = x_ref[:, pl.ds(pl.multiple_of(step * LANES, LANES), LANES)]
    dst_out[...] = dst_ref[...]
    weight_out[...] = weight_ref[...]

    @pl.when((step == 0) | (step == last))
    def _():
        sub = lax.broadcasted_iota(jnp.int32, (LANES, LANES), 0)
        lane = lax.broadcasted_iota(jnp.int32, (LANES, LANES), 1)
        base = jnp.where(step == 0, 0, rim)
        at = sub - jnp.where(step == 0, 0, LANES - 2 * rim)
        inside = (at >= base) & (at < base + rim)
        place = jnp.concatenate(
            [onehot((lane == at + m * 2 * rim) & inside) for m in range(slots)], axis=0
        )
        reads = []
        for m in range(slots):
            row = nbr_ref[m : m + 1, :]
            lower = jnp.where(row < rim, row + 1, 0)
            upper = jnp.where(row >= blocks + rim, row - blocks + 1, 0)
            reads.append(jnp.where(step == 0, lower, upper))
        reads = jnp.broadcast_to(jnp.concatenate(reads, axis=1), (PACK, slots * LANES))
        reads = reads.astype(jnp.float32).astype(jnp.bfloat16)
        kept = jnp.where(step == 0, 0.0, rimrow_ref[...])
        rimrow_ref[...] = kept + jnp.dot(reads, place, preferred_element_type=jnp.float32)
        for u in range(VARS):
            rows = jnp.concatenate([coup_ref[m, u] for m in range(slots)], axis=1)
            moved = jnp.dot(rows, place, preferred_element_type=jnp.float32)
            kept = jnp.where(step == 0, 0.0, rimcoup_ref[u].astype(jnp.float32))
            rimcoup_ref[u] = (kept + moved).astype(jnp.bfloat16)


def full_residual(local_ref, inc_ref, lower_ref, upper_ref, dst_ref, weight_ref, rimcoup_ref, rimrow_ref):
    blocks = local_ref.shape[1]
    slots = inc_ref.shape[0]
    rim = lower_ref.shape[0]
    rims = jnp.concatenate(
        [lower_ref[...], upper_ref[...], jnp.zeros((LANES - 2 * rim, BW), jnp.float32)], axis=0
    ).T
    sub = lax.broadcasted_iota(jnp.int32, (LANES, LANES), 0)
    near = pick(rims, onehot(sub + 1 == rimrow_ref[:1].astype(jnp.int32)))
    edge = []
    for u in range(VARS):
        total = None
        for v in range(VARS):
            span = slice(v * CELLS, (v + 1) * CELLS)
            term = rimcoup_ref[u, span, :].astype(jnp.float32) * near[span]
            total = term if total is None else total + term
        edge.append(total)
    edge = jnp.concatenate(edge, axis=0)
    rows = lax.broadcasted_iota(jnp.int32, (blocks, slots), 0)
    edge_rows = lax.broadcasted_iota(jnp.int32, (blocks, LANES), 0)
    place = lax.rem(lax.broadcasted_iota(jnp.int32, (1, LANES), 1), 2 * rim)
    place = jnp.where(place < rim, place, place + (blocks - 2 * rim))
    table = jnp.concatenate([onehot(rows == dst_ref[...]), onehot(edge_rows == place)], axis=1)
    high, low = split(jnp.concatenate([inc_ref[...].T * weight_ref[...], edge], axis=1))
    contract = (((1,), (1,)), ((), ()))
    return (
        local_ref[...]
        + lax.dot_general(high, table, contract, preferred_element_type=jnp.float32)
        + lax.dot_general(low, table, contract, preferred_element_type=jnp.float32)
    )


def precondition(diag_ref, resid_ref, u, at):
    total = None
    for v in range(VARS):
        span = pl.ds(v * CELLS + at, PACK)
        term = diag_ref[u, span, :].astype(jnp.float32) * resid_ref[span, :]
        total = term if total is None else total + term
    return total


def lane_sums(resid):
    square = jnp.sum(resid * resid, axis=0, keepdims=True)
    return sum(square[:, i : i + LANES] for i in range(0, square.shape[1], LANES))


def advance_kernel(
    local_ref, inc_ref, lower_ref, upper_ref, dst_ref, weight_ref, rimcoup_ref, rimrow_ref,
    diag_ref, x_ref, table_ref, sel_up_ref, sel_down_ref,
    next_ref, norm_ref, out_ref, up_ref, down_ref, resid, diag, diag_sem,
):
    fetch = pltpu.make_async_copy(diag_ref, diag, diag_sem)
    fetch.start()
    resid[...] = full_residual(
        local_ref, inc_ref, lower_ref, upper_ref, dst_ref, weight_ref, rimcoup_ref, rimrow_ref
    )
    fetch.wait()

    def cells(part, carry):
        at = pl.multiple_of(part * PACK, PACK)
        for u in range(VARS):
            span = pl.ds(u * CELLS + at, PACK)
            next_ref[span, :] = x_ref[span, :] + STEP_CFL * precondition(diag, resid, u, at)
        return carry

    lax.fori_loop(0, CELLS // PACK, cells, 0)
    send_blocks(
        next_ref[...], table_ref[...], sel_up_ref[...], sel_down_ref[...], out_ref, up_ref, down_ref
    )
    norm_ref[...] = lane_sums(resid[...])


def residual_kernel(
    local_ref, inc_ref, lower_ref, upper_ref, dst_ref, weight_ref, rimcoup_ref, rimrow_ref, norm_ref,
    resid_ref, sums_ref,
):
    resid = full_residual(
        local_ref, inc_ref, lower_ref, upper_ref, dst_ref, weight_ref, rimcoup_ref, rimrow_ref
    )
    resid_ref[...] = resid
    both = jnp.concatenate([norm_ref[...], lane_sums(resid)], axis=0)
    sums_ref[...] = jnp.broadcast_to(both[None], sums_ref.shape)


def direction_kernel(diag_ref, resid_ref, out_ref, resid_out):
    resid_out[...] = resid_ref[...]

    def cells(part, carry):
        at = pl.multiple_of(part * PACK, PACK)
        for u in range(VARS):
            out_ref[pl.ds(u * CELLS + at, PACK), :] = precondition(diag_ref, resid_ref, u, at)
        return carry

    lax.fori_loop(0, CELLS // PACK, cells, 0)


def finish_kernel(entries, sums_ref, x_ref, update_ref, out_ref):
    sums = jnp.sum(jnp.sum(sums_ref[...], axis=0), axis=1, keepdims=True) / entries + 1e-06
    cfl = STEP_CFL * jnp.sqrt(sums[0:1] / sums[1:2])
    out_ref[...] = x_ref[...] + cfl * update_ref[...]


VMEM = pl.BlockSpec(memory_space=pltpu.VMEM)
SMEM = pl.BlockSpec(memory_space=pltpu.SMEM)


def f32(*shape):
    return jax.ShapeDtypeStruct(shape, jnp.float32)


def bf16(*shape):
    return jax.ShapeDtypeStruct(shape, jnp.bfloat16)


def call(kernel, in_specs, out_shape, flops, moved, **more):
    many = isinstance(out_shape, (list, tuple))
    return pl.pallas_call(
        kernel,
        in_specs=in_specs,
        out_specs=more.pop("out_specs", [VMEM] * len(out_shape) if many else VMEM),
        out_shape=out_shape,
        compiler_params=pltpu.CompilerParams(vmem_limit_bytes=VMEM_LIMIT),
        cost_estimate=pl.CostEstimate(flops=flops, bytes_accessed=moved, transcendentals=0),
        **more,
    )


def shards(
    psi_init, source, coupling, diag_inv, neighbours, seam_perm, fringe_src, fringe_dst, fringe_weight
):
    blocks = psi_init.shape[0]
    slots = neighbours.shape[1]
    rim = seam_perm.shape[1]
    fringe = fringe_src.shape[1]
    peers = lax.axis_size("blk")
    devices = lax.axis_size("body") * peers
    up = [(i, (i + 1) % peers) for i in range(peers)]
    down = [(j, i) for i, j in up]
    here = functools.partial(pltpu.with_memory_space_constraint, memory_space=pltpu.HBM)
    x = here(psi_init.T)
    source_t = here(source.T)
    coup = here(coupling.transpose(1, 2, 3, 0))
    diag = here(diag_inv.transpose(1, 2, 0))
    nbr = here(neighbours.T)
    state = f32(BW, blocks)
    sent = [f32(fringe, BW), f32(rim, BW), f32(rim, BW)]
    size = 4 * BW * blocks
    square = bf16(LANES, LANES)

    donors = call(
        donors_kernel,
        [VMEM, VMEM, SMEM],
        sent + [bf16(blocks, fringe), square, square],
        4 * BW * blocks * fringe,
        2 * size,
    )
    column = pl.BlockSpec((BW, LANES), lambda i: (0, i))
    whole_row = pl.BlockSpec((1, fringe), lambda i: (0, 0))
    local_in = [
        pl.BlockSpec((BW, blocks), lambda i: (0, 0)),
        pl.BlockSpec((slots, LANES), lambda i: (0, i)),
        pl.BlockSpec((slots, VARS, BW, LANES), lambda i: (0, 0, 0, i)),
        column,
    ]
    local_more = dict(
        flops=4 * BW * 2 * LANES * slots * blocks,
        moved=coup.size * 2 + 4 * size,
        grid=(blocks // LANES,),
        scratch_shapes=[
            pltpu.VMEM((BW, blocks + LANES), jnp.bfloat16),
            pltpu.VMEM((BW, blocks + LANES), jnp.bfloat16),
            pltpu.VMEM((BW, slots * LANES), jnp.float32),
        ],
    )
    first_local = call(
        functools.partial(first_local_kernel, rim),
        local_in + [whole_row, whole_row],
        [
            state,
            bf16(VARS, BW, LANES),
            f32(PACK, LANES),
            state,
            jax.ShapeDtypeStruct((1, fringe), jnp.int32),
            f32(1, fringe),
        ],
        out_specs=[
            column,
            pl.BlockSpec((VARS, BW, LANES), lambda i: (0, 0, 0)),
            pl.BlockSpec((PACK, LANES), lambda i: (0, 0)),
            column,
            whole_row,
            whole_row,
        ],
        **local_more,
    )
    local = call(functools.partial(local_kernel, rim), local_in, state, out_specs=column, **local_more)
    advance = call(
        advance_kernel,
        [VMEM] * 8 + [pl.BlockSpec(memory_space=pltpu.HBM)] + [VMEM] * 4,
        [state, f32(1, LANES)] + sent,
        8 * BW * blocks * fringe,
        diag.size * 2 + 4 * size,
        scratch_shapes=[
            pltpu.VMEM((BW, blocks), jnp.float32),
            pltpu.VMEM((VARS, BW, blocks), jnp.bfloat16),
            pltpu.SemaphoreType.DMA,
        ],
    )
    residual = call(
        residual_kernel,
        [VMEM] * 9,
        [state, f32(devices, 2, LANES)],
        4 * BW * blocks * fringe,
        3 * size,
    )
    direction = call(
        direction_kernel, [VMEM] * 2, [state, state], diag.size * 2, diag.size * 2 + 2 * size
    )
    finish = call(
        functools.partial(finish_kernel, float(blocks * devices * BW)),
        [VMEM] * 3,
        state,
        2 * BW * blocks,
        3 * size,
    )

    def exchange(rows, to_up, to_down):
        rows = lax.all_to_all(rows, ("body", "blk"), split_axis=0, concat_axis=0, tiled=True)
        return rows, lax.ppermute(to_up, "blk", up), lax.ppermute(to_down, "blk", down)

    *out, table, sel_up, sel_down = donors(x, here(fringe_src), here(seam_perm))
    arrived = exchange(*out)
    part, rimcoup, rimrow, x, dst, weight = first_local(
        x, nbr, coup, source_t, here(fringe_dst), here(fringe_weight)
    )
    across = (dst, weight, rimcoup, rimrow)
    x, norm, *out = advance(part, *arrived, *across, diag, x, table, sel_up, sel_down)
    arrived = exchange(*out)
    part = local(x, nbr, coup, source_t)
    resid, sums = residual(part, *arrived, *across, norm)
    sums = lax.all_to_all(sums, ("body", "blk"), split_axis=0, concat_axis=0, tiled=True)
    update, resid = direction(diag, resid)
    x = finish(sums, x, update)
    return (x.T, resid.T)


def solution(mesh):
    return jax.shard_map(
        shards,
        mesh=mesh,
        in_specs=(
            P(("body", "blk"), None),
            P(("body", "blk"), None),
            P(("body", "blk"), None, None, None),
            P(("body", "blk"), None, None),
            P(("body", "blk"), None),
            P("body", None),
            P(("body", "blk"), None),
            P(("body", "blk"), None),
            P(("body", "blk"), None),
        ),
        out_specs=(P(("body", "blk"), None), P(("body", "blk"), None)),
        check_vma=False,
    )
```

```python
import functools
import math

import jax
import jax.numpy as jnp
from jax import lax
from jax.experimental import pallas as pl
from jax.experimental.pallas import tpu as pltpu
from jax.sharding import PartitionSpec as P

CELLS = 64
VARS = 5
BW = 320
STEP_CFL = 0.5
LANES = 128
PACK = 16
VMEM_LIMIT = 32 * 1024 * 1024


def split(x):
    high = x.astype(jnp.bfloat16)
    return high, (x - high.astype(jnp.float32)).astype(jnp.bfloat16)


def onehot(mask):
    return jnp.where(mask, 1.0, 0.0).astype(jnp.bfloat16)


def pick(x, table):
    high, low = split(x)
    return jnp.dot(high, table, preferred_element_type=jnp.float32) + jnp.dot(
        low, table, preferred_element_type=jnp.float32
    )


def send_blocks(x, table, sel_up, sel_down, out_ref, up_ref, down_ref):
    rim = up_ref.shape[0]
    index = lax.axis_index("blk")
    at_last = index == lax.axis_size("blk") - 1
    at_first = index == 0
    out_ref[...] = pick(x, table).T
    rims = pick(x[:, x.shape[1] - LANES :], sel_up) + pick(x[:, :LANES], sel_down)
    lane = lax.broadcasted_iota(jnp.int32, (1, LANES), 1)
    turn_up = (lane < rim) & at_last
    turn_down = (lane >= rim) & at_first
    angle = 2.0 * math.pi / 3.0
    cosine = jnp.where(turn_up | turn_down, math.cos(angle), 1.0)
    sine = jnp.where(turn_up, math.sin(angle), jnp.where(turn_down, -math.sin(angle), 0.0))
    first = rims[2 * CELLS : 3 * CELLS]
    second = rims[3 * CELLS : 4 * CELLS]
    rims = jnp.concatenate(
        [
            rims[: 2 * CELLS],
            cosine * first - sine * second,
            sine * first + cosine * second,
            rims[4 * CELLS :],
        ],
        axis=0,
    ).T
    up_ref[...] = rims[:rim]
    down_ref[...] = rims[rim : 2 * rim]


def donors_kernel(x_ref, src_ref, perm_ref, out_ref, up_ref, down_ref, table_ref, sel_up_ref, sel_down_ref):
    rim = up_ref.shape[0]
    index = lax.axis_index("blk")
    at_last = index == lax.axis_size("blk") - 1
    at_first = index == 0
    sub = lax.broadcasted_iota(jnp.int32, (LANES, LANES), 0)
    lane = lax.broadcasted_iota(jnp.int32, (LANES, LANES), 1)
    wanted = lane[:1]
    target = sub[:, :1]
    for j in range(rim):
        partner = perm_ref[0, j]
        wanted = jnp.where((lane[:1] == j) & at_last, partner, wanted)
        target = jnp.where((sub[:, :1] == j) & at_first, partner, target)
    sel_up = onehot((sub == wanted + (LANES - rim)) & (lane < rim))
    sel_down = onehot((target + rim == lane) & (sub < rim))
    rows = lax.broadcasted_iota(jnp.int32, table_ref.shape, 0)
    table = onehot(rows == src_ref[...])
    send_blocks(x_ref[...], table, sel_up, sel_down, out_ref, up_ref, down_ref)
    table_ref[...] = table
    sel_up_ref[...] = sel_up
    sel_down_ref[...] = sel_down


def local_kernel(
    rim, x_ref, nbr_ref, coup_ref, source_ref, out_ref, high, low, near, coup, source, sems, source_sem
):
    slots, blocks = nbr_ref.shape
    chunks = blocks // LANES
    spans = [slice(c * LANES, (c + 1) * LANES) for c in range(chunks)]
    copies = [
        pltpu.make_async_copy(coup_ref.at[:, :, :, spans[c]], coup.at[c], sems.at[c])
        for c in range(chunks)
    ]
    for copy in copies:
        copy.start()
    source_copy = pltpu.make_async_copy(source_ref, source, source_sem)
    source_copy.start()
    lane = lax.broadcasted_iota(jnp.int32, (BW, LANES), 1)
    moved = pltpu.roll(x_ref[...], rim, 1)
    head = jnp.where(lane < rim, 0.0, moved[:, :LANES])
    tail = jnp.where(lane < rim, moved[:, :LANES], 0.0)
    high[...], low[...] = split(jnp.concatenate([head, moved[:, LANES:], tail], axis=1))
    rows = lax.broadcasted_iota(jnp.int32, (2 * LANES, LANES), 0)

    def gather(c):
        window = slice(c * LANES, (c + 2) * LANES)
        table = jnp.concatenate(
            [onehot(rows == nbr_ref[m : m + 1, spans[c]] - c * LANES) for m in range(slots)], axis=1
        )
        near[c][...] = jnp.dot(high[:, window], table, preferred_element_type=jnp.float32) + jnp.dot(
            low[:, window], table, preferred_element_type=jnp.float32
        )

    gather(0)
    for c in range(chunks):
        copies[c].wait()
        if c == 0:
            source_copy.wait()
        if c + 1 < chunks:
            gather(c + 1)
        for at in range(0, CELLS, PACK):
            total = [None] * VARS
            for m in range(slots):
                for v in range(VARS):
                    span = slice(v * CELLS + at, v * CELLS + at + PACK)
                    value = near[c][span, m * LANES : (m + 1) * LANES]
                    for u in range(VARS):
                        term = coup[c, m, u, span, :].astype(jnp.float32) * value
                        total[u] = term if total[u] is None else total[u] + term
            for u in range(VARS):
                span = slice(u * CELLS + at, u * CELLS + at + PACK)
                out_ref[span, spans[c]] = source[span, spans[c]] - x_ref[span, spans[c]] + total[u]


def first_local_kernel(
    rim, x_ref, nbr_ref, coup_ref, source_ref, dst_ref, weight_ref,
    out_ref, rimcoup_ref, rimrow_ref, x_out, table_ref, weight_out,
    high, low, near, coup, source, sems, source_sem,
):
    slots, blocks = nbr_ref.shape
    fringe = dst_ref.shape[1]
    local_kernel(
        rim, x_ref, nbr_ref, coup_ref, source_ref, out_ref, high, low, near, coup, source, sems, source_sem
    )
    x_out[...] = x_ref[...]
    weight_out[...] = weight_ref[...]
    sub = lax.broadcasted_iota(jnp.int32, (LANES, LANES), 0)
    lane = lax.broadcasted_iota(jnp.int32, (LANES, LANES), 1)
    at_end = sub >= LANES // 2
    source_lane = sub - jnp.where(at_end, LANES - 2 * rim, 0)
    valid = (sub < rim) | (sub >= LANES - rim)
    place = jnp.concatenate(
        [onehot((lane == source_lane + m * 2 * rim) & valid) for m in range(slots)], axis=0
    )
    first_row = lane[:1] < LANES // 2
    reads = []
    for m in range(slots):
        lower = nbr_ref[m : m + 1, :LANES]
        upper = nbr_ref[m : m + 1, blocks - LANES :]
        lower = jnp.where(lower < rim, lower + 1, 0)
        upper = jnp.where(upper >= blocks + rim, upper - blocks + 1, 0)
        reads.append(jnp.where(first_row, lower, upper))
    reads = jnp.broadcast_to(jnp.concatenate(reads, axis=1), (PACK, slots * LANES))
    reads = reads.astype(jnp.float32).astype(jnp.bfloat16)
    rimrow_ref[...] = jnp.dot(reads, place, preferred_element_type=jnp.float32)
    first = lax.broadcasted_iota(jnp.int32, (BW, LANES), 1) < LANES // 2
    end = blocks // LANES - 1
    for u in range(VARS):
        rows = jnp.concatenate(
            [jnp.where(first, coup[0, m, u], coup[end, m, u]) for m in range(slots)], axis=1
        )
        rimcoup_ref[u] = jnp.dot(rows, place, preferred_element_type=jnp.float32).astype(jnp.bfloat16)
    targets = jnp.broadcast_to(dst_ref[...], (LANES, fringe)).T
    edge = lax.rem(sub, 2 * rim)
    edge = jnp.where(edge < rim, edge, edge + (blocks - 2 * rim))
    for c in range(blocks // LANES):
        span = slice(c * LANES, (c + 1) * LANES)
        block = lane[:1] + c * LANES
        table_ref[:fringe, span] = onehot(targets == block)
        table_ref[fringe:, span] = onehot(edge == block)


def full_residual(local_ref, inc_ref, lower_ref, upper_ref, table_ref, weight_ref, rimcoup_ref, rimrow_ref):
    rim = lower_ref.shape[0]
    rims = jnp.concatenate(
        [lower_ref[...], upper_ref[...], jnp.zeros((LANES - 2 * rim, BW), jnp.float32)], axis=0
    ).T
    sub = lax.broadcasted_iota(jnp.int32, (LANES, LANES), 0)
    near = pick(rims, onehot(sub + 1 == rimrow_ref[:1].astype(jnp.int32)))
    edge = []
    for u in range(VARS):
        total = None
        for v in range(VARS):
            span = slice(v * CELLS, (v + 1) * CELLS)
            term = rimcoup_ref[u, span, :].astype(jnp.float32) * near[span]
            total = term if total is None else total + term
        edge.append(total)
    edge = jnp.concatenate(edge, axis=0)
    arrived = jnp.concatenate([inc_ref[...].T * weight_ref[...], edge], axis=1)
    return local_ref[...] + pick(arrived, table_ref[...])


def precondition(diag_ref, resid_ref, u, at):
    total = None
    for v in range(VARS):
        span = pl.ds(v * CELLS + at, PACK)
        term = diag_ref[u, span, :].astype(jnp.float32) * resid_ref[span, :]
        total = term if total is None else total + term
    return total


def lane_sums(resid):
    square = jnp.sum(resid * resid, axis=0, keepdims=True)
    return sum(square[:, i : i + LANES] for i in range(0, square.shape[1], LANES))


def advance_kernel(
    local_ref, inc_ref, lower_ref, upper_ref, across_ref, weight_ref, rimcoup_ref, rimrow_ref,
    diag_ref, x_ref, table_ref, sel_up_ref, sel_down_ref,
    next_ref, norm_ref, out_ref, up_ref, down_ref, resid, diag, diag_sem,
):
    fetch = pltpu.make_async_copy(diag_ref, diag, diag_sem)
    fetch.start()
    resid[...] = full_residual(
        local_ref, inc_ref, lower_ref, upper_ref, across_ref, weight_ref, rimcoup_ref, rimrow_ref
    )
    fetch.wait()

    def cells(part, carry):
        at = pl.multiple_of(part * PACK, PACK)
        for u in range(VARS):
            span = pl.ds(u * CELLS + at, PACK)
            next_ref[span, :] = x_ref[span, :] + STEP_CFL * precondition(diag, resid, u, at)
        return carry

    lax.fori_loop(0, CELLS // PACK, cells, 0)
    send_blocks(
        next_ref[...], table_ref[...], sel_up_ref[...], sel_down_ref[...], out_ref, up_ref, down_ref
    )
    norm_ref[...] = lane_sums(resid[...])


def residual_kernel(
    local_ref, inc_ref, lower_ref, upper_ref, across_ref, weight_ref, rimcoup_ref, rimrow_ref, norm_ref,
    resid_ref, sums_ref,
):
    resid = full_residual(
        local_ref, inc_ref, lower_ref, upper_ref, across_ref, weight_ref, rimcoup_ref, rimrow_ref
    )
    resid_ref[...] = resid
    both = jnp.concatenate([norm_ref[...], lane_sums(resid)], axis=0)
    sums_ref[...] = jnp.broadcast_to(both[None], sums_ref.shape)


def direction_kernel(diag_ref, resid_ref, out_ref, resid_out):
    resid_out[...] = resid_ref[...]

    def cells(part, carry):
        at = pl.multiple_of(part * PACK, PACK)
        for u in range(VARS):
            out_ref[pl.ds(u * CELLS + at, PACK), :] = precondition(diag_ref, resid_ref, u, at)
        return carry

    lax.fori_loop(0, CELLS // PACK, cells, 0)


def finish_kernel(entries, sums_ref, x_ref, update_ref, out_ref):
    sums = jnp.sum(jnp.sum(sums_ref[...], axis=0), axis=1, keepdims=True) / entries + 1e-06
    cfl = STEP_CFL * jnp.sqrt(sums[0:1] / sums[1:2])
    out_ref[...] = x_ref[...] + cfl * update_ref[...]


VMEM = pl.BlockSpec(memory_space=pltpu.VMEM)
SMEM = pl.BlockSpec(memory_space=pltpu.SMEM)


def f32(*shape):
    return jax.ShapeDtypeStruct(shape, jnp.float32)


def bf16(*shape):
    return jax.ShapeDtypeStruct(shape, jnp.bfloat16)


def call(kernel, in_specs, out_shape, flops, moved, **more):
    many = isinstance(out_shape, (list, tuple))
    return pl.pallas_call(
        kernel,
        in_specs=in_specs,
        out_specs=more.pop("out_specs", [VMEM] * len(out_shape) if many else VMEM),
        out_shape=out_shape,
        compiler_params=pltpu.CompilerParams(vmem_limit_bytes=VMEM_LIMIT),
        cost_estimate=pl.CostEstimate(flops=flops, bytes_accessed=moved, transcendentals=0),
        **more,
    )


def shards(
    psi_init, source, coupling, diag_inv, neighbours, seam_perm, fringe_src, fringe_dst, fringe_weight
):
    blocks = psi_init.shape[0]
    slots = neighbours.shape[1]
    rim = seam_perm.shape[1]
    fringe = fringe_src.shape[1]
    peers = lax.axis_size("blk")
    devices = lax.axis_size("body") * peers
    up = [(i, (i + 1) % peers) for i in range(peers)]
    down = [(j, i) for i, j in up]
    here = functools.partial(pltpu.with_memory_space_constraint, memory_space=pltpu.HBM)
    x = here(psi_init.T)
    source_t = here(source.T)
    coup = here(coupling.transpose(1, 2, 3, 0))
    diag = here(diag_inv.transpose(1, 2, 0))
    nbr = here(neighbours.T)
    state = f32(BW, blocks)
    sent = [f32(fringe, BW), f32(rim, BW), f32(rim, BW)]
    size = 4 * BW * blocks
    square = bf16(LANES, LANES)

    donors = call(
        donors_kernel,
        [VMEM, VMEM, SMEM],
        sent + [bf16(blocks, fringe), square, square],
        4 * BW * blocks * fringe,
        2 * size,
    )
    hbm = pl.BlockSpec(memory_space=pltpu.HBM)
    chunks = blocks // LANES
    local_more = dict(
        flops=4 * BW * 2 * LANES * slots * blocks,
        moved=coup.size * 2 + 4 * size,
        scratch_shapes=[
            pltpu.VMEM((BW, blocks + LANES), jnp.bfloat16),
            pltpu.VMEM((BW, blocks + LANES), jnp.bfloat16),
            [pltpu.VMEM((BW, slots * LANES), jnp.float32)] * chunks,
            pltpu.VMEM((chunks, slots, VARS, BW, LANES), jnp.bfloat16),
            pltpu.VMEM((BW, blocks), jnp.float32),
            pltpu.SemaphoreType.DMA((chunks,)),
            pltpu.SemaphoreType.DMA,
        ],
    )
    first_local = call(
        functools.partial(first_local_kernel, rim),
        [VMEM, VMEM, hbm, hbm, VMEM, VMEM],
        [
            state,
            bf16(VARS, BW, LANES),
            f32(PACK, LANES),
            state,
            bf16(fringe + LANES, blocks),
            f32(1, fringe),
        ],
        **local_more,
    )
    local = call(functools.partial(local_kernel, rim), [VMEM, VMEM, hbm, hbm], state, **local_more)
    advance = call(
        advance_kernel,
        [VMEM] * 8 + [hbm] + [VMEM] * 4,
        [state, f32(1, LANES)] + sent,
        8 * BW * blocks * fringe,
        diag.size * 2 + 4 * size,
        scratch_shapes=[
            pltpu.VMEM((BW, blocks), jnp.float32),
            pltpu.VMEM((VARS, BW, blocks), jnp.bfloat16),
            pltpu.SemaphoreType.DMA,
        ],
    )
    residual = call(
        residual_kernel,
        [VMEM] * 9,
        [state, f32(peers, 2, LANES)],
        4 * BW * blocks * fringe,
        3 * size,
    )
    direction = call(
        direction_kernel, [VMEM] * 2, [state, state], diag.size * 2, diag.size * 2 + 2 * size
    )
    finish = call(
        functools.partial(finish_kernel, float(blocks * devices * BW)),
        [VMEM] * 3,
        state,
        2 * BW * blocks,
        3 * size,
    )

    def exchange(rows, to_up, to_down):
        rows = lax.all_to_all(rows, ("body", "blk"), split_axis=0, concat_axis=0, tiled=True)
        return rows, lax.ppermute(to_up, "blk", up), lax.ppermute(to_down, "blk", down)

    *out, table, sel_up, sel_down = donors(x, here(fringe_src), here(seam_perm))
    arrived = exchange(*out)
    part, rimcoup, rimrow, x, across, weight = first_local(
        x, nbr, coup, source_t, here(fringe_dst), here(fringe_weight)
    )
    across = (across, weight, rimcoup, rimrow)
    x, norm, *out = advance(part, *arrived, *across, diag, x, table, sel_up, sel_down)
    arrived = exchange(*out)
    part = local(x, nbr, coup, source_t)
    resid, sums = residual(part, *arrived, *across, norm)
    sums = lax.all_to_all(sums, "blk", split_axis=0, concat_axis=0, tiled=True)
    sums = jnp.broadcast_to(jnp.sum(sums, axis=0, keepdims=True), (devices // peers, 2, LANES))
    sums = lax.all_to_all(sums, "body", split_axis=0, concat_axis=0, tiled=True)
    update, resid = direction(diag, resid)
    x = finish(sums, x, update)
    return (x.T, resid.T)


def solution(mesh):
    return jax.shard_map(
        shards,
        mesh=mesh,
        in_specs=(
            P(("body", "blk"), None),
            P(("body", "blk"), None),
            P(("body", "blk"), None, None, None),
            P(("body", "blk"), None, None),
            P(("body", "blk"), None),
            P("body", None),
            P(("body", "blk"), None),
            P(("body", "blk"), None),
            P(("body", "blk"), None),
        ),
        out_specs=(P(("body", "blk"), None), P(("body", "blk"), None)),
        check_vma=False,
    )
```

```python
import functools
import math

import jax
import jax.numpy as jnp
from jax import lax
from jax.experimental import pallas as pl
from jax.experimental.pallas import tpu as pltpu
from jax.sharding import PartitionSpec as P

CELLS = 64
VARS = 5
BW = 320
STEP_CFL = 0.5
LANES = 128
PACK = 16
VMEM_LIMIT = 32 * 1024 * 1024


def split(x):
    high = x.astype(jnp.bfloat16)
    return high, (x - high.astype(jnp.float32)).astype(jnp.bfloat16)


def onehot(mask):
    return jnp.where(mask, 1.0, 0.0).astype(jnp.bfloat16)


def pick(x, table):
    high, low = split(x)
    return jnp.dot(high, table, preferred_element_type=jnp.float32) + jnp.dot(
        low, table, preferred_element_type=jnp.float32
    )


def send_blocks(x, table, sel_up, sel_down, out_ref, up_ref, down_ref, rows_ref, sem):
    rim = up_ref.shape[0]
    half = rows_ref.shape[2]
    rows = pick(x, table).T.reshape(rows_ref.shape[0], 2 * half, BW)
    for h in range(2):
        for tile in range(2):
            rows_ref[:, 2 * tile + h] = rows[:, h * half : (h + 1) * half, tile * LANES : (tile + 1) * LANES]
    rest = rows[:, :, 2 * LANES :]
    rows_ref[:, 4] = jnp.concatenate([rest[:, :half], rest[:, half:]], axis=2)
    copy = pltpu.make_async_copy(rows_ref, out_ref, sem)
    copy.start()
    index = lax.axis_index("blk")
    at_last = index == lax.axis_size("blk") - 1
    at_first = index == 0
    rims = pick(x[:, x.shape[1] - LANES :], sel_up) + pick(x[:, :LANES], sel_down)
    lane = lax.broadcasted_iota(jnp.int32, (1, LANES), 1)
    turn_up = (lane < rim) & at_last
    turn_down = (lane >= rim) & at_first
    angle = 2.0 * math.pi / 3.0
    cosine = jnp.where(turn_up | turn_down, math.cos(angle), 1.0)
    sine = jnp.where(turn_up, math.sin(angle), jnp.where(turn_down, -math.sin(angle), 0.0))
    first = rims[2 * CELLS : 3 * CELLS]
    second = rims[3 * CELLS : 4 * CELLS]
    rims = jnp.concatenate(
        [
            rims[: 2 * CELLS],
            cosine * first - sine * second,
            sine * first + cosine * second,
            rims[4 * CELLS :],
        ],
        axis=0,
    ).T
    up_ref[...] = rims[:rim]
    down_ref[...] = rims[rim : 2 * rim]
    return copy


def donors_kernel(
    x_ref, src_ref, perm_ref,
    out_ref, up_ref, down_ref, table_ref, sel_up_ref, sel_down_ref, x_out, rows_ref, sem,
):
    rim = up_ref.shape[0]
    index = lax.axis_index("blk")
    at_last = index == lax.axis_size("blk") - 1
    at_first = index == 0
    sub = lax.broadcasted_iota(jnp.int32, (LANES, LANES), 0)
    lane = lax.broadcasted_iota(jnp.int32, (LANES, LANES), 1)
    wanted = lane[:1]
    target = sub[:, :1]
    for j in range(rim):
        partner = perm_ref[0, j]
        wanted = jnp.where((lane[:1] == j) & at_last, partner, wanted)
        target = jnp.where((sub[:, :1] == j) & at_first, partner, target)
    sel_up = onehot((sub == wanted + (LANES - rim)) & (lane < rim))
    sel_down = onehot((target + rim == lane) & (sub < rim))
    rows = lax.broadcasted_iota(jnp.int32, table_ref.shape, 0)
    table = onehot(rows == src_ref[...])
    copy = send_blocks(
        x_ref[...], table, sel_up, sel_down, out_ref, up_ref, down_ref, rows_ref, sem
    )
    table_ref[...] = table
    sel_up_ref[...] = sel_up
    sel_down_ref[...] = sel_down
    x_out[...] = x_ref[...]
    copy.wait()


def local_kernel(
    rim, x_ref, nbr_ref, coup_ref, source_ref, out_ref, high, low, near, coup, source, sems, source_sem,
    beside=None,
):
    slots, blocks = nbr_ref.shape
    chunks = blocks // LANES
    spans = [slice(c * LANES, (c + 1) * LANES) for c in range(chunks)]
    copies = [
        pltpu.make_async_copy(coup_ref.at[:, :, :, spans[c]], coup.at[c], sems.at[c])
        for c in range(chunks)
    ]
    for copy in copies:
        copy.start()
    source_copy = pltpu.make_async_copy(source_ref, source, source_sem)
    source_copy.start()
    lane = lax.broadcasted_iota(jnp.int32, (BW, LANES), 1)
    moved = pltpu.roll(x_ref[...], rim, 1)
    head = jnp.where(lane < rim, 0.0, moved[:, :LANES])
    tail = jnp.where(lane < rim, moved[:, :LANES], 0.0)
    high[...], low[...] = split(jnp.concatenate([head, moved[:, LANES:], tail], axis=1))
    rows = lax.broadcasted_iota(jnp.int32, (2 * LANES, LANES), 0)

    def gather(c):
        window = slice(c * LANES, (c + 2) * LANES)
        table = jnp.concatenate(
            [onehot(rows == nbr_ref[m : m + 1, spans[c]] - c * LANES) for m in range(slots)], axis=1
        )
        near[c][...] = jnp.dot(high[:, window], table, preferred_element_type=jnp.float32) + jnp.dot(
            low[:, window], table, preferred_element_type=jnp.float32
        )

    gather(0)
    for c in range(chunks):
        copies[c].wait()
        if c == 0:
            source_copy.wait()
        if c + 1 < chunks:
            gather(c + 1)
        if beside is not None:
            beside(c)
        for at in range(0, CELLS, PACK):
            total = [None] * VARS
            for m in range(slots):
                for v in range(VARS):
                    span = slice(v * CELLS + at, v * CELLS + at + PACK)
                    value = near[c][span, m * LANES : (m + 1) * LANES]
                    for u in range(VARS):
                        term = coup[c, m, u, span, :].astype(jnp.float32) * value
                        total[u] = term if total[u] is None else total[u] + term
            for u in range(VARS):
                span = slice(u * CELLS + at, u * CELLS + at + PACK)
                out_ref[span, spans[c]] = source[span, spans[c]] - x_ref[span, spans[c]] + total[u]


def first_local_kernel(
    rim, x_ref, nbr_ref, coup_ref, source_ref, dst_ref, weight_ref,
    out_ref, rimcoup_ref, rimrow_ref, table_ref, weight_out,
    high, low, near, coup, source, sems, source_sem, lower_end,
):
    slots, blocks = nbr_ref.shape
    chunks = blocks // LANES
    fringe = dst_ref.shape[1]
    sub = lax.broadcasted_iota(jnp.int32, (LANES, LANES), 0)
    lane = lax.broadcasted_iota(jnp.int32, (LANES, LANES), 1)

    def place(first, to):
        at = sub - first
        inside = (at >= 0) & (at < rim)
        return jnp.concatenate(
            [onehot((lane == at + to + m * 2 * rim) & inside) for m in range(slots)], axis=0
        )

    def read(rows, table):
        rows = jnp.broadcast_to(jnp.concatenate(rows, axis=1), (PACK, slots * LANES))
        rows = rows.astype(jnp.float32).astype(jnp.bfloat16)
        return jnp.dot(rows, table, preferred_element_type=jnp.float32)

    def beside(c):
        if c not in (0, chunks - 1):
            return
        table = place(0, 0) if c == 0 else place(LANES - rim, rim)
        rows = [nbr_ref[m : m + 1, c * LANES : (c + 1) * LANES] for m in range(slots)]
        if c == 0:
            rows = [jnp.where(row < rim, row + 1, 0) for row in rows]
            rimrow_ref[...] = read(rows, table)
        else:
            rows = [jnp.where(row >= blocks + rim, row - blocks + 1, 0) for row in rows]
            rimrow_ref[...] += read(rows, table)
        for u in range(VARS):
            rows = jnp.concatenate([coup[c, m, u] for m in range(slots)], axis=1)
            moved = jnp.dot(rows, table, preferred_element_type=jnp.float32)
            if c == 0:
                lower_end[u] = moved
            else:
                rimcoup_ref[u] = (lower_end[u] + moved).astype(jnp.bfloat16)

    local_kernel(
        rim, x_ref, nbr_ref, coup_ref, source_ref, out_ref, high, low, near, coup, source, sems, source_sem,
        beside,
    )
    half = rim // 2
    column = lax.broadcasted_iota(jnp.int32, (fringe, fringe), 1)
    within = lax.rem(column, fringe // 2)
    slot = 2 * within - lax.rem(within, half) + jnp.where(column < fringe // 2, 0, half)
    order = onehot(lax.broadcasted_iota(jnp.int32, (fringe, fringe), 0) == slot)
    weights = jnp.broadcast_to(weight_ref[...], (PACK, fringe))
    top = weights.astype(jnp.bfloat16)
    rest = pick(weights - top.astype(jnp.float32), order)
    weight_out[...] = (jnp.dot(top, order, preferred_element_type=jnp.float32) + rest)[:1]
    targets = pick(jnp.broadcast_to(dst_ref[...], (LANES, fringe)).astype(jnp.float32), order).T
    targets = targets.astype(jnp.int32)
    edge = lax.rem(sub, 2 * rim)
    edge = jnp.where(edge < rim, edge, edge + (blocks - 2 * rim))
    for c in range(chunks):
        span = slice(c * LANES, (c + 1) * LANES)
        block = lane[:1] + c * LANES
        table_ref[:fringe, span] = onehot(targets == block)
        table_ref[fringe:, span] = onehot(edge == block)


def full_residual(local_ref, inc_ref, lower_ref, upper_ref, table_ref, weight_ref, rimcoup_ref, rimrow_ref):
    rim = lower_ref.shape[0]
    rims = jnp.concatenate(
        [lower_ref[...], upper_ref[...], jnp.zeros((LANES - 2 * rim, BW), jnp.float32)], axis=0
    ).T
    sub = lax.broadcasted_iota(jnp.int32, (LANES, LANES), 0)
    near = pick(rims, onehot(sub + 1 == rimrow_ref[:1].astype(jnp.int32)))
    edge = []
    for u in range(VARS):
        total = None
        for v in range(VARS):
            span = slice(v * CELLS, (v + 1) * CELLS)
            term = rimcoup_ref[u, span, :].astype(jnp.float32) * near[span]
            total = term if total is None else total + term
        edge.append(total)
    edge = jnp.concatenate(edge, axis=0)
    tiles = [inc_ref[:, tile].reshape(-1, LANES).T for tile in range(inc_ref.shape[1])]
    fringe = [
        jnp.concatenate([tiles[h], tiles[2 + h], tiles[4][h * CELLS : (h + 1) * CELLS]], axis=0)
        for h in range(2)
    ]
    arrived = jnp.concatenate([jnp.concatenate(fringe, axis=1) * weight_ref[...], edge], axis=1)
    return local_ref[...] + pick(arrived, table_ref[...])


def precondition(diag_ref, resid_ref, u, at):
    total = None
    for v in range(VARS):
        span = pl.ds(v * CELLS + at, PACK)
        term = diag_ref[u, span, :].astype(jnp.float32) * resid_ref[span, :]
        total = term if total is None else total + term
    return total


def lane_sums(resid):
    square = jnp.sum(resid * resid, axis=0, keepdims=True)
    return sum(square[:, i : i + LANES] for i in range(0, square.shape[1], LANES))


def advance_kernel(
    local_ref, inc_ref, lower_ref, upper_ref, across_ref, weight_ref, rimcoup_ref, rimrow_ref,
    diag_ref, x_ref, table_ref, sel_up_ref, sel_down_ref,
    next_ref, norm_ref, out_ref, up_ref, down_ref, resid, diag, diag_sems, rows_ref, sem,
):
    parts = CELLS // PACK
    fetches = []
    for part in range(parts):
        span = pl.ds(part * PACK, PACK)
        fetches.append(
            pltpu.make_async_copy(
                diag_ref.at[:, :, span], diag.at[:, :, span], diag_sems.at[part]
            )
        )
        fetches[part].start()
    resid[...] = full_residual(
        local_ref, inc_ref, lower_ref, upper_ref, across_ref, weight_ref, rimcoup_ref, rimrow_ref
    )
    for part in range(parts):
        fetches[part].wait()
        at = part * PACK
        for u in range(VARS):
            total = None
            for v in range(VARS):
                term = diag[u, v, at : at + PACK].astype(jnp.float32)
                term = term * resid[v * CELLS + at : v * CELLS + at + PACK]
                total = term if total is None else total + term
            span = slice(u * CELLS + at, u * CELLS + at + PACK)
            next_ref[span, :] = x_ref[span, :] + STEP_CFL * total
    copy = send_blocks(
        next_ref[...], table_ref[...], sel_up_ref[...], sel_down_ref[...],
        out_ref, up_ref, down_ref, rows_ref, sem,
    )
    norm_ref[...] = lane_sums(resid[...])
    copy.wait()


def residual_kernel(
    local_ref, inc_ref, lower_ref, upper_ref, across_ref, weight_ref, rimcoup_ref, rimrow_ref, norm_ref,
    resid_ref, sums_ref,
):
    resid = full_residual(
        local_ref, inc_ref, lower_ref, upper_ref, across_ref, weight_ref, rimcoup_ref, rimrow_ref
    )
    resid_ref[...] = resid
    both = jnp.concatenate([norm_ref[...], lane_sums(resid)], axis=0)
    sums_ref[...] = jnp.broadcast_to(both[None], sums_ref.shape)


def direction_kernel(diag_ref, resid_ref, out_ref, resid_out):
    resid_out[...] = resid_ref[...]

    def cells(part, carry):
        at = pl.multiple_of(part * PACK, PACK)
        for u in range(VARS):
            out_ref[pl.ds(u * CELLS + at, PACK), :] = precondition(diag_ref, resid_ref, u, at)
        return carry

    lax.fori_loop(0, CELLS // PACK, cells, 0)


def finish_kernel(entries, sums_ref, x_ref, update_ref, out_ref):
    sums = jnp.sum(jnp.sum(sums_ref[...], axis=0), axis=1, keepdims=True) / entries + 1e-06
    cfl = STEP_CFL * jnp.sqrt(sums[0:1] / sums[1:2])
    out_ref[...] = x_ref[...] + cfl * update_ref[...]


VMEM = pl.BlockSpec(memory_space=pltpu.VMEM)
SMEM = pl.BlockSpec(memory_space=pltpu.SMEM)


def f32(*shape):
    return jax.ShapeDtypeStruct(shape, jnp.float32)


def bf16(*shape):
    return jax.ShapeDtypeStruct(shape, jnp.bfloat16)


def call(kernel, in_specs, out_shape, flops, moved, **more):
    many = isinstance(out_shape, (list, tuple))
    return pl.pallas_call(
        kernel,
        in_specs=in_specs,
        out_specs=more.pop("out_specs", [VMEM] * len(out_shape) if many else VMEM),
        out_shape=out_shape,
        compiler_params=pltpu.CompilerParams(vmem_limit_bytes=VMEM_LIMIT),
        cost_estimate=pl.CostEstimate(flops=flops, bytes_accessed=moved, transcendentals=0),
        **more,
    )


def shards(
    psi_init, source, coupling, diag_inv, neighbours, seam_perm, fringe_src, fringe_dst, fringe_weight
):
    blocks = psi_init.shape[0]
    slots = neighbours.shape[1]
    rim = seam_perm.shape[1]
    fringe = fringe_src.shape[1]
    peers = lax.axis_size("blk")
    devices = lax.axis_size("body") * peers
    up = [(i, (i + 1) % peers) for i in range(peers)]
    down = [(j, i) for i, j in up]
    here = functools.partial(pltpu.with_memory_space_constraint, memory_space=pltpu.HBM)
    x = here(psi_init.T)
    source_t = here(source.T)
    coup = here(coupling.transpose(1, 2, 3, 0))
    diag = here(diag_inv.transpose(1, 2, 0))
    nbr = here(neighbours.T)
    state = f32(BW, blocks)
    hbm = pl.BlockSpec(memory_space=pltpu.HBM)
    message = (devices, BW * fringe // devices // (rim // 2 * LANES), rim // 2, LANES)
    sent = [f32(*message), f32(rim, BW), f32(rim, BW)]
    rows_scratch = [pltpu.VMEM(message, jnp.float32), pltpu.SemaphoreType.DMA]
    size = 4 * BW * blocks
    square = bf16(LANES, LANES)

    donors = call(
        donors_kernel,
        [VMEM, VMEM, SMEM],
        sent + [bf16(blocks, fringe), square, square, state],
        4 * BW * blocks * fringe,
        2 * size,
        out_specs=[hbm] + [VMEM] * 6,
        scratch_shapes=rows_scratch,
    )
    chunks = blocks // LANES
    scratch = [
        pltpu.VMEM((BW, blocks + LANES), jnp.bfloat16),
        pltpu.VMEM((BW, blocks + LANES), jnp.bfloat16),
        [pltpu.VMEM((BW, slots * LANES), jnp.float32)] * chunks,
        pltpu.VMEM((chunks, slots, VARS, BW, LANES), jnp.bfloat16),
        pltpu.VMEM((BW, blocks), jnp.float32),
        pltpu.SemaphoreType.DMA((chunks,)),
        pltpu.SemaphoreType.DMA,
    ]
    local_more = dict(
        flops=4 * BW * 2 * LANES * slots * blocks,
        moved=coup.size * 2 + 4 * size,
        scratch_shapes=scratch,
    )
    first_local = call(
        functools.partial(first_local_kernel, rim),
        [VMEM, VMEM, hbm, hbm, VMEM, VMEM],
        [
            state,
            bf16(VARS, BW, LANES),
            f32(PACK, LANES),
            bf16(fringe + LANES, blocks),
            f32(1, fringe),
        ],
        **dict(local_more, scratch_shapes=scratch + [pltpu.VMEM((VARS, BW, LANES), jnp.float32)]),
    )
    local = call(functools.partial(local_kernel, rim), [VMEM, VMEM, hbm, hbm], state, **local_more)
    advance = call(
        advance_kernel,
        [VMEM] * 8 + [hbm] + [VMEM] * 4,
        [state, f32(1, LANES)] + sent,
        8 * BW * blocks * fringe,
        diag.size * 2 + 4 * size,
        out_specs=[VMEM, VMEM, hbm, VMEM, VMEM],
        scratch_shapes=[
            pltpu.VMEM((BW, blocks), jnp.float32),
            pltpu.VMEM((VARS, VARS, CELLS, blocks), jnp.bfloat16),
            pltpu.SemaphoreType.DMA((CELLS // PACK,)),
        ]
        + rows_scratch,
    )
    residual = call(
        residual_kernel,
        [VMEM] * 9,
        [state, f32(devices, 2, LANES)],
        4 * BW * blocks * fringe,
        3 * size,
    )
    direction = call(
        direction_kernel, [VMEM] * 2, [state, state], diag.size * 2, diag.size * 2 + 2 * size
    )
    finish = call(
        functools.partial(finish_kernel, float(blocks * devices * BW)),
        [VMEM] * 3,
        state,
        2 * BW * blocks,
        3 * size,
    )

    def exchange(rows, to_up, to_down):
        rows = lax.all_to_all(rows, ("body", "blk"), split_axis=0, concat_axis=0, tiled=True)
        return rows, lax.ppermute(to_up, "blk", up), lax.ppermute(to_down, "blk", down)

    *out, table, sel_up, sel_down, x_here = donors(x, here(fringe_src), here(seam_perm))
    arrived = exchange(*out)
    part, rimcoup, rimrow, across, weight = first_local(
        x_here, nbr, coup, source_t, here(fringe_dst), here(fringe_weight)
    )
    across = (across, weight, rimcoup, rimrow)
    parts = here(diag_inv.transpose(1, 2, 0).reshape(VARS, VARS, CELLS, blocks))
    x, norm, *out = advance(part, *arrived, *across, parts, x_here, table, sel_up, sel_down)
    arrived = exchange(*out)
    part = local(x, nbr, coup, source_t)
    resid, sums = residual(part, *arrived, *across, norm)
    sums = lax.all_to_all(sums, ("body", "blk"), split_axis=0, concat_axis=0, tiled=True)
    update, resid = direction(diag, resid)
    x = finish(sums, x, update)
    return (x.T, resid.T)


def solution(mesh):
    return jax.shard_map(
        shards,
        mesh=mesh,
        in_specs=(
            P(("body", "blk"), None),
            P(("body", "blk"), None),
            P(("body", "blk"), None, None, None),
            P(("body", "blk"), None, None),
            P(("body", "blk"), None),
            P("body", None),
            P(("body", "blk"), None),
            P(("body", "blk"), None),
            P(("body", "blk"), None),
        ),
        out_specs=(P(("body", "blk"), None), P(("body", "blk"), None)),
        check_vma=False,
    )
```

```python
import functools
import math

import jax
import jax.numpy as jnp
from jax import lax
from jax.experimental import pallas as pl
from jax.experimental.pallas import tpu as pltpu
from jax.sharding import PartitionSpec as P

CELLS = 64
VARS = 5
BW = 320
STEP_CFL = 0.5
LANES = 128
PACK = 16
VMEM_LIMIT = 32 * 1024 * 1024


def split(x):
    high = x.astype(jnp.bfloat16)
    return high, (x - high.astype(jnp.float32)).astype(jnp.bfloat16)


def onehot(mask):
    return jnp.where(mask, 1.0, 0.0).astype(jnp.bfloat16)


def pick(x, table):
    high, low = split(x)
    return jnp.dot(high, table, preferred_element_type=jnp.float32) + jnp.dot(
        low, table, preferred_element_type=jnp.float32
    )


def send_blocks(x, table, sel_up, sel_down, out_ref, up_ref, down_ref, rows_ref, sem):
    rim = up_ref.shape[0]
    half = rows_ref.shape[2]
    rows = pick(x, table).T.reshape(rows_ref.shape[0], 2 * half, BW)
    for h in range(2):
        for tile in range(2):
            rows_ref[:, 2 * tile + h] = rows[:, h * half : (h + 1) * half, tile * LANES : (tile + 1) * LANES]
    rest = rows[:, :, 2 * LANES :]
    rows_ref[:, 4] = jnp.concatenate([rest[:, :half], rest[:, half:]], axis=2)
    copy = pltpu.make_async_copy(rows_ref, out_ref, sem)
    copy.start()
    index = lax.axis_index("blk")
    at_last = index == lax.axis_size("blk") - 1
    at_first = index == 0
    rims = pick(x[:, x.shape[1] - LANES :], sel_up) + pick(x[:, :LANES], sel_down)
    lane = lax.broadcasted_iota(jnp.int32, (1, LANES), 1)
    turn_up = (lane < rim) & at_last
    turn_down = (lane >= rim) & at_first
    angle = 2.0 * math.pi / 3.0
    cosine = jnp.where(turn_up | turn_down, math.cos(angle), 1.0)
    sine = jnp.where(turn_up, math.sin(angle), jnp.where(turn_down, -math.sin(angle), 0.0))
    first = rims[2 * CELLS : 3 * CELLS]
    second = rims[3 * CELLS : 4 * CELLS]
    rims = jnp.concatenate(
        [
            rims[: 2 * CELLS],
            cosine * first - sine * second,
            sine * first + cosine * second,
            rims[4 * CELLS :],
        ],
        axis=0,
    ).T
    up_ref[...] = rims[:rim]
    down_ref[...] = rims[rim : 2 * rim]
    return copy


def donors_kernel(
    x_ref, src_ref, perm_ref,
    out_ref, up_ref, down_ref, table_ref, sel_up_ref, sel_down_ref, x_out, rows_ref, sem,
):
    rim = up_ref.shape[0]
    index = lax.axis_index("blk")
    at_last = index == lax.axis_size("blk") - 1
    at_first = index == 0
    sub = lax.broadcasted_iota(jnp.int32, (LANES, LANES), 0)
    lane = lax.broadcasted_iota(jnp.int32, (LANES, LANES), 1)
    wanted = lane[:1]
    target = sub[:, :1]
    for j in range(rim):
        partner = perm_ref[0, j]
        wanted = jnp.where((lane[:1] == j) & at_last, partner, wanted)
        target = jnp.where((sub[:, :1] == j) & at_first, partner, target)
    sel_up = onehot((sub == wanted + (LANES - rim)) & (lane < rim))
    sel_down = onehot((target + rim == lane) & (sub < rim))
    rows = lax.broadcasted_iota(jnp.int32, table_ref.shape, 0)
    table = onehot(rows == src_ref[...])
    copy = send_blocks(
        x_ref[...], table, sel_up, sel_down, out_ref, up_ref, down_ref, rows_ref, sem
    )
    table_ref[...] = table
    sel_up_ref[...] = sel_up
    sel_down_ref[...] = sel_down
    x_out[...] = x_ref[...]
    copy.wait()


def local_kernel(
    rim, x_ref, nbr_ref, coup_ref, source_ref, out_ref, high, low, near, coup, source, sems, source_sem,
    beside=None,
):
    slots, blocks = nbr_ref.shape
    chunks = blocks // LANES
    spans = [slice(c * LANES, (c + 1) * LANES) for c in range(chunks)]
    copies = [
        pltpu.make_async_copy(coup_ref.at[:, :, :, spans[c]], coup.at[c], sems.at[c])
        for c in range(chunks)
    ]
    for copy in copies:
        copy.start()
    source_copy = pltpu.make_async_copy(source_ref, source, source_sem)
    source_copy.start()
    lane = lax.broadcasted_iota(jnp.int32, (BW, LANES), 1)
    moved = pltpu.roll(x_ref[...], rim, 1)
    head = jnp.where(lane < rim, 0.0, moved[:, :LANES])
    tail = jnp.where(lane < rim, moved[:, :LANES], 0.0)
    high[...], low[...] = split(jnp.concatenate([head, moved[:, LANES:], tail], axis=1))
    rows = lax.broadcasted_iota(jnp.int32, (2 * LANES, LANES), 0)

    def gather(c):
        window = slice(c * LANES, (c + 2) * LANES)
        table = jnp.concatenate(
            [onehot(rows == nbr_ref[m : m + 1, spans[c]] - c * LANES) for m in range(slots)], axis=1
        )
        near[c][...] = jnp.dot(high[:, window], table, preferred_element_type=jnp.float32) + jnp.dot(
            low[:, window], table, preferred_element_type=jnp.float32
        )

    gather(0)
    for c in range(chunks):
        copies[c].wait()
        if c == 0:
            source_copy.wait()
        if c + 1 < chunks:
            gather(c + 1)
        if beside is not None:
            beside(c)
        for at in range(0, CELLS, PACK):
            total = [None] * VARS
            for m in range(slots):
                for v in range(VARS):
                    span = slice(v * CELLS + at, v * CELLS + at + PACK)
                    value = near[c][span, m * LANES : (m + 1) * LANES]
                    for u in range(VARS):
                        term = coup[c, m, u, span, :].astype(jnp.float32) * value
                        total[u] = term if total[u] is None else total[u] + term
            for u in range(VARS):
                span = slice(u * CELLS + at, u * CELLS + at + PACK)
                out_ref[span, spans[c]] = source[span, spans[c]] - x_ref[span, spans[c]] + total[u]


def first_local_kernel(
    rim, x_ref, nbr_ref, coup_ref, source_ref, dst_ref, weight_ref,
    out_ref, rimcoup_ref, rimrow_ref, table_ref, weight_out,
    high, low, near, coup, source, sems, source_sem, lower_end,
):
    slots, blocks = nbr_ref.shape
    chunks = blocks // LANES
    fringe = dst_ref.shape[1]
    sub = lax.broadcasted_iota(jnp.int32, (LANES, LANES), 0)
    lane = lax.broadcasted_iota(jnp.int32, (LANES, LANES), 1)

    def place(first, to):
        at = sub - first
        inside = (at >= 0) & (at < rim)
        return jnp.concatenate(
            [onehot((lane == at + to + m * 2 * rim) & inside) for m in range(slots)], axis=0
        )

    def read(rows, table):
        rows = jnp.broadcast_to(jnp.concatenate(rows, axis=1), (PACK, slots * LANES))
        rows = rows.astype(jnp.float32).astype(jnp.bfloat16)
        return jnp.dot(rows, table, preferred_element_type=jnp.float32)

    def beside(c):
        if c not in (0, chunks - 1):
            return
        table = place(0, 0) if c == 0 else place(LANES - rim, rim)
        rows = [nbr_ref[m : m + 1, c * LANES : (c + 1) * LANES] for m in range(slots)]
        if c == 0:
            rows = [jnp.where(row < rim, row + 1, 0) for row in rows]
            rimrow_ref[...] = read(rows, table)
        else:
            rows = [jnp.where(row >= blocks + rim, row - blocks + 1, 0) for row in rows]
            rimrow_ref[...] += read(rows, table)
        rows = jnp.concatenate([coup[c, m].reshape(VARS * BW, LANES) for m in range(slots)], axis=1)
        moved = jnp.dot(rows, table, preferred_element_type=jnp.float32)
        if c == 0:
            lower_end[...] = moved
        else:
            moved = (lower_end[...] + moved).astype(jnp.bfloat16)
            rimcoup_ref[...] = moved.reshape(VARS, BW, LANES)

    local_kernel(
        rim, x_ref, nbr_ref, coup_ref, source_ref, out_ref, high, low, near, coup, source, sems, source_sem,
        beside,
    )
    weight_out[...] = weight_ref[...]
    targets = jnp.broadcast_to(dst_ref[...], (LANES, fringe)).T
    edge = lax.rem(sub, 2 * rim)
    edge = jnp.where(edge < rim, edge, edge + (blocks - 2 * rim))
    for c in range(chunks):
        span = slice(c * LANES, (c + 1) * LANES)
        block = lane[:1] + c * LANES
        table_ref[:fringe, span] = onehot(targets == block)
        table_ref[fringe:, span] = onehot(edge == block)


def full_residual(local_ref, inc_ref, lower_ref, upper_ref, table_ref, weight_ref, rimcoup_ref, rimrow_ref):
    rim = lower_ref.shape[0]
    rims = jnp.concatenate(
        [lower_ref[...], upper_ref[...], jnp.zeros((LANES - 2 * rim, BW), jnp.float32)], axis=0
    ).T
    sub = lax.broadcasted_iota(jnp.int32, (LANES, LANES), 0)
    near = pick(rims, onehot(sub + 1 == rimrow_ref[:1].astype(jnp.int32)))
    edge = []
    for u in range(VARS):
        total = None
        for v in range(VARS):
            span = slice(v * CELLS, (v + 1) * CELLS)
            term = rimcoup_ref[u, span, :].astype(jnp.float32) * near[span]
            total = term if total is None else total + term
        edge.append(total)
    edge = jnp.concatenate(edge, axis=0)
    rest = inc_ref[:, 4]
    rest = jnp.concatenate([rest[:, :, :CELLS], rest[:, :, CELLS:]], axis=1).reshape(-1, CELLS)
    fringe = [inc_ref[:, 0:2].reshape(-1, LANES).T, inc_ref[:, 2:4].reshape(-1, LANES).T, rest.T]
    arrived = jnp.concatenate([jnp.concatenate(fringe, axis=0) * weight_ref[...], edge], axis=1)
    return local_ref[...] + pick(arrived, table_ref[...])


def precondition(diag_ref, resid_ref, u, at):
    total = None
    for v in range(VARS):
        span = pl.ds(v * CELLS + at, PACK)
        term = diag_ref[u, span, :].astype(jnp.float32) * resid_ref[span, :]
        total = term if total is None else total + term
    return total


def lane_sums(resid):
    square = jnp.sum(resid * resid, axis=0, keepdims=True)
    return sum(square[:, i : i + LANES] for i in range(0, square.shape[1], LANES))


def advance_kernel(
    local_ref, inc_ref, lower_ref, upper_ref, across_ref, weight_ref, rimcoup_ref, rimrow_ref,
    diag_ref, x_ref, table_ref, sel_up_ref, sel_down_ref,
    next_ref, norm_ref, out_ref, up_ref, down_ref, resid, diag, diag_sems, rows_ref, sem,
):
    parts = CELLS // PACK
    fetches = []
    for part in range(parts):
        span = pl.ds(part * PACK, PACK)
        fetches.append(
            pltpu.make_async_copy(
                diag_ref.at[:, :, span], diag.at[:, :, span], diag_sems.at[part]
            )
        )
        fetches[part].start()
    resid[...] = full_residual(
        local_ref, inc_ref, lower_ref, upper_ref, across_ref, weight_ref, rimcoup_ref, rimrow_ref
    )
    for part in range(parts):
        fetches[part].wait()
        at = part * PACK
        for u in range(VARS):
            total = None
            for v in range(VARS):
                term = diag[u, v, at : at + PACK].astype(jnp.float32)
                term = term * resid[v * CELLS + at : v * CELLS + at + PACK]
                total = term if total is None else total + term
            span = slice(u * CELLS + at, u * CELLS + at + PACK)
            next_ref[span, :] = x_ref[span, :] + STEP_CFL * total
    copy = send_blocks(
        next_ref[...], table_ref[...], sel_up_ref[...], sel_down_ref[...],
        out_ref, up_ref, down_ref, rows_ref, sem,
    )
    norm_ref[...] = lane_sums(resid[...])
    copy.wait()


def residual_kernel(
    local_ref, inc_ref, lower_ref, upper_ref, across_ref, weight_ref, rimcoup_ref, rimrow_ref, norm_ref,
    resid_ref, sums_ref,
):
    resid = full_residual(
        local_ref, inc_ref, lower_ref, upper_ref, across_ref, weight_ref, rimcoup_ref, rimrow_ref
    )
    resid_ref[...] = resid
    both = jnp.concatenate([norm_ref[...], lane_sums(resid)], axis=0)
    sums_ref[...] = jnp.broadcast_to(both[None], sums_ref.shape)


def direction_kernel(diag_ref, resid_ref, out_ref, resid_out):
    resid_out[...] = resid_ref[...]

    def cells(part, carry):
        at = pl.multiple_of(part * PACK, PACK)
        for u in range(VARS):
            out_ref[pl.ds(u * CELLS + at, PACK), :] = precondition(diag_ref, resid_ref, u, at)
        return carry

    lax.fori_loop(0, CELLS // PACK, cells, 0)


def finish_kernel(entries, sums_ref, x_ref, update_ref, out_ref):
    sums = jnp.sum(jnp.sum(sums_ref[...], axis=0), axis=1, keepdims=True) / entries + 1e-06
    cfl = STEP_CFL * jnp.sqrt(sums[0:1] / sums[1:2])
    out_ref[...] = x_ref[...] + cfl * update_ref[...]


VMEM = pl.BlockSpec(memory_space=pltpu.VMEM)
SMEM = pl.BlockSpec(memory_space=pltpu.SMEM)


def f32(*shape):
    return jax.ShapeDtypeStruct(shape, jnp.float32)


def bf16(*shape):
    return jax.ShapeDtypeStruct(shape, jnp.bfloat16)


def call(kernel, in_specs, out_shape, flops, moved, **more):
    many = isinstance(out_shape, (list, tuple))
    return pl.pallas_call(
        kernel,
        in_specs=in_specs,
        out_specs=more.pop("out_specs", [VMEM] * len(out_shape) if many else VMEM),
        out_shape=out_shape,
        compiler_params=pltpu.CompilerParams(vmem_limit_bytes=VMEM_LIMIT),
        cost_estimate=pl.CostEstimate(flops=flops, bytes_accessed=moved, transcendentals=0),
        **more,
    )


def shards(
    psi_init, source, coupling, diag_inv, neighbours, seam_perm, fringe_src, fringe_dst, fringe_weight
):
    blocks = psi_init.shape[0]
    slots = neighbours.shape[1]
    rim = seam_perm.shape[1]
    fringe = fringe_src.shape[1]
    peers = lax.axis_size("blk")
    devices = lax.axis_size("body") * peers
    up = [(i, (i + 1) % peers) for i in range(peers)]
    down = [(j, i) for i, j in up]
    here = functools.partial(pltpu.with_memory_space_constraint, memory_space=pltpu.HBM)
    x = here(psi_init.T)
    source_t = here(source.T)
    coup = here(coupling.transpose(1, 2, 3, 0))
    diag = here(diag_inv.transpose(1, 2, 0))
    nbr = here(neighbours.T)
    state = f32(BW, blocks)
    hbm = pl.BlockSpec(memory_space=pltpu.HBM)
    message = (devices, BW * fringe // devices // (rim // 2 * LANES), rim // 2, LANES)
    sent = [f32(*message), f32(rim, BW), f32(rim, BW)]
    rows_scratch = [pltpu.VMEM(message, jnp.float32), pltpu.SemaphoreType.DMA]
    size = 4 * BW * blocks
    square = bf16(LANES, LANES)

    donors = call(
        donors_kernel,
        [VMEM, VMEM, SMEM],
        sent + [bf16(blocks, fringe), square, square, state],
        4 * BW * blocks * fringe,
        2 * size,
        out_specs=[hbm] + [VMEM] * 6,
        scratch_shapes=rows_scratch,
    )
    chunks = blocks // LANES
    scratch = [
        pltpu.VMEM((BW, blocks + LANES), jnp.bfloat16),
        pltpu.VMEM((BW, blocks + LANES), jnp.bfloat16),
        [pltpu.VMEM((BW, slots * LANES), jnp.float32)] * chunks,
        pltpu.VMEM((chunks, slots, VARS, BW, LANES), jnp.bfloat16),
        pltpu.VMEM((BW, blocks), jnp.float32),
        pltpu.SemaphoreType.DMA((chunks,)),
        pltpu.SemaphoreType.DMA,
    ]
    local_more = dict(
        flops=4 * BW * 2 * LANES * slots * blocks,
        moved=coup.size * 2 + 4 * size,
        scratch_shapes=scratch,
    )
    first_local = call(
        functools.partial(first_local_kernel, rim),
        [VMEM, VMEM, hbm, hbm, VMEM, VMEM],
        [
            state,
            bf16(VARS, BW, LANES),
            f32(PACK, LANES),
            bf16(fringe + LANES, blocks),
            f32(1, fringe),
        ],
        **dict(local_more, scratch_shapes=scratch + [pltpu.VMEM((VARS * BW, LANES), jnp.float32)]),
    )
    local = call(functools.partial(local_kernel, rim), [VMEM, VMEM, hbm, hbm], state, **local_more)
    advance = call(
        advance_kernel,
        [VMEM] * 8 + [hbm] + [VMEM] * 4,
        [state, f32(1, LANES)] + sent,
        8 * BW * blocks * fringe,
        diag.size * 2 + 4 * size,
        out_specs=[VMEM, VMEM, hbm, VMEM, VMEM],
        scratch_shapes=[
            pltpu.VMEM((BW, blocks), jnp.float32),
            pltpu.VMEM((VARS, VARS, CELLS, blocks), jnp.bfloat16),
            pltpu.SemaphoreType.DMA((CELLS // PACK,)),
        ]
        + rows_scratch,
    )
    residual = call(
        residual_kernel,
        [VMEM] * 9,
        [state, f32(devices, 2, LANES)],
        4 * BW * blocks * fringe,
        3 * size,
    )
    direction = call(
        direction_kernel, [VMEM] * 2, [state, state], diag.size * 2, diag.size * 2 + 2 * size
    )
    finish = call(
        functools.partial(finish_kernel, float(blocks * devices * BW)),
        [VMEM] * 3,
        state,
        2 * BW * blocks,
        3 * size,
    )

    def exchange(rows, to_up, to_down):
        rows = lax.all_to_all(rows, ("body", "blk"), split_axis=0, concat_axis=0, tiled=True)
        return rows, lax.ppermute(to_up, "blk", up), lax.ppermute(to_down, "blk", down)

    *out, table, sel_up, sel_down, x_here = donors(x, here(fringe_src), here(seam_perm))
    arrived = exchange(*out)
    part, rimcoup, rimrow, across, weight = first_local(
        x_here, nbr, coup, source_t, here(fringe_dst), here(fringe_weight)
    )
    across = (across, weight, rimcoup, rimrow)
    parts = here(diag_inv.transpose(1, 2, 0).reshape(VARS, VARS, CELLS, blocks))
    x, norm, *out = advance(part, *arrived, *across, parts, x_here, table, sel_up, sel_down)
    arrived = exchange(*out)
    part = local(x, nbr, coup, source_t)
    resid, sums = residual(part, *arrived, *across, norm)
    sums = lax.all_to_all(sums, ("body", "blk"), split_axis=0, concat_axis=0, tiled=True)
    update, resid = direction(diag, resid)
    x = finish(sums, x, update)
    return (x.T, resid.T)


def solution(mesh):
    return jax.shard_map(
        shards,
        mesh=mesh,
        in_specs=(
            P(("body", "blk"), None),
            P(("body", "blk"), None),
            P(("body", "blk"), None, None, None),
            P(("body", "blk"), None, None),
            P(("body", "blk"), None),
            P("body", None),
            P(("body", "blk"), None),
            P(("body", "blk"), None),
            P(("body", "blk"), None),
        ),
        out_specs=(P(("body", "blk"), None), P(("body", "blk"), None)),
        check_vma=False,
    )
```

```python
import functools
import math

import jax
import jax.numpy as jnp
from jax import lax
from jax.experimental import pallas as pl
from jax.experimental.pallas import tpu as pltpu
from jax.sharding import PartitionSpec as P

CELLS = 64
VARS = 5
BW = 320
STEP_CFL = 0.5
LANES = 128
PACK = 16
VMEM_LIMIT = 32 * 1024 * 1024


def split(x):
    high = x.astype(jnp.bfloat16)
    return high, (x - high.astype(jnp.float32)).astype(jnp.bfloat16)


def onehot(mask):
    return jnp.where(mask, 1.0, 0.0).astype(jnp.bfloat16)


def pick(x, table):
    high, low = split(x)
    return jnp.dot(high, table, preferred_element_type=jnp.float32) + jnp.dot(
        low, table, preferred_element_type=jnp.float32
    )


def send_blocks(x, table, select, out_ref, up_ref, down_ref, rows_ref, sem):
    rim = up_ref.shape[0]
    half = rows_ref.shape[2]
    rows = pick(x, table).T.reshape(rows_ref.shape[0], 2 * half, BW)
    for h in range(2):
        for tile in range(2):
            rows_ref[:, 2 * tile + h] = rows[:, h * half : (h + 1) * half, tile * LANES : (tile + 1) * LANES]
    rest = rows[:, :, 2 * LANES :]
    rows_ref[:, 4] = jnp.concatenate([rest[:, :half], rest[:, half:]], axis=2)
    copy = pltpu.make_async_copy(rows_ref, out_ref, sem)
    copy.start()
    index = lax.axis_index("blk")
    at_last = index == lax.axis_size("blk") - 1
    at_first = index == 0
    first = lax.broadcasted_iota(jnp.int32, (BW, LANES), 1) < LANES // 2
    ends = split(jnp.where(first, x[:, :LANES], x[:, x.shape[1] - LANES :]))
    rims = jnp.dot(jnp.concatenate(ends, axis=1), select, preferred_element_type=jnp.float32)
    lane = lax.broadcasted_iota(jnp.int32, (1, LANES), 1)
    turn_up = (lane < rim) & at_last
    turn_down = (lane >= rim) & at_first
    angle = 2.0 * math.pi / 3.0
    cosine = jnp.where(turn_up | turn_down, math.cos(angle), 1.0)
    sine = jnp.where(turn_up, math.sin(angle), jnp.where(turn_down, -math.sin(angle), 0.0))
    first = rims[2 * CELLS : 3 * CELLS]
    second = rims[3 * CELLS : 4 * CELLS]
    rims = jnp.concatenate(
        [
            rims[: 2 * CELLS],
            cosine * first - sine * second,
            sine * first + cosine * second,
            rims[4 * CELLS :],
        ],
        axis=0,
    ).T
    up_ref[...] = rims[:rim]
    down_ref[...] = rims[rim : 2 * rim]
    return copy


def donors_kernel(
    x_ref, src_ref, perm_ref,
    out_ref, up_ref, down_ref, table_ref, select_ref, x_out, rows_ref, sem,
):
    rim = up_ref.shape[0]
    index = lax.axis_index("blk")
    at_last = index == lax.axis_size("blk") - 1
    at_first = index == 0
    sub = lax.broadcasted_iota(jnp.int32, (LANES, LANES), 0)
    lane = lax.broadcasted_iota(jnp.int32, (LANES, LANES), 1)
    wanted = lane[:1]
    target = sub[:, :1]
    for j in range(rim):
        partner = perm_ref[0, j]
        wanted = jnp.where((lane[:1] == j) & at_last, partner, wanted)
        target = jnp.where((sub[:, :1] == j) & at_first, partner, target)
    to_up = (sub == wanted + (LANES - rim)) & (lane < rim)
    to_down = (target + rim == lane) & (sub < rim)
    select = onehot(to_up | to_down)
    select = jnp.concatenate([select, select], axis=0)
    rows = lax.broadcasted_iota(jnp.int32, table_ref.shape, 0)
    table = onehot(rows == src_ref[...])
    copy = send_blocks(
        x_ref[...], table, select, out_ref, up_ref, down_ref, rows_ref, sem
    )
    table_ref[...] = table
    select_ref[...] = select
    x_out[...] = x_ref[...]
    copy.wait()


def take(x, lanes):
    return jnp.take_along_axis(x, lanes, axis=1, mode="promise_in_bounds")


def local_kernel(rim, x_ref, nbr_ref, coup_ref, source_ref, out_ref, coup, source, sems, source_sem):
    slots, blocks = nbr_ref.shape
    chunks = blocks // LANES
    spans = [slice(c * LANES, (c + 1) * LANES) for c in range(chunks)]
    copies = [
        pltpu.make_async_copy(coup_ref.at[:, :, :, spans[c]], coup.at[c], sems.at[c])
        for c in range(chunks)
    ]
    for copy in copies:
        copy.start()
    source_copy = pltpu.make_async_copy(source_ref, source, source_sem)
    source_copy.start()
    first = lax.broadcasted_iota(jnp.int32, (PACK, LANES), 1) < LANES // 2
    nothing = jnp.zeros((PACK, LANES), jnp.float32)
    for c in range(chunks):
        picks = []
        for m in range(slots):
            at = jnp.broadcast_to(nbr_ref[m : m + 1, spans[c]] - (rim + c * LANES), (PACK, LANES))
            picks.append((lax.bitwise_and(at, LANES - 1), (at >= 0) & (at < LANES)))
        copies[c].wait()
        if c == 0:
            source_copy.wait()
        for at in range(0, CELLS, PACK):
            total = [None] * VARS
            for v in range(VARS):
                span = slice(v * CELLS + at, v * CELLS + at + PACK)
                own = x_ref[span, spans[c]]
                after = x_ref[span, spans[c + 1]] if c + 1 < chunks else nothing
                before = x_ref[span, spans[c - 1]] if c > 0 else nothing
                beside = jnp.where(first, after, before)
                for m in range(slots):
                    lanes, inside = picks[m]
                    value = jnp.where(inside, take(own, lanes), take(beside, lanes))
                    for u in range(VARS):
                        term = coup[c, m, u, span, :].astype(jnp.float32) * value
                        total[u] = term if total[u] is None else total[u] + term
            for u in range(VARS):
                span = slice(u * CELLS + at, u * CELLS + at + PACK)
                out_ref[span, spans[c]] = source[span, spans[c]] - x_ref[span, spans[c]] + total[u]


def first_local_kernel(
    rim, x_ref, nbr_ref, coup_ref, source_ref, dst_ref, weight_ref,
    out_ref, rimcoup_ref, rimrow_ref, table_ref, weight_out, coup, source, sems, source_sem,
):
    slots, blocks = nbr_ref.shape
    chunks = blocks // LANES
    fringe = dst_ref.shape[1]
    local_kernel(rim, x_ref, nbr_ref, coup_ref, source_ref, out_ref, coup, source, sems, source_sem)
    lane = lax.broadcasted_iota(jnp.int32, (PACK, LANES), 1)
    first = lane < LANES // 2
    masks = [lax.rem(lane + rim + LANES - m * 2 * rim, LANES) < 2 * rim for m in range(slots)]

    def merged(ends, nothing):
        result = nothing
        for m in range(slots):
            both = jnp.where(first, *ends(m))
            if m > 0:
                both = pltpu.roll(both, m * 2 * rim, 1)
            result = jnp.where(masks[m], both, result)
        return result

    def rows(m):
        lower = jnp.broadcast_to(nbr_ref[m : m + 1, :LANES], (PACK, LANES))
        upper = jnp.broadcast_to(nbr_ref[m : m + 1, blocks - LANES :], (PACK, LANES))
        return jnp.where(lower < rim, lower, -LANES), jnp.where(upper >= blocks + rim, upper - blocks, -LANES)

    rimrow_ref[...] = merged(rows, jnp.full((PACK, LANES), -LANES, jnp.int32))
    for u in range(VARS):
        for at in range(0, BW, PACK):
            span = slice(at, at + PACK)
            rimcoup_ref[u, span, :] = merged(
                lambda m: (coup[0, m, u, span, :], coup[chunks - 1, m, u, span, :]),
                jnp.zeros((PACK, LANES), jnp.bfloat16),
            )
    weight_out[...] = weight_ref[...]
    targets = jnp.broadcast_to(dst_ref[...], (LANES, fringe)).T
    for c in range(chunks):
        table_ref[:, c * LANES : (c + 1) * LANES] = onehot(targets == lane[:1] + c * LANES)


def full_residual(local_ref, inc_ref, lower_ref, upper_ref, table_ref, weight_ref, rimcoup_ref, rimrow_ref):
    rim = lower_ref.shape[0]
    blocks = local_ref.shape[1]
    rims = jnp.concatenate(
        [lower_ref[...], upper_ref[...], jnp.zeros((LANES - 2 * rim, BW), jnp.float32)], axis=0
    ).T
    high, low = split(rims)
    low = pltpu.roll(low.astype(jnp.float32), 2 * rim, 1)
    rims = (high.astype(jnp.float32) + low).astype(jnp.bfloat16)
    sub = lax.broadcasted_iota(jnp.int32, (LANES, LANES), 0)
    row = rimrow_ref[:1]
    reads = onehot((sub == row) | (sub == row + 2 * rim))
    near = jnp.dot(rims, reads, preferred_element_type=jnp.float32)
    edge = []
    for u in range(VARS):
        total = None
        for v in range(VARS):
            span = slice(v * CELLS, (v + 1) * CELLS)
            term = rimcoup_ref[u, span, :].astype(jnp.float32) * near[span]
            total = term if total is None else total + term
        edge.append(total)
    edge = jnp.concatenate(edge, axis=0)
    shift = LANES // 2
    while shift >= 2 * rim:
        edge = edge + pltpu.roll(edge, shift, 1)
        shift //= 2
    lane = lax.broadcasted_iota(jnp.int32, (BW, LANES), 1)
    rest = inc_ref[:, 4]
    rest = jnp.concatenate([rest[:, :, :CELLS], rest[:, :, CELLS:]], axis=1).reshape(-1, CELLS)
    fringe = [inc_ref[:, 0:2].reshape(-1, LANES).T, inc_ref[:, 2:4].reshape(-1, LANES).T, rest.T]
    total = local_ref[...] + pick(jnp.concatenate(fringe, axis=0) * weight_ref[...], table_ref[...])
    lower = total[:, :LANES] + jnp.where(lane < rim, edge, 0.0)
    upper = total[:, blocks - LANES :] + jnp.where(lane >= LANES - rim, edge, 0.0)
    return jnp.concatenate([lower, total[:, LANES : blocks - LANES], upper], axis=1)


def precondition(diag_ref, resid_ref, u, at):
    total = None
    for v in range(VARS):
        span = pl.ds(v * CELLS + at, PACK)
        term = diag_ref[u, span, :].astype(jnp.float32) * resid_ref[span, :]
        total = term if total is None else total + term
    return total


def lane_sums(resid):
    square = jnp.sum(resid * resid, axis=0, keepdims=True)
    return sum(square[:, i : i + LANES] for i in range(0, square.shape[1], LANES))


def advance_kernel(
    local_ref, inc_ref, lower_ref, upper_ref, across_ref, weight_ref, rimcoup_ref, rimrow_ref,
    diag_ref, x_ref, table_ref, select_ref,
    next_ref, norm_ref, out_ref, up_ref, down_ref, resid, diag, diag_sems, rows_ref, sem,
):
    parts = CELLS // PACK
    fetches = []
    for part in range(parts):
        span = pl.ds(part * PACK, PACK)
        fetches.append(
            pltpu.make_async_copy(
                diag_ref.at[:, :, span], diag.at[:, :, span], diag_sems.at[part]
            )
        )
        fetches[part].start()
    resid[...] = full_residual(
        local_ref, inc_ref, lower_ref, upper_ref, across_ref, weight_ref, rimcoup_ref, rimrow_ref
    )
    for part in range(parts):
        fetches[part].wait()
        at = part * PACK
        for u in range(VARS):
            total = None
            for v in range(VARS):
                term = diag[u, v, at : at + PACK].astype(jnp.float32)
                term = term * resid[v * CELLS + at : v * CELLS + at + PACK]
                total = term if total is None else total + term
            span = slice(u * CELLS + at, u * CELLS + at + PACK)
            next_ref[span, :] = x_ref[span, :] + STEP_CFL * total
    copy = send_blocks(
        next_ref[...], table_ref[...], select_ref[...], out_ref, up_ref, down_ref, rows_ref, sem
    )
    norm_ref[...] = lane_sums(resid[...])
    copy.wait()


def residual_kernel(
    local_ref, inc_ref, lower_ref, upper_ref, across_ref, weight_ref, rimcoup_ref, rimrow_ref, norm_ref,
    resid_ref, sums_ref,
):
    resid = full_residual(
        local_ref, inc_ref, lower_ref, upper_ref, across_ref, weight_ref, rimcoup_ref, rimrow_ref
    )
    resid_ref[...] = resid
    both = jnp.concatenate([norm_ref[...], lane_sums(resid)], axis=0)
    sums_ref[...] = jnp.broadcast_to(both[None], sums_ref.shape)


def direction_kernel(diag_ref, resid_ref, out_ref, resid_out):
    resid_out[...] = resid_ref[...]

    def cells(part, carry):
        at = pl.multiple_of(part * PACK, PACK)
        for u in range(VARS):
            out_ref[pl.ds(u * CELLS + at, PACK), :] = precondition(diag_ref, resid_ref, u, at)
        return carry

    lax.fori_loop(0, CELLS // PACK, cells, 0)


def finish_kernel(entries, sums_ref, x_ref, update_ref, out_ref):
    sums = jnp.sum(jnp.sum(sums_ref[...], axis=0), axis=1, keepdims=True) / entries + 1e-06
    cfl = STEP_CFL * jnp.sqrt(sums[0:1] / sums[1:2])
    out_ref[...] = x_ref[...] + cfl * update_ref[...]


VMEM = pl.BlockSpec(memory_space=pltpu.VMEM)
SMEM = pl.BlockSpec(memory_space=pltpu.SMEM)


def f32(*shape):
    return jax.ShapeDtypeStruct(shape, jnp.float32)


def bf16(*shape):
    return jax.ShapeDtypeStruct(shape, jnp.bfloat16)


def call(kernel, in_specs, out_shape, flops, moved, **more):
    many = isinstance(out_shape, (list, tuple))
    return pl.pallas_call(
        kernel,
        in_specs=in_specs,
        out_specs=more.pop("out_specs", [VMEM] * len(out_shape) if many else VMEM),
        out_shape=out_shape,
        compiler_params=pltpu.CompilerParams(vmem_limit_bytes=VMEM_LIMIT),
        cost_estimate=pl.CostEstimate(flops=flops, bytes_accessed=moved, transcendentals=0),
        **more,
    )


def shards(
    psi_init, source, coupling, diag_inv, neighbours, seam_perm, fringe_src, fringe_dst, fringe_weight
):
    blocks = psi_init.shape[0]
    slots = neighbours.shape[1]
    rim = seam_perm.shape[1]
    fringe = fringe_src.shape[1]
    peers = lax.axis_size("blk")
    devices = lax.axis_size("body") * peers
    up = [(i, (i + 1) % peers) for i in range(peers)]
    down = [(j, i) for i, j in up]
    here = functools.partial(pltpu.with_memory_space_constraint, memory_space=pltpu.HBM)
    x = here(psi_init.T)
    source_t = here(source.T)
    coup = here(coupling.transpose(1, 2, 3, 0))
    diag = here(diag_inv.transpose(1, 2, 0))
    nbr = here(neighbours.T)
    state = f32(BW, blocks)
    hbm = pl.BlockSpec(memory_space=pltpu.HBM)
    message = (devices, BW * fringe // devices // (rim // 2 * LANES), rim // 2, LANES)
    sent = [f32(*message), f32(rim, BW), f32(rim, BW)]
    rows_scratch = [pltpu.VMEM(message, jnp.float32), pltpu.SemaphoreType.DMA]
    size = 4 * BW * blocks

    donors = call(
        donors_kernel,
        [VMEM, VMEM, SMEM],
        sent + [bf16(blocks, fringe), bf16(2 * LANES, LANES), state],
        4 * BW * blocks * fringe,
        2 * size,
        out_specs=[hbm] + [VMEM] * 5,
        scratch_shapes=rows_scratch,
    )
    chunks = blocks // LANES
    scratch = [
        pltpu.VMEM((chunks, slots, VARS, BW, LANES), jnp.bfloat16),
        pltpu.VMEM((BW, blocks), jnp.float32),
        pltpu.SemaphoreType.DMA((chunks,)),
        pltpu.SemaphoreType.DMA,
    ]
    local_more = dict(
        flops=4 * BW * 2 * LANES * slots * blocks,
        moved=coup.size * 2 + 4 * size,
        scratch_shapes=scratch,
    )
    first_local = call(
        functools.partial(first_local_kernel, rim),
        [VMEM, VMEM, hbm, hbm, VMEM, VMEM],
        [
            state,
            bf16(VARS, BW, LANES),
            jax.ShapeDtypeStruct((PACK, LANES), jnp.int32),
            bf16(fringe, blocks),
            f32(1, fringe),
        ],
        **local_more,
    )
    local = call(functools.partial(local_kernel, rim), [VMEM, VMEM, hbm, hbm], state, **local_more)
    advance = call(
        advance_kernel,
        [VMEM] * 8 + [hbm] + [VMEM] * 3,
        [state, f32(1, LANES)] + sent,
        8 * BW * blocks * fringe,
        diag.size * 2 + 4 * size,
        out_specs=[VMEM, VMEM, hbm, VMEM, VMEM],
        scratch_shapes=[
            pltpu.VMEM((BW, blocks), jnp.float32),
            pltpu.VMEM((VARS, VARS, CELLS, blocks), jnp.bfloat16),
            pltpu.SemaphoreType.DMA((CELLS // PACK,)),
        ]
        + rows_scratch,
    )
    residual = call(
        residual_kernel,
        [VMEM] * 9,
        [state, f32(devices, 2, LANES)],
        4 * BW * blocks * fringe,
        3 * size,
    )
    direction = call(
        direction_kernel, [VMEM] * 2, [state, state], diag.size * 2, diag.size * 2 + 2 * size
    )
    finish = call(
        functools.partial(finish_kernel, float(blocks * devices * BW)),
        [VMEM] * 3,
        state,
        2 * BW * blocks,
        3 * size,
    )

    def exchange(rows, to_up, to_down):
        rows = lax.all_to_all(rows, ("body", "blk"), split_axis=0, concat_axis=0, tiled=True)
        return rows, lax.ppermute(to_up, "blk", up), lax.ppermute(to_down, "blk", down)

    *out, table, select, x_here = donors(x, here(fringe_src), here(seam_perm))
    arrived = exchange(*out)
    part, rimcoup, rimrow, across, weight = first_local(
        x_here, nbr, coup, source_t, here(fringe_dst), here(fringe_weight)
    )
    across = (across, weight, rimcoup, rimrow)
    parts = here(diag_inv.transpose(1, 2, 0).reshape(VARS, VARS, CELLS, blocks))
    x, norm, *out = advance(part, *arrived, *across, parts, x_here, table, select)
    arrived = exchange(*out)
    part = local(x, nbr, coup, source_t)
    resid, sums = residual(part, *arrived, *across, norm)
    sums = lax.all_to_all(sums, ("body", "blk"), split_axis=0, concat_axis=0, tiled=True)
    update, resid = direction(diag, resid)
    x = finish(sums, x, update)
    return (x.T, resid.T)


def solution(mesh):
    return jax.shard_map(
        shards,
        mesh=mesh,
        in_specs=(
            P(("body", "blk"), None),
            P(("body", "blk"), None),
            P(("body", "blk"), None, None, None),
            P(("body", "blk"), None, None),
            P(("body", "blk"), None),
            P("body", None),
            P(("body", "blk"), None),
            P(("body", "blk"), None),
            P(("body", "blk"), None),
        ),
        out_specs=(P(("body", "blk"), None), P(("body", "blk"), None)),
        check_vma=False,
    )
```

```python
import functools
import math

import jax
import jax.numpy as jnp
from jax import lax
from jax.experimental import pallas as pl
from jax.experimental.pallas import tpu as pltpu
from jax.sharding import PartitionSpec as P

CELLS = 64
VARS = 5
BW = 320
STEP_CFL = 0.5
LANES = 128
PACK = 16
VMEM_LIMIT = 32 * 1024 * 1024


def split(x):
    high = x.astype(jnp.bfloat16)
    return high, (x - high.astype(jnp.float32)).astype(jnp.bfloat16)


def onehot(mask):
    return jnp.where(mask, 1.0, 0.0).astype(jnp.bfloat16)


def pick(x, table):
    high, low = split(x)
    return jnp.dot(high, table, preferred_element_type=jnp.float32) + jnp.dot(
        low, table, preferred_element_type=jnp.float32
    )


def send_blocks(x, table, select, out_ref, up_ref, down_ref, rows_ref, sem):
    rim = up_ref.shape[0]
    half = rows_ref.shape[2]
    rows = pick(x, table).T.reshape(rows_ref.shape[0], 2 * half, BW)
    for h in range(2):
        for tile in range(2):
            rows_ref[:, 2 * tile + h] = rows[:, h * half : (h + 1) * half, tile * LANES : (tile + 1) * LANES]
    rest = rows[:, :, 2 * LANES :]
    rows_ref[:, 4] = jnp.concatenate([rest[:, :half], rest[:, half:]], axis=2)
    copy = pltpu.make_async_copy(rows_ref, out_ref, sem)
    copy.start()
    index = lax.axis_index("blk")
    at_last = index == lax.axis_size("blk") - 1
    at_first = index == 0
    first = lax.broadcasted_iota(jnp.int32, (BW, LANES), 1) < LANES // 2
    ends = split(jnp.where(first, x[:, :LANES], x[:, x.shape[1] - LANES :]))
    rims = jnp.dot(jnp.concatenate(ends, axis=1), select, preferred_element_type=jnp.float32)
    lane = lax.broadcasted_iota(jnp.int32, (1, LANES), 1)
    turn_up = (lane < rim) & at_last
    turn_down = (lane >= rim) & at_first
    angle = 2.0 * math.pi / 3.0
    cosine = jnp.where(turn_up | turn_down, math.cos(angle), 1.0)
    sine = jnp.where(turn_up, math.sin(angle), jnp.where(turn_down, -math.sin(angle), 0.0))
    first = rims[2 * CELLS : 3 * CELLS]
    second = rims[3 * CELLS : 4 * CELLS]
    rims = jnp.concatenate(
        [
            rims[: 2 * CELLS],
            cosine * first - sine * second,
            sine * first + cosine * second,
            rims[4 * CELLS :],
        ],
        axis=0,
    ).T
    up_ref[...] = rims[:rim]
    down_ref[...] = rims[rim : 2 * rim]
    return copy


def donors_kernel(
    x_ref, src_ref, perm_ref,
    out_ref, up_ref, down_ref, table_ref, select_ref, x_out, rows_ref, sem,
):
    rim = up_ref.shape[0]
    index = lax.axis_index("blk")
    at_last = index == lax.axis_size("blk") - 1
    at_first = index == 0
    sub = lax.broadcasted_iota(jnp.int32, (LANES, LANES), 0)
    lane = lax.broadcasted_iota(jnp.int32, (LANES, LANES), 1)
    wanted = lane[:1]
    target = sub[:, :1]
    for j in range(rim):
        partner = perm_ref[0, j]
        wanted = jnp.where((lane[:1] == j) & at_last, partner, wanted)
        target = jnp.where((sub[:, :1] == j) & at_first, partner, target)
    to_up = (sub == wanted + (LANES - rim)) & (lane < rim)
    to_down = (target + rim == lane) & (sub < rim)
    select = onehot(to_up | to_down)
    select = jnp.concatenate([select, select], axis=0)
    rows = lax.broadcasted_iota(jnp.int32, table_ref.shape, 0)
    table = onehot(rows == src_ref[...])
    copy = send_blocks(
        x_ref[...], table, select, out_ref, up_ref, down_ref, rows_ref, sem
    )
    table_ref[...] = table
    select_ref[...] = select
    x_out[...] = x_ref[...]
    copy.wait()


def local_kernel(
    rim, x_ref, nbr_ref, coup_ref, source_ref, out_ref, high, low, near, coup, source, sems, source_sem
):
    slots, blocks = nbr_ref.shape
    chunks = blocks // LANES
    spans = [slice(c * LANES, (c + 1) * LANES) for c in range(chunks)]
    copies = [
        pltpu.make_async_copy(coup_ref.at[:, :, :, spans[c]], coup.at[c], sems.at[c])
        for c in range(chunks)
    ]
    for copy in copies:
        copy.start()
    source_copy = pltpu.make_async_copy(source_ref, source, source_sem)
    source_copy.start()
    lane = lax.broadcasted_iota(jnp.int32, (BW, LANES), 1)
    moved = pltpu.roll(x_ref[...], rim, 1)
    head = jnp.where(lane < rim, 0.0, moved[:, :LANES])
    tail = jnp.where(lane < rim, moved[:, :LANES], 0.0)
    high[...], low[...] = split(jnp.concatenate([head, moved[:, LANES:], tail], axis=1))
    rows = lax.broadcasted_iota(jnp.int32, (2 * LANES, LANES), 0)

    pairs = range(0, slots, 2)

    def gather(c, m):
        window = slice(c * LANES, (c + 2) * LANES)
        table = jnp.concatenate(
            [onehot(rows == nbr_ref[i : i + 1, spans[c]] - c * LANES) for i in (m, m + 1)], axis=1
        )
        near[c][:, m * LANES : (m + 2) * LANES] = jnp.dot(
            high[:, window], table, preferred_element_type=jnp.float32
        ) + jnp.dot(low[:, window], table, preferred_element_type=jnp.float32)

    for m in pairs:
        gather(0, m)
    for c in range(chunks):
        copies[c].wait()
        if c == 0:
            source_copy.wait()
        ahead = list(pairs) if c + 1 < chunks else []
        for at in range(0, CELLS, PACK):
            if ahead:
                gather(c + 1, ahead.pop(0))
            total = [None] * VARS
            for m in range(slots):
                for v in range(VARS):
                    span = slice(v * CELLS + at, v * CELLS + at + PACK)
                    value = near[c][span, m * LANES : (m + 1) * LANES]
                    for u in range(VARS):
                        term = coup[c, m, u, span, :].astype(jnp.float32) * value
                        total[u] = term if total[u] is None else total[u] + term
            for u in range(VARS):
                span = slice(u * CELLS + at, u * CELLS + at + PACK)
                out_ref[span, spans[c]] = source[span, spans[c]] - x_ref[span, spans[c]] + total[u]


def first_local_kernel(
    rim, x_ref, nbr_ref, coup_ref, source_ref, dst_ref, weight_ref,
    out_ref, rimcoup_ref, rimrow_ref, table_ref, weight_out,
    high, low, near, coup, source, sems, source_sem,
):
    slots, blocks = nbr_ref.shape
    chunks = blocks // LANES
    fringe = dst_ref.shape[1]
    local_kernel(
        rim, x_ref, nbr_ref, coup_ref, source_ref, out_ref, high, low, near, coup, source, sems, source_sem
    )
    lane = lax.broadcasted_iota(jnp.int32, (PACK, LANES), 1)
    first = lane < LANES // 2
    masks = [lax.rem(lane + rim + LANES - m * 2 * rim, LANES) < 2 * rim for m in range(slots)]

    def merged(ends, nothing):
        result = nothing
        for m in range(slots):
            both = jnp.where(first, *ends(m))
            if m > 0:
                both = pltpu.roll(both, m * 2 * rim, 1)
            result = jnp.where(masks[m], both, result)
        return result

    def rows(m):
        lower = jnp.broadcast_to(nbr_ref[m : m + 1, :LANES], (PACK, LANES))
        upper = jnp.broadcast_to(nbr_ref[m : m + 1, blocks - LANES :], (PACK, LANES))
        return jnp.where(lower < rim, lower, -LANES), jnp.where(upper >= blocks + rim, upper - blocks, -LANES)

    rimrow_ref[...] = merged(rows, jnp.full((PACK, LANES), -LANES, jnp.int32))
    for u in range(VARS):
        for at in range(0, BW, PACK):
            span = slice(at, at + PACK)
            rimcoup_ref[u, span, :] = merged(
                lambda m: (coup[0, m, u, span, :], coup[chunks - 1, m, u, span, :]),
                jnp.zeros((PACK, LANES), jnp.bfloat16),
            )
    weight_out[...] = weight_ref[...]
    targets = jnp.broadcast_to(dst_ref[...], (LANES, fringe)).T
    for c in range(chunks):
        table_ref[:, c * LANES : (c + 1) * LANES] = onehot(targets == lane[:1] + c * LANES)


def full_residual(local_ref, inc_ref, lower_ref, upper_ref, table_ref, weight_ref, rimcoup_ref, rimrow_ref):
    rim = lower_ref.shape[0]
    blocks = local_ref.shape[1]
    rims = jnp.concatenate(
        [lower_ref[...], upper_ref[...], jnp.zeros((LANES - 2 * rim, BW), jnp.float32)], axis=0
    ).T
    high, low = split(rims)
    low = pltpu.roll(low.astype(jnp.float32), 2 * rim, 1)
    rims = (high.astype(jnp.float32) + low).astype(jnp.bfloat16)
    sub = lax.broadcasted_iota(jnp.int32, (LANES, LANES), 0)
    row = rimrow_ref[:1]
    reads = onehot((sub == row) | (sub == row + 2 * rim))
    near = jnp.dot(rims, reads, preferred_element_type=jnp.float32)
    edge = []
    for u in range(VARS):
        total = None
        for v in range(VARS):
            span = slice(v * CELLS, (v + 1) * CELLS)
            term = rimcoup_ref[u, span, :].astype(jnp.float32) * near[span]
            total = term if total is None else total + term
        edge.append(total)
    edge = jnp.concatenate(edge, axis=0)
    shift = LANES // 2
    while shift >= 2 * rim:
        edge = edge + pltpu.roll(edge, shift, 1)
        shift //= 2
    lane = lax.broadcasted_iota(jnp.int32, (BW, LANES), 1)
    rest = inc_ref[:, 4]
    rest = jnp.concatenate([rest[:, :, :CELLS], rest[:, :, CELLS:]], axis=1).reshape(-1, CELLS)
    fringe = [inc_ref[:, 0:2].reshape(-1, LANES).T, inc_ref[:, 2:4].reshape(-1, LANES).T, rest.T]
    total = local_ref[...] + pick(jnp.concatenate(fringe, axis=0) * weight_ref[...], table_ref[...])
    lower = total[:, :LANES] + jnp.where(lane < rim, edge, 0.0)
    upper = total[:, blocks - LANES :] + jnp.where(lane >= LANES - rim, edge, 0.0)
    return jnp.concatenate([lower, total[:, LANES : blocks - LANES], upper], axis=1)


def precondition(diag_ref, resid_ref, u, at):
    total = None
    for v in range(VARS):
        span = pl.ds(v * CELLS + at, PACK)
        term = diag_ref[u, span, :].astype(jnp.float32) * resid_ref[span, :]
        total = term if total is None else total + term
    return total


def lane_sums(resid):
    square = jnp.sum(resid * resid, axis=0, keepdims=True)
    return sum(square[:, i : i + LANES] for i in range(0, square.shape[1], LANES))


def advance_kernel(
    local_ref, inc_ref, lower_ref, upper_ref, across_ref, weight_ref, rimcoup_ref, rimrow_ref,
    diag_ref, x_ref, table_ref, select_ref,
    next_ref, norm_ref, out_ref, up_ref, down_ref, resid, diag, diag_sems, rows_ref, sem,
):
    parts = CELLS // PACK
    fetches = []
    for part in range(parts):
        span = pl.ds(part * PACK, PACK)
        fetches.append(
            pltpu.make_async_copy(
                diag_ref.at[:, :, span], diag.at[:, :, span], diag_sems.at[part]
            )
        )
        fetches[part].start()
    resid[...] = full_residual(
        local_ref, inc_ref, lower_ref, upper_ref, across_ref, weight_ref, rimcoup_ref, rimrow_ref
    )
    for part in range(parts):
        fetches[part].wait()
        at = part * PACK
        for u in range(VARS):
            total = None
            for v in range(VARS):
                term = diag[u, v, at : at + PACK].astype(jnp.float32)
                term = term * resid[v * CELLS + at : v * CELLS + at + PACK]
                total = term if total is None else total + term
            span = slice(u * CELLS + at, u * CELLS + at + PACK)
            next_ref[span, :] = x_ref[span, :] + STEP_CFL * total
    copy = send_blocks(
        next_ref[...], table_ref[...], select_ref[...], out_ref, up_ref, down_ref, rows_ref, sem
    )
    norm_ref[...] = lane_sums(resid[...])
    copy.wait()


def residual_kernel(
    local_ref, inc_ref, lower_ref, upper_ref, across_ref, weight_ref, rimcoup_ref, rimrow_ref, norm_ref,
    resid_ref, sums_ref,
):
    resid = full_residual(
        local_ref, inc_ref, lower_ref, upper_ref, across_ref, weight_ref, rimcoup_ref, rimrow_ref
    )
    resid_ref[...] = resid
    both = jnp.concatenate([norm_ref[...], lane_sums(resid)], axis=0)
    sums_ref[...] = jnp.broadcast_to(both[None], sums_ref.shape)


def direction_kernel(diag_ref, resid_ref, out_ref, resid_out):
    resid_out[...] = resid_ref[...]

    def cells(part, carry):
        at = pl.multiple_of(part * PACK, PACK)
        for u in range(VARS):
            out_ref[pl.ds(u * CELLS + at, PACK), :] = precondition(diag_ref, resid_ref, u, at)
        return carry

    lax.fori_loop(0, CELLS // PACK, cells, 0)


def finish_kernel(entries, sums_ref, x_ref, update_ref, out_ref):
    sums = jnp.sum(jnp.sum(sums_ref[...], axis=0), axis=1, keepdims=True) / entries + 1e-06
    cfl = STEP_CFL * jnp.sqrt(sums[0:1] / sums[1:2])
    out_ref[...] = x_ref[...] + cfl * update_ref[...]


VMEM = pl.BlockSpec(memory_space=pltpu.VMEM)
SMEM = pl.BlockSpec(memory_space=pltpu.SMEM)


def f32(*shape):
    return jax.ShapeDtypeStruct(shape, jnp.float32)


def bf16(*shape):
    return jax.ShapeDtypeStruct(shape, jnp.bfloat16)


def call(kernel, in_specs, out_shape, flops, moved, **more):
    many = isinstance(out_shape, (list, tuple))
    return pl.pallas_call(
        kernel,
        in_specs=in_specs,
        out_specs=more.pop("out_specs", [VMEM] * len(out_shape) if many else VMEM),
        out_shape=out_shape,
        compiler_params=pltpu.CompilerParams(vmem_limit_bytes=VMEM_LIMIT),
        cost_estimate=pl.CostEstimate(flops=flops, bytes_accessed=moved, transcendentals=0),
        **more,
    )


def shards(
    psi_init, source, coupling, diag_inv, neighbours, seam_perm, fringe_src, fringe_dst, fringe_weight
):
    blocks = psi_init.shape[0]
    slots = neighbours.shape[1]
    rim = seam_perm.shape[1]
    fringe = fringe_src.shape[1]
    peers = lax.axis_size("blk")
    devices = lax.axis_size("body") * peers
    up = [(i, (i + 1) % peers) for i in range(peers)]
    down = [(j, i) for i, j in up]
    here = functools.partial(pltpu.with_memory_space_constraint, memory_space=pltpu.HBM)
    x = here(psi_init.T)
    source_t = here(source.T)
    coup = here(coupling.transpose(1, 2, 3, 0))
    diag = here(diag_inv.transpose(1, 2, 0))
    nbr = here(neighbours.T)
    state = f32(BW, blocks)
    hbm = pl.BlockSpec(memory_space=pltpu.HBM)
    message = (devices, BW * fringe // devices // (rim // 2 * LANES), rim // 2, LANES)
    sent = [f32(*message), f32(rim, BW), f32(rim, BW)]
    rows_scratch = [pltpu.VMEM(message, jnp.float32), pltpu.SemaphoreType.DMA]
    size = 4 * BW * blocks

    donors = call(
        donors_kernel,
        [VMEM, VMEM, SMEM],
        sent + [bf16(blocks, fringe), bf16(2 * LANES, LANES), state],
        4 * BW * blocks * fringe,
        2 * size,
        out_specs=[hbm] + [VMEM] * 5,
        scratch_shapes=rows_scratch,
    )
    chunks = blocks // LANES
    scratch = [
        pltpu.VMEM((BW, blocks + LANES), jnp.bfloat16),
        pltpu.VMEM((BW, blocks + LANES), jnp.bfloat16),
        [pltpu.VMEM((BW, slots * LANES), jnp.float32)] * chunks,
        pltpu.VMEM((chunks, slots, VARS, BW, LANES), jnp.bfloat16),
        pltpu.VMEM((BW, blocks), jnp.float32),
        pltpu.SemaphoreType.DMA((chunks,)),
        pltpu.SemaphoreType.DMA,
    ]
    local_more = dict(
        flops=4 * BW * 2 * LANES * slots * blocks,
        moved=coup.size * 2 + 4 * size,
        scratch_shapes=scratch,
    )
    first_local = call(
        functools.partial(first_local_kernel, rim),
        [VMEM, VMEM, hbm, hbm, VMEM, VMEM],
        [
            state,
            bf16(VARS, BW, LANES),
            jax.ShapeDtypeStruct((PACK, LANES), jnp.int32),
            bf16(fringe, blocks),
            f32(1, fringe),
        ],
        **local_more,
    )
    local = call(functools.partial(local_kernel, rim), [VMEM, VMEM, hbm, hbm], state, **local_more)
    advance = call(
        advance_kernel,
        [VMEM] * 8 + [hbm] + [VMEM] * 3,
        [state, f32(1, LANES)] + sent,
        8 * BW * blocks * fringe,
        diag.size * 2 + 4 * size,
        out_specs=[VMEM, VMEM, hbm, VMEM, VMEM],
        scratch_shapes=[
            pltpu.VMEM((BW, blocks), jnp.float32),
            pltpu.VMEM((VARS, VARS, CELLS, blocks), jnp.bfloat16),
            pltpu.SemaphoreType.DMA((CELLS // PACK,)),
        ]
        + rows_scratch,
    )
    residual = call(
        residual_kernel,
        [VMEM] * 9,
        [state, f32(devices, 2, LANES)],
        4 * BW * blocks * fringe,
        3 * size,
    )
    direction = call(
        direction_kernel, [VMEM] * 2, [state, state], diag.size * 2, diag.size * 2 + 2 * size
    )
    finish = call(
        functools.partial(finish_kernel, float(blocks * devices * BW)),
        [VMEM] * 3,
        state,
        2 * BW * blocks,
        3 * size,
    )

    def exchange(rows, to_up, to_down):
        rows = lax.all_to_all(rows, ("body", "blk"), split_axis=0, concat_axis=0, tiled=True)
        return rows, lax.ppermute(to_up, "blk", up), lax.ppermute(to_down, "blk", down)

    *out, table, select, x_here = donors(x, here(fringe_src), here(seam_perm))
    arrived = exchange(*out)
    part, rimcoup, rimrow, across, weight = first_local(
        x_here, nbr, coup, source_t, here(fringe_dst), here(fringe_weight)
    )
    across = (across, weight, rimcoup, rimrow)
    parts = here(diag_inv.transpose(1, 2, 0).reshape(VARS, VARS, CELLS, blocks))
    x, norm, *out = advance(part, *arrived, *across, parts, x_here, table, select)
    arrived = exchange(*out)
    part = local(x, nbr, coup, source_t)
    resid, sums = residual(part, *arrived, *across, norm)
    sums = lax.all_to_all(sums, ("body", "blk"), split_axis=0, concat_axis=0, tiled=True)
    update, resid = direction(diag, resid)
    x = finish(sums, x, update)
    return (x.T, resid.T)


def solution(mesh):
    return jax.shard_map(
        shards,
        mesh=mesh,
        in_specs=(
            P(("body", "blk"), None),
            P(("body", "blk"), None),
            P(("body", "blk"), None, None, None),
            P(("body", "blk"), None, None),
            P(("body", "blk"), None),
            P("body", None),
            P(("body", "blk"), None),
            P(("body", "blk"), None),
            P(("body", "blk"), None),
        ),
        out_specs=(P(("body", "blk"), None), P(("body", "blk"), None)),
        check_vma=False,
    )
```

```python
import functools
import math

import jax
import jax.numpy as jnp
from jax import lax
from jax.experimental import pallas as pl
from jax.experimental.pallas import tpu as pltpu
from jax.sharding import PartitionSpec as P

CELLS = 64
VARS = 5
BW = 320
STEP_CFL = 0.5
LANES = 128
PACK = 16
VMEM_LIMIT = 32 * 1024 * 1024


def split(x):
    high = x.astype(jnp.bfloat16)
    return high, (x - high.astype(jnp.float32)).astype(jnp.bfloat16)


def onehot(mask):
    return jnp.where(mask, 1.0, 0.0).astype(jnp.bfloat16)


def pick(x, table):
    both = jnp.dot(jnp.concatenate(split(x), axis=0), table, preferred_element_type=jnp.float32)
    return both[: x.shape[0]] + both[x.shape[0] :]


def send_blocks(x, table, select, out_ref, up_ref, down_ref, rows_ref, sem):
    rim = up_ref.shape[0]
    half = rows_ref.shape[2]
    rows = pick(x, table).T.reshape(rows_ref.shape[0], 2 * half, BW)
    for h in range(2):
        for tile in range(2):
            rows_ref[:, 2 * tile + h] = rows[:, h * half : (h + 1) * half, tile * LANES : (tile + 1) * LANES]
    rest = rows[:, :, 2 * LANES :]
    rows_ref[:, 4] = jnp.concatenate([rest[:, :half], rest[:, half:]], axis=2)
    copy = pltpu.make_async_copy(rows_ref, out_ref, sem)
    copy.start()
    index = lax.axis_index("blk")
    at_last = index == lax.axis_size("blk") - 1
    at_first = index == 0
    first = lax.broadcasted_iota(jnp.int32, (BW, LANES), 1) < LANES // 2
    ends = split(jnp.where(first, x[:, :LANES], x[:, x.shape[1] - LANES :]))
    rims = jnp.dot(jnp.concatenate(ends, axis=1), select, preferred_element_type=jnp.float32)
    lane = lax.broadcasted_iota(jnp.int32, (1, LANES), 1)
    turn_up = (lane < rim) & at_last
    turn_down = (lane >= rim) & at_first
    angle = 2.0 * math.pi / 3.0
    cosine = jnp.where(turn_up | turn_down, math.cos(angle), 1.0)
    sine = jnp.where(turn_up, math.sin(angle), jnp.where(turn_down, -math.sin(angle), 0.0))
    first = rims[2 * CELLS : 3 * CELLS]
    second = rims[3 * CELLS : 4 * CELLS]
    rims = jnp.concatenate(
        [
            rims[: 2 * CELLS],
            cosine * first - sine * second,
            sine * first + cosine * second,
            rims[4 * CELLS :],
        ],
        axis=0,
    ).T
    up_ref[...] = rims[:rim]
    down_ref[...] = rims[rim : 2 * rim]
    return copy


def donors_kernel(
    x_ref, src_ref, perm_ref,
    out_ref, up_ref, down_ref, table_ref, select_ref, x_out, rows_ref, sem,
):
    rim = up_ref.shape[0]
    index = lax.axis_index("blk")
    at_last = index == lax.axis_size("blk") - 1
    at_first = index == 0
    sub = lax.broadcasted_iota(jnp.int32, (LANES, LANES), 0)
    lane = lax.broadcasted_iota(jnp.int32, (LANES, LANES), 1)
    wanted = lane[:1]
    target = sub[:, :1]
    for j in range(rim):
        partner = perm_ref[0, j]
        wanted = jnp.where((lane[:1] == j) & at_last, partner, wanted)
        target = jnp.where((sub[:, :1] == j) & at_first, partner, target)
    to_up = (sub == wanted + (LANES - rim)) & (lane < rim)
    to_down = (target + rim == lane) & (sub < rim)
    select = onehot(to_up | to_down)
    select = jnp.concatenate([select, select], axis=0)
    rows = lax.broadcasted_iota(jnp.int32, table_ref.shape, 0)
    table = onehot(rows == src_ref[...])
    copy = send_blocks(
        x_ref[...], table, select, out_ref, up_ref, down_ref, rows_ref, sem
    )
    table_ref[...] = table
    select_ref[...] = select
    x_out[...] = x_ref[...]
    copy.wait()


def local_kernel(
    rim, x_ref, nbr_ref, coup_ref, source_ref, out_ref, terms, near, coup, source, sems, source_sem,
    at_start=None, at_end=None,
):
    slots, blocks = nbr_ref.shape
    chunks = blocks // LANES
    spans = [slice(c * LANES, (c + 1) * LANES) for c in range(chunks)]
    copies = [
        pltpu.make_async_copy(coup_ref.at[:, :, :, spans[c]], coup.at[c], sems.at[c])
        for c in range(chunks)
    ]
    for copy in copies:
        copy.start()
    source_copy = pltpu.make_async_copy(source_ref, source, source_sem)
    source_copy.start()
    lane = lax.broadcasted_iota(jnp.int32, (BW, LANES), 1)
    moved = pltpu.roll(x_ref[...], rim, 1)
    head = jnp.where(lane < rim, 0.0, moved[:, :LANES])
    tail = jnp.where(lane < rim, moved[:, :LANES], 0.0)
    terms[:BW], terms[BW:] = split(jnp.concatenate([head, moved[:, LANES:], tail], axis=1))
    rows = lax.broadcasted_iota(jnp.int32, (2 * LANES, LANES), 0)

    pairs = range(0, slots, 2)

    def gather(c, m):
        window = slice(c * LANES, (c + 2) * LANES)
        table = jnp.concatenate(
            [onehot(rows == nbr_ref[i : i + 1, spans[c]] - c * LANES) for i in (m, m + 1)], axis=1
        )
        both = jnp.dot(terms[:, window], table, preferred_element_type=jnp.float32)
        near[c][:, m * LANES : (m + 2) * LANES] = both[:BW] + both[BW:]

    for m in pairs:
        gather(0, m)
    if at_start is not None:
        at_start()
    for c in range(chunks):
        copies[c].wait()
        if c == 0:
            source_copy.wait()
        ahead = list(pairs) if c + 1 < chunks else []
        for at in range(0, CELLS, PACK):
            if ahead:
                gather(c + 1, ahead.pop(0))
            if at_end is not None and c + 1 == chunks:
                at_end(at)
            total = [None] * VARS
            for m in range(slots):
                for v in range(VARS):
                    span = slice(v * CELLS + at, v * CELLS + at + PACK)
                    value = near[c][span, m * LANES : (m + 1) * LANES]
                    for u in range(VARS):
                        term = coup[c, m, u, span, :].astype(jnp.float32) * value
                        total[u] = term if total[u] is None else total[u] + term
            for u in range(VARS):
                span = slice(u * CELLS + at, u * CELLS + at + PACK)
                out_ref[span, spans[c]] = source[span, spans[c]] - x_ref[span, spans[c]] + total[u]


def first_local_kernel(
    rim, x_ref, nbr_ref, coup_ref, source_ref, dst_ref, weight_ref,
    out_ref, rimcoup_ref, rimrow_ref, table_ref, weight_out,
    terms, near, coup, source, sems, source_sem,
):
    slots, blocks = nbr_ref.shape
    chunks = blocks // LANES
    fringe = dst_ref.shape[1]
    lane = lax.broadcasted_iota(jnp.int32, (PACK, LANES), 1)
    first = lane < LANES // 2
    masks = [lax.rem(lane + rim + LANES - m * 2 * rim, LANES) < 2 * rim for m in range(slots)]

    def merged(ends, nothing):
        result = nothing
        for m in range(slots):
            both = jnp.where(first, *ends(m))
            if m > 0:
                both = pltpu.roll(both, m * 2 * rim, 1)
            result = jnp.where(masks[m], both, result)
        return result

    def rows(m):
        lower = jnp.broadcast_to(nbr_ref[m : m + 1, :LANES], (PACK, LANES))
        upper = jnp.broadcast_to(nbr_ref[m : m + 1, blocks - LANES :], (PACK, LANES))
        return jnp.where(lower < rim, lower, -LANES), jnp.where(upper >= blocks + rim, upper - blocks, -LANES)

    def tables():
        rimrow_ref[...] = merged(rows, jnp.full((PACK, LANES), -LANES, jnp.int32))
        weight_out[...] = weight_ref[...]
        targets = jnp.broadcast_to(dst_ref[...], (LANES, fringe)).T
        for c in range(chunks):
            table_ref[:, c * LANES : (c + 1) * LANES] = onehot(targets == lane[:1] + c * LANES)

    def rim_coupling(at):
        for u in range(VARS):
            for v in range(VARS):
                span = slice(v * CELLS + at, v * CELLS + at + PACK)
                rimcoup_ref[u, span, :] = merged(
                    lambda m: (coup[0, m, u, span, :], coup[chunks - 1, m, u, span, :]),
                    jnp.zeros((PACK, LANES), jnp.bfloat16),
                )

    local_kernel(
        rim, x_ref, nbr_ref, coup_ref, source_ref, out_ref, terms, near, coup, source, sems, source_sem,
        tables, rim_coupling,
    )


def full_residual(local_ref, inc_ref, lower_ref, upper_ref, table_ref, weight_ref, rimcoup_ref, rimrow_ref):
    rim = lower_ref.shape[0]
    blocks = local_ref.shape[1]
    rims = jnp.concatenate(
        [lower_ref[...], upper_ref[...], jnp.zeros((LANES - 2 * rim, BW), jnp.float32)], axis=0
    ).T
    high, low = split(rims)
    low = pltpu.roll(low.astype(jnp.float32), 2 * rim, 1)
    rims = (high.astype(jnp.float32) + low).astype(jnp.bfloat16)
    sub = lax.broadcasted_iota(jnp.int32, (LANES, LANES), 0)
    row = rimrow_ref[:1]
    reads = onehot((sub == row) | (sub == row + 2 * rim))
    near = jnp.dot(rims, reads, preferred_element_type=jnp.float32)
    edge = []
    for u in range(VARS):
        total = None
        for v in range(VARS):
            span = slice(v * CELLS, (v + 1) * CELLS)
            term = rimcoup_ref[u, span, :].astype(jnp.float32) * near[span]
            total = term if total is None else total + term
        edge.append(total)
    edge = jnp.concatenate(edge, axis=0)
    shift = LANES // 2
    while shift >= 2 * rim:
        edge = edge + pltpu.roll(edge, shift, 1)
        shift //= 2
    lane = lax.broadcasted_iota(jnp.int32, (BW, LANES), 1)
    rest = inc_ref[:, 4]
    rest = jnp.concatenate([rest[:, :, :CELLS], rest[:, :, CELLS:]], axis=1).reshape(-1, CELLS)
    fringe = [inc_ref[:, 0:2].reshape(-1, LANES).T, inc_ref[:, 2:4].reshape(-1, LANES).T, rest.T]
    total = local_ref[...] + pick(jnp.concatenate(fringe, axis=0) * weight_ref[...], table_ref[...])
    lower = total[:, :LANES] + jnp.where(lane < rim, edge, 0.0)
    upper = total[:, blocks - LANES :] + jnp.where(lane >= LANES - rim, edge, 0.0)
    return jnp.concatenate([lower, total[:, LANES : blocks - LANES], upper], axis=1)


def precondition(diag_ref, resid_ref, u, at):
    total = None
    for v in range(VARS):
        span = pl.ds(v * CELLS + at, PACK)
        term = diag_ref[u, span, :].astype(jnp.float32) * resid_ref[span, :]
        total = term if total is None else total + term
    return total


def lane_sums(resid):
    square = jnp.sum(resid * resid, axis=0, keepdims=True)
    return sum(square[:, i : i + LANES] for i in range(0, square.shape[1], LANES))


def advance_kernel(
    local_ref, inc_ref, lower_ref, upper_ref, across_ref, weight_ref, rimcoup_ref, rimrow_ref,
    diag_ref, x_ref, table_ref, select_ref,
    next_ref, norm_ref, out_ref, up_ref, down_ref, resid, diag, diag_sems, rows_ref, sem,
):
    fetches = [
        pltpu.make_async_copy(diag_ref.at[u], diag.at[u], diag_sems.at[u]) for u in range(VARS)
    ]
    for fetch in fetches:
        fetch.start()
    resid[...] = full_residual(
        local_ref, inc_ref, lower_ref, upper_ref, across_ref, weight_ref, rimcoup_ref, rimrow_ref
    )
    for u in range(VARS):
        fetches[u].wait()
        for at in range(0, CELLS, PACK):
            total = None
            for v in range(VARS):
                span = slice(v * CELLS + at, v * CELLS + at + PACK)
                term = diag[u, span].astype(jnp.float32) * resid[span]
                total = term if total is None else total + term
            span = slice(u * CELLS + at, u * CELLS + at + PACK)
            next_ref[span, :] = x_ref[span, :] + STEP_CFL * total
    copy = send_blocks(
        next_ref[...], table_ref[...], select_ref[...], out_ref, up_ref, down_ref, rows_ref, sem
    )
    norm_ref[...] = lane_sums(resid[...])
    copy.wait()


def residual_kernel(
    local_ref, inc_ref, lower_ref, upper_ref, across_ref, weight_ref, rimcoup_ref, rimrow_ref, norm_ref,
    resid_ref, sums_ref,
):
    resid = full_residual(
        local_ref, inc_ref, lower_ref, upper_ref, across_ref, weight_ref, rimcoup_ref, rimrow_ref
    )
    resid_ref[...] = resid
    both = jnp.concatenate([norm_ref[...], lane_sums(resid)], axis=0)
    sums_ref[...] = jnp.broadcast_to(both[None], sums_ref.shape)


def direction_kernel(diag_ref, resid_ref, out_ref, resid_out):
    resid_out[...] = resid_ref[...]

    def cells(part, carry):
        at = pl.multiple_of(part * PACK, PACK)
        for u in range(VARS):
            out_ref[pl.ds(u * CELLS + at, PACK), :] = precondition(diag_ref, resid_ref, u, at)
        return carry

    lax.fori_loop(0, CELLS // PACK, cells, 0)


def finish_kernel(entries, sums_ref, x_ref, update_ref, out_ref):
    sums = jnp.sum(jnp.sum(sums_ref[...], axis=0), axis=1, keepdims=True) / entries + 1e-06
    cfl = STEP_CFL * jnp.sqrt(sums[0:1] / sums[1:2])
    out_ref[...] = x_ref[...] + cfl * update_ref[...]


VMEM = pl.BlockSpec(memory_space=pltpu.VMEM)
SMEM = pl.BlockSpec(memory_space=pltpu.SMEM)


def f32(*shape):
    return jax.ShapeDtypeStruct(shape, jnp.float32)


def bf16(*shape):
    return jax.ShapeDtypeStruct(shape, jnp.bfloat16)


def call(kernel, in_specs, out_shape, flops, moved, **more):
    many = isinstance(out_shape, (list, tuple))
    return pl.pallas_call(
        kernel,
        in_specs=in_specs,
        out_specs=more.pop("out_specs", [VMEM] * len(out_shape) if many else VMEM),
        out_shape=out_shape,
        compiler_params=pltpu.CompilerParams(vmem_limit_bytes=VMEM_LIMIT),
        cost_estimate=pl.CostEstimate(flops=flops, bytes_accessed=moved, transcendentals=0),
        **more,
    )


def shards(
    psi_init, source, coupling, diag_inv, neighbours, seam_perm, fringe_src, fringe_dst, fringe_weight
):
    blocks = psi_init.shape[0]
    slots = neighbours.shape[1]
    rim = seam_perm.shape[1]
    fringe = fringe_src.shape[1]
    peers = lax.axis_size("blk")
    devices = lax.axis_size("body") * peers
    up = [(i, (i + 1) % peers) for i in range(peers)]
    down = [(j, i) for i, j in up]
    here = functools.partial(pltpu.with_memory_space_constraint, memory_space=pltpu.HBM)
    x = here(psi_init.T)
    source_t = here(source.T)
    coup = here(coupling.transpose(1, 2, 3, 0))
    diag = here(diag_inv.transpose(1, 2, 0))
    nbr = here(neighbours.T)
    state = f32(BW, blocks)
    hbm = pl.BlockSpec(memory_space=pltpu.HBM)
    message = (devices, BW * fringe // devices // (rim // 2 * LANES), rim // 2, LANES)
    sent = [f32(*message), f32(rim, BW), f32(rim, BW)]
    rows_scratch = [pltpu.VMEM(message, jnp.float32), pltpu.SemaphoreType.DMA]
    size = 4 * BW * blocks

    donors = call(
        donors_kernel,
        [VMEM, VMEM, SMEM],
        sent + [bf16(blocks, fringe), bf16(2 * LANES, LANES), state],
        4 * BW * blocks * fringe,
        2 * size,
        out_specs=[hbm] + [VMEM] * 5,
        scratch_shapes=rows_scratch,
    )
    chunks = blocks // LANES
    scratch = [
        pltpu.VMEM((2 * BW, blocks + LANES), jnp.bfloat16),
        [pltpu.VMEM((BW, slots * LANES), jnp.float32)] * chunks,
        pltpu.VMEM((chunks, slots, VARS, BW, LANES), jnp.bfloat16),
        pltpu.VMEM((BW, blocks), jnp.float32),
        pltpu.SemaphoreType.DMA((chunks,)),
        pltpu.SemaphoreType.DMA,
    ]
    local_more = dict(
        flops=4 * BW * 2 * LANES * slots * blocks,
        moved=coup.size * 2 + 4 * size,
        scratch_shapes=scratch,
    )
    first_local = call(
        functools.partial(first_local_kernel, rim),
        [VMEM, VMEM, hbm, hbm, VMEM, VMEM],
        [
            state,
            bf16(VARS, BW, LANES),
            jax.ShapeDtypeStruct((PACK, LANES), jnp.int32),
            bf16(fringe, blocks),
            f32(1, fringe),
        ],
        **local_more,
    )
    local = call(functools.partial(local_kernel, rim), [VMEM, VMEM, hbm, hbm], state, **local_more)
    advance = call(
        advance_kernel,
        [VMEM] * 8 + [hbm] + [VMEM] * 3,
        [state, f32(1, LANES)] + sent,
        8 * BW * blocks * fringe,
        diag.size * 2 + 4 * size,
        out_specs=[VMEM, VMEM, hbm, VMEM, VMEM],
        scratch_shapes=[
            pltpu.VMEM((BW, blocks), jnp.float32),
            pltpu.VMEM((VARS, BW, blocks), jnp.bfloat16),
            pltpu.SemaphoreType.DMA((VARS,)),
        ]
        + rows_scratch,
    )
    residual = call(
        residual_kernel,
        [VMEM] * 9,
        [state, f32(devices, 2, LANES)],
        4 * BW * blocks * fringe,
        3 * size,
    )
    direction = call(
        direction_kernel, [VMEM] * 2, [state, state], diag.size * 2, diag.size * 2 + 2 * size
    )
    finish = call(
        functools.partial(finish_kernel, float(blocks * devices * BW)),
        [VMEM] * 3,
        state,
        2 * BW * blocks,
        3 * size,
    )

    def exchange(rows, to_up, to_down):
        rows = lax.all_to_all(rows, ("body", "blk"), split_axis=0, concat_axis=0, tiled=True)
        return rows, lax.ppermute(to_up, "blk", up), lax.ppermute(to_down, "blk", down)

    *out, table, select, x_here = donors(x, here(fringe_src), here(seam_perm))
    arrived = exchange(*out)
    part, rimcoup, rimrow, across, weight = first_local(
        x_here, nbr, coup, source_t, here(fringe_dst), here(fringe_weight)
    )
    across = (across, weight, rimcoup, rimrow)
    x, norm, *out = advance(part, *arrived, *across, diag, x_here, table, select)
    arrived = exchange(*out)
    part = local(x, nbr, coup, source_t)
    resid, sums = residual(part, *arrived, *across, norm)
    sums = lax.all_to_all(sums, ("body", "blk"), split_axis=0, concat_axis=0, tiled=True)
    update, resid = direction(diag, resid)
    x = finish(sums, x, update)
    return (x.T, resid.T)


def solution(mesh):
    return jax.shard_map(
        shards,
        mesh=mesh,
        in_specs=(
            P(("body", "blk"), None),
            P(("body", "blk"), None),
            P(("body", "blk"), None, None, None),
            P(("body", "blk"), None, None),
            P(("body", "blk"), None),
            P("body", None),
            P(("body", "blk"), None),
            P(("body", "blk"), None),
            P(("body", "blk"), None),
        ),
        out_specs=(P(("body", "blk"), None), P(("body", "blk"), None)),
        check_vma=False,
    )
```

```python
import functools
import math

import jax
import jax.numpy as jnp
from jax import lax
from jax.experimental import pallas as pl
from jax.experimental.pallas import tpu as pltpu
from jax.sharding import PartitionSpec as P

CELLS = 64
VARS = 5
BW = 320
STEP_CFL = 0.5
LANES = 128
PACK = 16
VMEM_LIMIT = 32 * 1024 * 1024


def split(x):
    high = x.astype(jnp.bfloat16)
    return high, (x - high.astype(jnp.float32)).astype(jnp.bfloat16)


def onehot(mask):
    return jnp.where(mask, 1.0, 0.0).astype(jnp.bfloat16)


def pick(x, table):
    both = jnp.dot(jnp.concatenate(split(x), axis=0), table, preferred_element_type=jnp.float32)
    return both[: x.shape[0]] + both[x.shape[0] :]


def send_blocks(x, table, select, out_ref, up_ref, down_ref, rows_ref, sem):
    rim = up_ref.shape[0]
    half = rows_ref.shape[2]
    rows = pick(x, table).T.reshape(rows_ref.shape[0], 2 * half, BW)
    for h in range(2):
        for tile in range(2):
            rows_ref[:, 2 * tile + h] = rows[:, h * half : (h + 1) * half, tile * LANES : (tile + 1) * LANES]
    rest = rows[:, :, 2 * LANES :]
    rows_ref[:, 4] = jnp.concatenate([rest[:, :half], rest[:, half:]], axis=2)
    copy = pltpu.make_async_copy(rows_ref, out_ref, sem)
    copy.start()
    index = lax.axis_index("blk")
    at_last = index == lax.axis_size("blk") - 1
    at_first = index == 0
    first = lax.broadcasted_iota(jnp.int32, (BW, LANES), 1) < LANES // 2
    ends = split(jnp.where(first, x[:, :LANES], x[:, x.shape[1] - LANES :]))
    rims = jnp.dot(jnp.concatenate(ends, axis=1), select, preferred_element_type=jnp.float32)
    lane = lax.broadcasted_iota(jnp.int32, (1, LANES), 1)
    turn_up = (lane < rim) & at_last
    turn_down = (lane >= rim) & at_first
    angle = 2.0 * math.pi / 3.0
    cosine = jnp.where(turn_up | turn_down, math.cos(angle), 1.0)
    sine = jnp.where(turn_up, math.sin(angle), jnp.where(turn_down, -math.sin(angle), 0.0))
    first = rims[2 * CELLS : 3 * CELLS]
    second = rims[3 * CELLS : 4 * CELLS]
    rims = jnp.concatenate(
        [
            rims[: 2 * CELLS],
            cosine * first - sine * second,
            sine * first + cosine * second,
            rims[4 * CELLS :],
        ],
        axis=0,
    ).T
    up_ref[...] = rims[:rim]
    down_ref[...] = rims[rim : 2 * rim]
    return copy


def donors_kernel(
    x_ref, src_ref, perm_ref,
    out_ref, up_ref, down_ref, table_ref, select_ref, x_out, rows_ref, sem, src, perm, sems,
):
    small = [
        pltpu.make_async_copy(src_ref, src, sems.at[VARS]),
        pltpu.make_async_copy(perm_ref, perm, sems.at[VARS + 1]),
    ]
    large = []
    for v in range(VARS):
        span = pl.ds(v * CELLS, CELLS)
        large.append(pltpu.make_async_copy(x_ref.at[span], x_out.at[span], sems.at[v]))
    for copy in small:
        copy.start()
    for v in range(VARS):
        large[v].start(priority=v % 2)
    for copy in small:
        copy.wait()
    rim = up_ref.shape[0]
    index = lax.axis_index("blk")
    at_last = index == lax.axis_size("blk") - 1
    at_first = index == 0
    sub = lax.broadcasted_iota(jnp.int32, (LANES, LANES), 0)
    lane = lax.broadcasted_iota(jnp.int32, (LANES, LANES), 1)
    wanted = lane[:1]
    target = sub[:, :1]
    for j in range(rim):
        partner = perm[0, j]
        wanted = jnp.where((lane[:1] == j) & at_last, partner, wanted)
        target = jnp.where((sub[:, :1] == j) & at_first, partner, target)
    to_up = (sub == wanted + (LANES - rim)) & (lane < rim)
    to_down = (target + rim == lane) & (sub < rim)
    select = onehot(to_up | to_down)
    select = jnp.concatenate([select, select], axis=0)
    rows = lax.broadcasted_iota(jnp.int32, table_ref.shape, 0)
    table = onehot(rows == src[...])
    for copy in large:
        copy.wait()
    copy = send_blocks(
        x_out[...], table, select, out_ref, up_ref, down_ref, rows_ref, sem
    )
    table_ref[...] = table
    select_ref[...] = select
    copy.wait()


def local_kernel(
    rim, x_ref, nbr_ref, coup_ref, source_ref, out_ref, terms, near, coup, source, sems, source_sem,
    at_start=None, with_ends=None,
):
    slots, blocks = nbr_ref.shape
    chunks = blocks // LANES
    spans = [slice(c * LANES, (c + 1) * LANES) for c in range(chunks)]
    order = [0, chunks - 1, *range(1, chunks - 1)]
    source_copy = pltpu.make_async_copy(source_ref, source, source_sem)
    copies = {}
    for c in order:
        copies[c] = [
            pltpu.make_async_copy(coup_ref.at[m, :, :, spans[c]], coup.at[c, m], sems.at[c, m])
            for m in range(slots)
        ]
        for m in range(slots):
            copies[c][m].start(priority=m % 2)
        if c == order[0]:
            source_copy.start()
    lane = lax.broadcasted_iota(jnp.int32, (BW, LANES), 1)
    moved = pltpu.roll(x_ref[...], rim, 1)
    head = jnp.where(lane < rim, 0.0, moved[:, :LANES])
    tail = jnp.where(lane < rim, moved[:, :LANES], 0.0)
    terms[:BW], terms[BW:] = split(jnp.concatenate([head, moved[:, LANES:], tail], axis=1))
    rows = lax.broadcasted_iota(jnp.int32, (2 * LANES, LANES), 0)

    pairs = range(0, slots, 2)

    def gather(c, m):
        window = slice(c * LANES, (c + 2) * LANES)
        table = jnp.concatenate(
            [onehot(rows == nbr_ref[i : i + 1, spans[c]] - c * LANES) for i in (m, m + 1)], axis=1
        )
        both = jnp.dot(terms[:, window], table, preferred_element_type=jnp.float32)
        near[c][:, m * LANES : (m + 2) * LANES] = both[:BW] + both[BW:]

    for m in pairs:
        gather(order[0], m)
    if at_start is not None:
        at_start()
    for step, c in enumerate(order):
        for copy in copies[c]:
            copy.wait()
        if step == 0:
            source_copy.wait()
        ahead = list(pairs) if step + 1 < chunks else []
        for at in range(0, CELLS, PACK):
            if ahead:
                gather(order[step + 1], ahead.pop(0))
            if with_ends is not None and step in (1, 2) and (at < CELLS // 2) == (step == 1):
                with_ends(at)
            total = [None] * VARS
            for m in range(slots):
                for v in range(VARS):
                    span = slice(v * CELLS + at, v * CELLS + at + PACK)
                    value = near[c][span, m * LANES : (m + 1) * LANES]
                    for u in range(VARS):
                        term = coup[c, m, u, span, :].astype(jnp.float32) * value
                        total[u] = term if total[u] is None else total[u] + term
            for u in range(VARS):
                span = slice(u * CELLS + at, u * CELLS + at + PACK)
                out_ref[span, spans[c]] = source[span, spans[c]] - x_ref[span, spans[c]] + total[u]


def first_local_kernel(
    rim, x_ref, nbr_ref, coup_ref, source_ref, dst_ref, weight_ref,
    out_ref, rimcoup_ref, rimrow_ref, table_ref, weight_out,
    terms, near, coup, source, sems, source_sem,
):
    slots, blocks = nbr_ref.shape
    chunks = blocks // LANES
    fringe = dst_ref.shape[1]
    lane = lax.broadcasted_iota(jnp.int32, (PACK, LANES), 1)
    first = lane < LANES // 2
    masks = [lax.rem(lane + rim + LANES - m * 2 * rim, LANES) < 2 * rim for m in range(slots)]

    def merged(ends, nothing):
        result = nothing
        for m in range(slots):
            both = jnp.where(first, *ends(m))
            if m > 0:
                both = pltpu.roll(both, m * 2 * rim, 1)
            result = jnp.where(masks[m], both, result)
        return result

    def rows(m):
        lower = jnp.broadcast_to(nbr_ref[m : m + 1, :LANES], (PACK, LANES))
        upper = jnp.broadcast_to(nbr_ref[m : m + 1, blocks - LANES :], (PACK, LANES))
        return jnp.where(lower < rim, lower, -LANES), jnp.where(upper >= blocks + rim, upper - blocks, -LANES)

    def tables():
        rimrow_ref[...] = merged(rows, jnp.full((PACK, LANES), -LANES, jnp.int32))
        weight_out[...] = weight_ref[...]
        targets = jnp.broadcast_to(dst_ref[...], (LANES, fringe)).T
        for c in range(chunks):
            table_ref[:, c * LANES : (c + 1) * LANES] = onehot(targets == lane[:1] + c * LANES)

    def rim_coupling(at):
        for u in range(VARS):
            for v in range(VARS):
                span = slice(v * CELLS + at, v * CELLS + at + PACK)
                rimcoup_ref[u, span, :] = merged(
                    lambda m: (coup[0, m, u, span, :], coup[chunks - 1, m, u, span, :]),
                    jnp.zeros((PACK, LANES), jnp.bfloat16),
                )

    local_kernel(
        rim, x_ref, nbr_ref, coup_ref, source_ref, out_ref, terms, near, coup, source, sems, source_sem,
        tables, rim_coupling,
    )


def full_residual(local_ref, inc_ref, lower_ref, upper_ref, table_ref, weight_ref, rimcoup_ref, rimrow_ref):
    rim = lower_ref.shape[0]
    blocks = local_ref.shape[1]
    rims = jnp.concatenate(
        [lower_ref[...], upper_ref[...], jnp.zeros((LANES - 2 * rim, BW), jnp.float32)], axis=0
    ).T
    high, low = split(rims)
    low = pltpu.roll(low.astype(jnp.float32), 2 * rim, 1)
    rims = (high.astype(jnp.float32) + low).astype(jnp.bfloat16)
    sub = lax.broadcasted_iota(jnp.int32, (LANES, LANES), 0)
    row = rimrow_ref[:1]
    reads = onehot((sub == row) | (sub == row + 2 * rim))
    near = jnp.dot(rims, reads, preferred_element_type=jnp.float32)
    edge = []
    for u in range(VARS):
        total = None
        for v in range(VARS):
            span = slice(v * CELLS, (v + 1) * CELLS)
            term = rimcoup_ref[u, span, :].astype(jnp.float32) * near[span]
            total = term if total is None else total + term
        edge.append(total)
    edge = jnp.concatenate(edge, axis=0)
    shift = LANES // 2
    while shift >= 2 * rim:
        edge = edge + pltpu.roll(edge, shift, 1)
        shift //= 2
    lane = lax.broadcasted_iota(jnp.int32, (BW, LANES), 1)
    rest = inc_ref[:, 4]
    rest = jnp.concatenate([rest[:, :, :CELLS], rest[:, :, CELLS:]], axis=1).reshape(-1, CELLS)
    fringe = [inc_ref[:, 0:2].reshape(-1, LANES).T, inc_ref[:, 2:4].reshape(-1, LANES).T, rest.T]
    total = local_ref[...] + pick(jnp.concatenate(fringe, axis=0) * weight_ref[...], table_ref[...])
    lower = total[:, :LANES] + jnp.where(lane < rim, edge, 0.0)
    upper = total[:, blocks - LANES :] + jnp.where(lane >= LANES - rim, edge, 0.0)
    return jnp.concatenate([lower, total[:, LANES : blocks - LANES], upper], axis=1)


def precondition(diag_ref, resid_ref, u, at):
    total = None
    for v in range(VARS):
        span = pl.ds(v * CELLS + at, PACK)
        term = diag_ref[u, span, :].astype(jnp.float32) * resid_ref[span, :]
        total = term if total is None else total + term
    return total


def lane_sums(resid):
    square = jnp.sum(resid * resid, axis=0, keepdims=True)
    return sum(square[:, i : i + LANES] for i in range(0, square.shape[1], LANES))


def advance_kernel(
    local_ref, inc_ref, lower_ref, upper_ref, across_ref, weight_ref, rimcoup_ref, rimrow_ref,
    diag_ref, x_ref, table_ref, select_ref,
    next_ref, norm_ref, out_ref, up_ref, down_ref, resid, diag, diag_sems, rows_ref, sem,
):
    fetches = []
    for u in range(VARS):
        halves = [slice(0, BW // 2), slice(BW // 2, BW)]
        fetches.append(
            [
                pltpu.make_async_copy(diag_ref.at[u, halves[i]], diag.at[u, halves[i]], diag_sems.at[u, i])
                for i in range(2)
            ]
        )
        for i in range(2):
            fetches[u][i].start(priority=i)
    resid[...] = full_residual(
        local_ref, inc_ref, lower_ref, upper_ref, across_ref, weight_ref, rimcoup_ref, rimrow_ref
    )
    for u in range(VARS):
        for fetch in fetches[u]:
            fetch.wait()
        for at in range(0, CELLS, PACK):
            total = None
            for v in range(VARS):
                span = slice(v * CELLS + at, v * CELLS + at + PACK)
                term = diag[u, span].astype(jnp.float32) * resid[span]
                total = term if total is None else total + term
            span = slice(u * CELLS + at, u * CELLS + at + PACK)
            next_ref[span, :] = x_ref[span, :] + STEP_CFL * total
    copy = send_blocks(
        next_ref[...], table_ref[...], select_ref[...], out_ref, up_ref, down_ref, rows_ref, sem
    )
    norm_ref[...] = lane_sums(resid[...])
    copy.wait()


def residual_kernel(
    local_ref, inc_ref, lower_ref, upper_ref, across_ref, weight_ref, rimcoup_ref, rimrow_ref, norm_ref,
    resid_ref, sums_ref,
):
    resid = full_residual(
        local_ref, inc_ref, lower_ref, upper_ref, across_ref, weight_ref, rimcoup_ref, rimrow_ref
    )
    resid_ref[...] = resid
    both = jnp.concatenate([norm_ref[...], lane_sums(resid)], axis=0)
    sums_ref[...] = jnp.broadcast_to(both[None], sums_ref.shape)


def direction_kernel(diag_ref, resid_ref, out_ref, resid_out):
    resid_out[...] = resid_ref[...]

    def cells(part, carry):
        at = pl.multiple_of(part * PACK, PACK)
        for u in range(VARS):
            out_ref[pl.ds(u * CELLS + at, PACK), :] = precondition(diag_ref, resid_ref, u, at)
        return carry

    lax.fori_loop(0, CELLS // PACK, cells, 0)


def finish_kernel(entries, sums_ref, x_ref, update_ref, out_ref):
    sums = jnp.sum(jnp.sum(sums_ref[...], axis=0), axis=1, keepdims=True) / entries + 1e-06
    cfl = STEP_CFL * jnp.sqrt(sums[0:1] / sums[1:2])
    out_ref[...] = x_ref[...] + cfl * update_ref[...]


VMEM = pl.BlockSpec(memory_space=pltpu.VMEM)


def f32(*shape):
    return jax.ShapeDtypeStruct(shape, jnp.float32)


def bf16(*shape):
    return jax.ShapeDtypeStruct(shape, jnp.bfloat16)


def call(kernel, in_specs, out_shape, flops, moved, **more):
    many = isinstance(out_shape, (list, tuple))
    return pl.pallas_call(
        kernel,
        in_specs=in_specs,
        out_specs=more.pop("out_specs", [VMEM] * len(out_shape) if many else VMEM),
        out_shape=out_shape,
        compiler_params=pltpu.CompilerParams(vmem_limit_bytes=VMEM_LIMIT),
        cost_estimate=pl.CostEstimate(flops=flops, bytes_accessed=moved, transcendentals=0),
        **more,
    )


def shards(
    psi_init, source, coupling, diag_inv, neighbours, seam_perm, fringe_src, fringe_dst, fringe_weight
):
    blocks = psi_init.shape[0]
    slots = neighbours.shape[1]
    rim = seam_perm.shape[1]
    fringe = fringe_src.shape[1]
    peers = lax.axis_size("blk")
    devices = lax.axis_size("body") * peers
    up = [(i, (i + 1) % peers) for i in range(peers)]
    down = [(j, i) for i, j in up]
    here = functools.partial(pltpu.with_memory_space_constraint, memory_space=pltpu.HBM)
    x = here(psi_init.T)
    source_t = here(source.T)
    coup = here(coupling.transpose(1, 2, 3, 0))
    diag = here(diag_inv.transpose(1, 2, 0))
    nbr = here(neighbours.T)
    state = f32(BW, blocks)
    hbm = pl.BlockSpec(memory_space=pltpu.HBM)
    message = (devices, BW * fringe // devices // (rim // 2 * LANES), rim // 2, LANES)
    sent = [f32(*message), f32(rim, BW), f32(rim, BW)]
    rows_scratch = [pltpu.VMEM(message, jnp.float32), pltpu.SemaphoreType.DMA]
    size = 4 * BW * blocks

    donors = call(
        donors_kernel,
        [hbm] * 3,
        sent + [bf16(blocks, fringe), bf16(2 * LANES, LANES), state],
        4 * BW * blocks * fringe,
        2 * size,
        out_specs=[hbm] + [VMEM] * 5,
        scratch_shapes=rows_scratch
        + [
            pltpu.VMEM((1, fringe), jnp.int32),
            pltpu.SMEM((1, rim), jnp.int32),
            pltpu.SemaphoreType.DMA((VARS + 2,)),
        ],
    )
    chunks = blocks // LANES
    scratch = [
        pltpu.VMEM((2 * BW, blocks + LANES), jnp.bfloat16),
        [pltpu.VMEM((BW, slots * LANES), jnp.float32)] * chunks,
        pltpu.VMEM((chunks, slots, VARS, BW, LANES), jnp.bfloat16),
        pltpu.VMEM((BW, blocks), jnp.float32),
        pltpu.SemaphoreType.DMA((chunks, slots)),
        pltpu.SemaphoreType.DMA,
    ]
    local_more = dict(
        flops=4 * BW * 2 * LANES * slots * blocks,
        moved=coup.size * 2 + 4 * size,
        scratch_shapes=scratch,
    )
    first_local = call(
        functools.partial(first_local_kernel, rim),
        [VMEM, VMEM, hbm, hbm, VMEM, VMEM],
        [
            state,
            bf16(VARS, BW, LANES),
            jax.ShapeDtypeStruct((PACK, LANES), jnp.int32),
            bf16(fringe, blocks),
            f32(1, fringe),
        ],
        **local_more,
    )
    local = call(functools.partial(local_kernel, rim), [VMEM, VMEM, hbm, hbm], state, **local_more)
    advance = call(
        advance_kernel,
        [VMEM] * 8 + [hbm] + [VMEM] * 3,
        [state, f32(1, LANES)] + sent,
        8 * BW * blocks * fringe,
        diag.size * 2 + 4 * size,
        out_specs=[VMEM, VMEM, hbm, VMEM, VMEM],
        scratch_shapes=[
            pltpu.VMEM((BW, blocks), jnp.float32),
            pltpu.VMEM((VARS, BW, blocks), jnp.bfloat16),
            pltpu.SemaphoreType.DMA((VARS, 2)),
        ]
        + rows_scratch,
    )
    residual = call(
        residual_kernel,
        [VMEM] * 9,
        [state, f32(devices, 2, LANES)],
        4 * BW * blocks * fringe,
        3 * size,
    )
    direction = call(
        direction_kernel, [VMEM] * 2, [state, state], diag.size * 2, diag.size * 2 + 2 * size
    )
    finish = call(
        functools.partial(finish_kernel, float(blocks * devices * BW)),
        [VMEM] * 3,
        state,
        2 * BW * blocks,
        3 * size,
    )

    def exchange(rows, to_up, to_down):
        rows = lax.all_to_all(rows, ("body", "blk"), split_axis=0, concat_axis=0, tiled=True)
        return rows, lax.ppermute(to_up, "blk", up), lax.ppermute(to_down, "blk", down)

    *out, table, select, x_here = donors(x, here(fringe_src), here(seam_perm))
    arrived = exchange(*out)
    part, rimcoup, rimrow, across, weight = first_local(
        x_here, nbr, coup, source_t, here(fringe_dst), here(fringe_weight)
    )
    across = (across, weight, rimcoup, rimrow)
    x, norm, *out = advance(part, *arrived, *across, diag, x_here, table, select)
    arrived = exchange(*out)
    part = local(x, nbr, coup, source_t)
    resid, sums = residual(part, *arrived, *across, norm)
    sums = lax.all_to_all(sums, ("body", "blk"), split_axis=0, concat_axis=0, tiled=True)
    update, resid = direction(diag, resid)
    x = finish(sums, x, update)
    return (x.T, resid.T)


def solution(mesh):
    return jax.shard_map(
        shards,
        mesh=mesh,
        in_specs=(
            P(("body", "blk"), None),
            P(("body", "blk"), None),
            P(("body", "blk"), None, None, None),
            P(("body", "blk"), None, None),
            P(("body", "blk"), None),
            P("body", None),
            P(("body", "blk"), None),
            P(("body", "blk"), None),
            P(("body", "blk"), None),
        ),
        out_specs=(P(("body", "blk"), None), P(("body", "blk"), None)),
        check_vma=False,
    )
```

```python
import functools
import math

import jax
import jax.numpy as jnp
from jax import lax
from jax.experimental import pallas as pl
from jax.experimental.pallas import tpu as pltpu
from jax.sharding import PartitionSpec as P

CELLS = 64
VARS = 5
BW = 320
STEP_CFL = 0.5
LANES = 128
PACK = 16
VMEM_LIMIT = 32 * 1024 * 1024


def split(x):
    high = x.astype(jnp.bfloat16)
    return high, (x - high.astype(jnp.float32)).astype(jnp.bfloat16)


def onehot(mask):
    return jnp.where(mask, 1.0, 0.0).astype(jnp.bfloat16)


def pick(x, table):
    both = jnp.dot(jnp.concatenate(split(x), axis=0), table, preferred_element_type=jnp.float32)
    return both[: x.shape[0]] + both[x.shape[0] :]


def send_blocks(x, table, select, out_ref, up_ref, down_ref, rows_ref, sem):
    rim = up_ref.shape[0]
    half = rows_ref.shape[2]
    rows = pick(x, table).T.reshape(rows_ref.shape[0], 2 * half, BW)
    for h in range(2):
        for tile in range(2):
            rows_ref[:, 2 * tile + h] = rows[:, h * half : (h + 1) * half, tile * LANES : (tile + 1) * LANES]
    rest = rows[:, :, 2 * LANES :]
    rows_ref[:, 4] = jnp.concatenate([rest[:, :half], rest[:, half:]], axis=2)
    copy = pltpu.make_async_copy(rows_ref, out_ref, sem)
    copy.start()
    index = lax.axis_index("blk")
    at_last = index == lax.axis_size("blk") - 1
    at_first = index == 0
    first = lax.broadcasted_iota(jnp.int32, (BW, LANES), 1) < LANES // 2
    ends = split(jnp.where(first, x[:, :LANES], x[:, x.shape[1] - LANES :]))
    rims = jnp.dot(jnp.concatenate(ends, axis=1), select, preferred_element_type=jnp.float32)
    lane = lax.broadcasted_iota(jnp.int32, (1, LANES), 1)
    turn_up = (lane < rim) & at_last
    turn_down = (lane >= rim) & at_first
    angle = 2.0 * math.pi / 3.0
    cosine = jnp.where(turn_up | turn_down, math.cos(angle), 1.0)
    sine = jnp.where(turn_up, math.sin(angle), jnp.where(turn_down, -math.sin(angle), 0.0))
    first = rims[2 * CELLS : 3 * CELLS]
    second = rims[3 * CELLS : 4 * CELLS]
    rims = jnp.concatenate(
        [
            rims[: 2 * CELLS],
            cosine * first - sine * second,
            sine * first + cosine * second,
            rims[4 * CELLS :],
        ],
        axis=0,
    ).T
    up_ref[...] = rims[:rim]
    down_ref[...] = rims[rim : 2 * rim]
    return copy


def donors_kernel(
    x_ref, src_ref, perm_ref,
    out_ref, up_ref, down_ref, table_ref, select_ref, x_out, rows_ref, sem,
):
    rim = up_ref.shape[0]
    index = lax.axis_index("blk")
    at_last = index == lax.axis_size("blk") - 1
    at_first = index == 0
    sub = lax.broadcasted_iota(jnp.int32, (LANES, LANES), 0)
    lane = lax.broadcasted_iota(jnp.int32, (LANES, LANES), 1)
    wanted = lane[:1]
    target = sub[:, :1]
    for j in range(rim):
        partner = perm_ref[0, j]
        wanted = jnp.where((lane[:1] == j) & at_last, partner, wanted)
        target = jnp.where((sub[:, :1] == j) & at_first, partner, target)
    to_up = (sub == wanted + (LANES - rim)) & (lane < rim)
    to_down = (target + rim == lane) & (sub < rim)
    select = onehot(to_up | to_down)
    select = jnp.concatenate([select, select], axis=0)
    rows = lax.broadcasted_iota(jnp.int32, table_ref.shape, 0)
    table = onehot(rows == src_ref[...])
    copy = send_blocks(
        x_ref[...], table, select, out_ref, up_ref, down_ref, rows_ref, sem
    )
    table_ref[...] = table
    select_ref[...] = select
    x_out[...] = x_ref[...]
    copy.wait()


def local_kernel(
    rim, x_ref, nbr_ref, coup_ref, source_ref, out_ref, terms, near, coup, source, sems, source_sem,
    at_start=None, with_ends=None,
):
    slots, blocks = nbr_ref.shape
    chunks = blocks // LANES
    spans = [slice(c * LANES, (c + 1) * LANES) for c in range(chunks)]
    order = [0, chunks - 1, *range(1, chunks - 1)]
    source_copy = pltpu.make_async_copy(source_ref, source, source_sem)
    copies = {}
    for c in order:
        copies[c] = pltpu.make_async_copy(coup_ref.at[:, :, :, spans[c]], coup.at[c], sems.at[c])
        copies[c].start()
        if c == order[0]:
            source_copy.start()
    lane = lax.broadcasted_iota(jnp.int32, (BW, LANES), 1)
    moved = pltpu.roll(x_ref[...], rim, 1)
    head = jnp.where(lane < rim, 0.0, moved[:, :LANES])
    tail = jnp.where(lane < rim, moved[:, :LANES], 0.0)
    terms[:BW], terms[BW:] = split(jnp.concatenate([head, moved[:, LANES:], tail], axis=1))
    rows = lax.broadcasted_iota(jnp.int32, (2 * LANES, LANES), 0)

    pairs = range(0, slots, 2)

    def gather(c, m):
        window = slice(c * LANES, (c + 2) * LANES)
        table = jnp.concatenate(
            [onehot(rows == nbr_ref[i : i + 1, spans[c]] - c * LANES) for i in (m, m + 1)], axis=1
        )
        both = jnp.dot(terms[:, window], table, preferred_element_type=jnp.float32)
        near[c][:, m * LANES : (m + 2) * LANES] = both[:BW] + both[BW:]

    for m in pairs:
        gather(order[0], m)
    if at_start is not None:
        at_start()
    for step, c in enumerate(order):
        copies[c].wait()
        if step == 0:
            source_copy.wait()
        ahead = list(pairs) if step + 1 < chunks else []
        for at in range(0, CELLS, PACK):
            if ahead:
                gather(order[step + 1], ahead.pop(0))
            if with_ends is not None and step in (1, 2) and (at < CELLS // 2) == (step == 1):
                with_ends(at)
            total = [None] * VARS
            for m in range(slots):
                for v in range(VARS):
                    span = slice(v * CELLS + at, v * CELLS + at + PACK)
                    value = near[c][span, m * LANES : (m + 1) * LANES]
                    for u in range(VARS):
                        term = coup[c, m, u, span, :].astype(jnp.float32) * value
                        total[u] = term if total[u] is None else total[u] + term
            for u in range(VARS):
                span = slice(u * CELLS + at, u * CELLS + at + PACK)
                out_ref[span, spans[c]] = source[span, spans[c]] - x_ref[span, spans[c]] + total[u]


def first_local_kernel(
    rim, x_ref, nbr_ref, coup_ref, source_ref, dst_ref, weight_ref,
    out_ref, rimcoup_ref, rimrow_ref, table_ref, weight_out,
    terms, near, coup, source, sems, source_sem,
):
    slots, blocks = nbr_ref.shape
    chunks = blocks // LANES
    fringe = dst_ref.shape[1]
    lane = lax.broadcasted_iota(jnp.int32, (PACK, LANES), 1)
    first = lane < LANES // 2
    masks = [lax.rem(lane + rim + LANES - m * 2 * rim, LANES) < 2 * rim for m in range(slots)]

    def merged(ends, nothing):
        result = nothing
        for m in range(slots):
            both = jnp.where(first, *ends(m))
            if m > 0:
                both = pltpu.roll(both, m * 2 * rim, 1)
            result = jnp.where(masks[m], both, result)
        return result

    def rows(m):
        lower = jnp.broadcast_to(nbr_ref[m : m + 1, :LANES], (PACK, LANES))
        upper = jnp.broadcast_to(nbr_ref[m : m + 1, blocks - LANES :], (PACK, LANES))
        return jnp.where(lower < rim, lower, -LANES), jnp.where(upper >= blocks + rim, upper - blocks, -LANES)

    def tables():
        rimrow_ref[...] = merged(rows, jnp.full((PACK, LANES), -LANES, jnp.int32))
        weight_out[...] = weight_ref[...]
        targets = jnp.broadcast_to(dst_ref[...], (LANES, fringe)).T
        for c in range(chunks):
            table_ref[:, c * LANES : (c + 1) * LANES] = onehot(targets == lane[:1] + c * LANES)

    def rim_coupling(at):
        for u in range(VARS):
            for v in range(VARS):
                span = slice(v * CELLS + at, v * CELLS + at + PACK)
                rimcoup_ref[u, span, :] = merged(
                    lambda m: (coup[0, m, u, span, :], coup[chunks - 1, m, u, span, :]),
                    jnp.zeros((PACK, LANES), jnp.bfloat16),
                )

    local_kernel(
        rim, x_ref, nbr_ref, coup_ref, source_ref, out_ref, terms, near, coup, source, sems, source_sem,
        tables, rim_coupling,
    )


def full_residual(local_ref, inc_ref, lower_ref, upper_ref, table_ref, weight_ref, rimcoup_ref, rimrow_ref):
    rim = lower_ref.shape[0]
    blocks = local_ref.shape[1]
    rims = jnp.concatenate(
        [lower_ref[...], upper_ref[...], jnp.zeros((LANES - 2 * rim, BW), jnp.float32)], axis=0
    ).T
    high, low = split(rims)
    low = pltpu.roll(low.astype(jnp.float32), 2 * rim, 1)
    rims = (high.astype(jnp.float32) + low).astype(jnp.bfloat16)
    sub = lax.broadcasted_iota(jnp.int32, (LANES, LANES), 0)
    row = rimrow_ref[:1]
    reads = onehot((sub == row) | (sub == row + 2 * rim))
    near = jnp.dot(rims, reads, preferred_element_type=jnp.float32)
    edge = []
    for u in range(VARS):
        total = None
        for v in range(VARS):
            span = slice(v * CELLS, (v + 1) * CELLS)
            term = rimcoup_ref[u, span, :].astype(jnp.float32) * near[span]
            total = term if total is None else total + term
        edge.append(total)
    edge = jnp.concatenate(edge, axis=0)
    shift = LANES // 2
    while shift >= 2 * rim:
        edge = edge + pltpu.roll(edge, shift, 1)
        shift //= 2
    lane = lax.broadcasted_iota(jnp.int32, (BW, LANES), 1)
    rest = inc_ref[:, 4]
    rest = jnp.concatenate([rest[:, :, :CELLS], rest[:, :, CELLS:]], axis=1).reshape(-1, CELLS)
    fringe = [inc_ref[:, 0:2].reshape(-1, LANES).T, inc_ref[:, 2:4].reshape(-1, LANES).T, rest.T]
    total = local_ref[...] + pick(jnp.concatenate(fringe, axis=0) * weight_ref[...], table_ref[...])
    lower = total[:, :LANES] + jnp.where(lane < rim, edge, 0.0)
    upper = total[:, blocks - LANES :] + jnp.where(lane >= LANES - rim, edge, 0.0)
    return jnp.concatenate([lower, total[:, LANES : blocks - LANES], upper], axis=1)


def precondition(diag_ref, resid_ref, u, at):
    total = None
    for v in range(VARS):
        span = pl.ds(v * CELLS + at, PACK)
        term = diag_ref[u, span, :].astype(jnp.float32) * resid_ref[span, :]
        total = term if total is None else total + term
    return total


def lane_sums(resid):
    square = jnp.sum(resid * resid, axis=0, keepdims=True)
    return sum(square[:, i : i + LANES] for i in range(0, square.shape[1], LANES))


def advance_kernel(
    local_ref, inc_ref, lower_ref, upper_ref, across_ref, weight_ref, rimcoup_ref, rimrow_ref,
    diag_ref, x_ref, table_ref, select_ref,
    next_ref, norm_ref, out_ref, up_ref, down_ref, resid, diag, diag_sem, rows_ref, sem,
):
    fetch = pltpu.make_async_copy(diag_ref, diag, diag_sem)
    fetch.start()
    resid[...] = full_residual(
        local_ref, inc_ref, lower_ref, upper_ref, across_ref, weight_ref, rimcoup_ref, rimrow_ref
    )
    fetch.wait()
    for u in range(VARS):
        for at in range(0, CELLS, PACK):
            total = None
            for v in range(VARS):
                span = slice(v * CELLS + at, v * CELLS + at + PACK)
                term = diag[u, span].astype(jnp.float32) * resid[span]
                total = term if total is None else total + term
            span = slice(u * CELLS + at, u * CELLS + at + PACK)
            next_ref[span, :] = x_ref[span, :] + STEP_CFL * total
    copy = send_blocks(
        next_ref[...], table_ref[...], select_ref[...], out_ref, up_ref, down_ref, rows_ref, sem
    )
    norm_ref[...] = lane_sums(resid[...])
    copy.wait()


def residual_kernel(
    local_ref, inc_ref, lower_ref, upper_ref, across_ref, weight_ref, rimcoup_ref, rimrow_ref, norm_ref,
    resid_ref, sums_ref,
):
    resid = full_residual(
        local_ref, inc_ref, lower_ref, upper_ref, across_ref, weight_ref, rimcoup_ref, rimrow_ref
    )
    resid_ref[...] = resid
    both = jnp.concatenate([norm_ref[...], lane_sums(resid)], axis=0)
    sums_ref[...] = jnp.broadcast_to(both[None], sums_ref.shape)


def direction_kernel(diag_ref, resid_ref, out_ref, resid_out):
    resid_out[...] = resid_ref[...]

    def cells(part, carry):
        at = pl.multiple_of(part * PACK, PACK)
        for u in range(VARS):
            out_ref[pl.ds(u * CELLS + at, PACK), :] = precondition(diag_ref, resid_ref, u, at)
        return carry

    lax.fori_loop(0, CELLS // PACK, cells, 0)


def finish_kernel(entries, sums_ref, x_ref, update_ref, out_ref):
    sums = jnp.sum(jnp.sum(sums_ref[...], axis=0), axis=1, keepdims=True) / entries + 1e-06
    cfl = STEP_CFL * jnp.sqrt(sums[0:1] / sums[1:2])
    out_ref[...] = x_ref[...] + cfl * update_ref[...]


VMEM = pl.BlockSpec(memory_space=pltpu.VMEM)
SMEM = pl.BlockSpec(memory_space=pltpu.SMEM)


def f32(*shape):
    return jax.ShapeDtypeStruct(shape, jnp.float32)


def bf16(*shape):
    return jax.ShapeDtypeStruct(shape, jnp.bfloat16)


def call(kernel, in_specs, out_shape, flops, moved, **more):
    many = isinstance(out_shape, (list, tuple))
    return pl.pallas_call(
        kernel,
        in_specs=in_specs,
        out_specs=more.pop("out_specs", [VMEM] * len(out_shape) if many else VMEM),
        out_shape=out_shape,
        compiler_params=pltpu.CompilerParams(vmem_limit_bytes=VMEM_LIMIT),
        cost_estimate=pl.CostEstimate(flops=flops, bytes_accessed=moved, transcendentals=0),
        **more,
    )


def shards(
    psi_init, source, coupling, diag_inv, neighbours, seam_perm, fringe_src, fringe_dst, fringe_weight
):
    blocks = psi_init.shape[0]
    slots = neighbours.shape[1]
    rim = seam_perm.shape[1]
    fringe = fringe_src.shape[1]
    peers = lax.axis_size("blk")
    devices = lax.axis_size("body") * peers
    up = [(i, (i + 1) % peers) for i in range(peers)]
    down = [(j, i) for i, j in up]
    here = functools.partial(pltpu.with_memory_space_constraint, memory_space=pltpu.HBM)
    x = here(psi_init.T)
    source_t = here(source.T)
    coup = here(coupling.transpose(1, 2, 3, 0))
    diag = here(diag_inv.transpose(1, 2, 0))
    nbr = here(neighbours.T)
    state = f32(BW, blocks)
    hbm = pl.BlockSpec(memory_space=pltpu.HBM)
    message = (devices, BW * fringe // devices // (rim // 2 * LANES), rim // 2, LANES)
    sent = [f32(*message), f32(rim, BW), f32(rim, BW)]
    rows_scratch = [pltpu.VMEM(message, jnp.float32), pltpu.SemaphoreType.DMA]
    size = 4 * BW * blocks

    donors = call(
        donors_kernel,
        [VMEM, VMEM, SMEM],
        sent + [bf16(blocks, fringe), bf16(2 * LANES, LANES), state],
        4 * BW * blocks * fringe,
        2 * size,
        out_specs=[hbm] + [VMEM] * 5,
        scratch_shapes=rows_scratch,
    )
    chunks = blocks // LANES
    scratch = [
        pltpu.VMEM((2 * BW, blocks + LANES), jnp.bfloat16),
        [pltpu.VMEM((BW, slots * LANES), jnp.float32)] * chunks,
        pltpu.VMEM((chunks, slots, VARS, BW, LANES), jnp.bfloat16),
        pltpu.VMEM((BW, blocks), jnp.float32),
        pltpu.SemaphoreType.DMA((chunks,)),
        pltpu.SemaphoreType.DMA,
    ]
    local_more = dict(
        flops=4 * BW * 2 * LANES * slots * blocks,
        moved=coup.size * 2 + 4 * size,
        scratch_shapes=scratch,
    )
    first_local = call(
        functools.partial(first_local_kernel, rim),
        [VMEM, VMEM, hbm, hbm, VMEM, VMEM],
        [
            state,
            bf16(VARS, BW, LANES),
            jax.ShapeDtypeStruct((PACK, LANES), jnp.int32),
            bf16(fringe, blocks),
            f32(1, fringe),
        ],
        **local_more,
    )
    local = call(functools.partial(local_kernel, rim), [VMEM, VMEM, hbm, hbm], state, **local_more)
    advance = call(
        advance_kernel,
        [VMEM] * 8 + [hbm] + [VMEM] * 3,
        [state, f32(1, LANES)] + sent,
        8 * BW * blocks * fringe,
        diag.size * 2 + 4 * size,
        out_specs=[VMEM, VMEM, hbm, VMEM, VMEM],
        scratch_shapes=[
            pltpu.VMEM((BW, blocks), jnp.float32),
            pltpu.VMEM((VARS, BW, blocks), jnp.bfloat16),
            pltpu.SemaphoreType.DMA,
        ]
        + rows_scratch,
    )
    residual = call(
        residual_kernel,
        [VMEM] * 9,
        [state, f32(devices, 2, LANES)],
        4 * BW * blocks * fringe,
        3 * size,
    )
    direction = call(
        direction_kernel, [VMEM] * 2, [state, state], diag.size * 2, diag.size * 2 + 2 * size
    )
    finish = call(
        functools.partial(finish_kernel, float(blocks * devices * BW)),
        [VMEM] * 3,
        state,
        2 * BW * blocks,
        3 * size,
    )

    def exchange(rows, to_up, to_down):
        rows = lax.all_to_all(rows, ("body", "blk"), split_axis=0, concat_axis=0, tiled=True)
        return rows, lax.ppermute(to_up, "blk", up), lax.ppermute(to_down, "blk", down)

    *out, table, select, x_here = donors(x, here(fringe_src), here(seam_perm))
    arrived = exchange(*out)
    part, rimcoup, rimrow, across, weight = first_local(
        x_here, nbr, coup, source_t, here(fringe_dst), here(fringe_weight)
    )
    across = (across, weight, rimcoup, rimrow)
    x, norm, *out = advance(part, *arrived, *across, diag, x_here, table, select)
    arrived = exchange(*out)
    part = local(x, nbr, coup, source_t)
    resid, sums = residual(part, *arrived, *across, norm)
    sums = lax.all_to_all(sums, ("body", "blk"), split_axis=0, concat_axis=0, tiled=True)
    update, resid = direction(diag, resid)
    x = finish(sums, x, update)
    return (x.T, resid.T)


def solution(mesh):
    return jax.shard_map(
        shards,
        mesh=mesh,
        in_specs=(
            P(("body", "blk"), None),
            P(("body", "blk"), None),
            P(("body", "blk"), None, None, None),
            P(("body", "blk"), None, None),
            P(("body", "blk"), None),
            P("body", None),
            P(("body", "blk"), None),
            P(("body", "blk"), None),
            P(("body", "blk"), None),
        ),
        out_specs=(P(("body", "blk"), None), P(("body", "blk"), None)),
        check_vma=False,
    )
```

```python
import functools
import math

import jax
import jax.numpy as jnp
from jax import lax
from jax.experimental import pallas as pl
from jax.experimental.pallas import tpu as pltpu
from jax.sharding import PartitionSpec as P

CELLS = 64
VARS = 5
BW = 320
STEP_CFL = 0.5
LANES = 128
PACK = 16
VMEM_LIMIT = 32 * 1024 * 1024


def split(x):
    high = x.astype(jnp.bfloat16)
    return high, (x - high.astype(jnp.float32)).astype(jnp.bfloat16)


def onehot(mask):
    return jnp.where(mask, 1.0, 0.0).astype(jnp.bfloat16)


def pick(x, table):
    both = jnp.dot(jnp.concatenate(split(x), axis=0), table, preferred_element_type=jnp.float32)
    return both[: x.shape[0]] + both[x.shape[0] :]


def send_blocks(x, src, select, out_ref, up_ref, down_ref, rows_ref, sem):
    rim = up_ref.shape[0]
    half = rows_ref.shape[2]
    table = onehot(lax.broadcasted_iota(jnp.int32, (x.shape[1], src.shape[1]), 0) == src)
    rows = pick(x, table).T.reshape(rows_ref.shape[0], 2 * half, BW)
    for h in range(2):
        for tile in range(2):
            rows_ref[:, 2 * tile + h] = rows[:, h * half : (h + 1) * half, tile * LANES : (tile + 1) * LANES]
    rest = rows[:, :, 2 * LANES :]
    rows_ref[:, 4] = jnp.concatenate([rest[:, :half], rest[:, half:]], axis=2)
    copy = pltpu.make_async_copy(rows_ref, out_ref, sem)
    copy.start()
    index = lax.axis_index("blk")
    at_last = index == lax.axis_size("blk") - 1
    at_first = index == 0
    first = lax.broadcasted_iota(jnp.int32, (BW, LANES), 1) < LANES // 2
    ends = split(jnp.where(first, x[:, :LANES], x[:, x.shape[1] - LANES :]))
    rims = jnp.dot(jnp.concatenate(ends, axis=1), select, preferred_element_type=jnp.float32)
    lane = lax.broadcasted_iota(jnp.int32, (1, LANES), 1)
    turn_up = (lane < rim) & at_last
    turn_down = (lane >= rim) & at_first
    angle = 2.0 * math.pi / 3.0
    cosine = jnp.where(turn_up | turn_down, math.cos(angle), 1.0)
    sine = jnp.where(turn_up, math.sin(angle), jnp.where(turn_down, -math.sin(angle), 0.0))
    first = rims[2 * CELLS : 3 * CELLS]
    second = rims[3 * CELLS : 4 * CELLS]
    rims = jnp.concatenate(
        [
            rims[: 2 * CELLS],
            cosine * first - sine * second,
            sine * first + cosine * second,
            rims[4 * CELLS :],
        ],
        axis=0,
    ).T
    up_ref[...] = rims[:rim]
    down_ref[...] = rims[rim : 2 * rim]
    return copy


def donors_kernel(
    x_ref, src_ref, perm_ref,
    out_ref, up_ref, down_ref, src_out, select_ref, x_out, rows_ref, sem,
):
    rim = up_ref.shape[0]
    index = lax.axis_index("blk")
    at_last = index == lax.axis_size("blk") - 1
    at_first = index == 0
    sub = lax.broadcasted_iota(jnp.int32, (LANES, LANES), 0)
    lane = lax.broadcasted_iota(jnp.int32, (LANES, LANES), 1)
    wanted = lane[:1]
    target = sub[:, :1]
    for j in range(rim):
        partner = perm_ref[0, j]
        wanted = jnp.where((lane[:1] == j) & at_last, partner, wanted)
        target = jnp.where((sub[:, :1] == j) & at_first, partner, target)
    to_up = (sub == wanted + (LANES - rim)) & (lane < rim)
    to_down = (target + rim == lane) & (sub < rim)
    select = onehot(to_up | to_down)
    select = jnp.concatenate([select, select], axis=0)
    copy = send_blocks(
        x_ref[...], src_ref[...], select, out_ref, up_ref, down_ref, rows_ref, sem
    )
    src_out[...] = src_ref[...]
    select_ref[...] = select
    x_out[...] = x_ref[...]
    copy.wait()


def local_kernel(
    rim, x_ref, nbr_ref, coup_ref, source_ref, out_ref, terms, near, coup, source, sems, source_sem,
    at_start=None, tables=None, with_ends=None, after_part=None, after_chunk=None,
):
    slots, blocks = nbr_ref.shape
    chunks = blocks // LANES
    spans = [slice(c * LANES, (c + 1) * LANES) for c in range(chunks)]
    order = [0, chunks - 1, *range(1, chunks - 1)]
    source_copy = pltpu.make_async_copy(source_ref, source, source_sem)
    copies = {}
    for c in order:
        copies[c] = pltpu.make_async_copy(coup_ref.at[:, :, :, spans[c]], coup.at[c], sems.at[c])
        copies[c].start()
        if c == order[0]:
            source_copy.start()
            if at_start is not None:
                at_start()
    lane = lax.broadcasted_iota(jnp.int32, (BW, LANES), 1)
    moved = pltpu.roll(x_ref[...], rim, 1)
    head = jnp.where(lane < rim, 0.0, moved[:, :LANES])
    tail = jnp.where(lane < rim, moved[:, :LANES], 0.0)
    terms[:BW], terms[BW:] = split(jnp.concatenate([head, moved[:, LANES:], tail], axis=1))
    rows = lax.broadcasted_iota(jnp.int32, (2 * LANES, LANES), 0)

    pairs = range(0, slots, 2)

    def gather(c, m):
        window = slice(c * LANES, (c + 2) * LANES)
        table = jnp.concatenate(
            [onehot(rows == nbr_ref[i : i + 1, spans[c]] - c * LANES) for i in (m, m + 1)], axis=1
        )
        both = jnp.dot(terms[:, window], table, preferred_element_type=jnp.float32)
        near[c][:, m * LANES : (m + 2) * LANES] = both[:BW] + both[BW:]

    for m in pairs:
        gather(order[0], m)
    if tables is not None:
        tables()
    for step, c in enumerate(order):
        copies[c].wait()
        if step == 0:
            source_copy.wait()
        ahead = list(pairs) if step + 1 < chunks else []
        for at in range(0, CELLS, PACK):
            if ahead:
                gather(order[step + 1], ahead.pop(0))
            if with_ends is not None and step in (1, 2) and (at < CELLS // 2) == (step == 1):
                with_ends(at)
            total = [None] * VARS
            for m in range(slots):
                for v in range(VARS):
                    span = slice(v * CELLS + at, v * CELLS + at + PACK)
                    value = near[c][span, m * LANES : (m + 1) * LANES]
                    for u in range(VARS):
                        term = coup[c, m, u, span, :].astype(jnp.float32) * value
                        total[u] = term if total[u] is None else total[u] + term
            for u in range(VARS):
                span = slice(u * CELLS + at, u * CELLS + at + PACK)
                total[u] = source[span, spans[c]] - x_ref[span, spans[c]] + total[u]
                out_ref[span, spans[c]] = total[u]
            if after_part is not None:
                after_part(at, spans[c], total)
        if after_chunk is not None:
            after_chunk(c, spans[c])


def first_local_kernel(
    rim, x_ref, nbr_ref, coup_ref, source_ref, diag_ref, dst_ref, weight_ref,
    base_ref, local_ref, rimcoup_ref, rimrow_ref, table_ref, weight_out, diag_out,
    terms, near, coup, source, sems, source_sem, local, local_sems, diag_sem,
):
    slots, blocks = nbr_ref.shape
    chunks = blocks // LANES
    fringe = dst_ref.shape[1]
    lane = lax.broadcasted_iota(jnp.int32, (PACK, LANES), 1)
    first = lane < LANES // 2
    masks = [lax.rem(lane + rim + LANES - m * 2 * rim, LANES) < 2 * rim for m in range(slots)]

    def merged(ends, nothing):
        result = nothing
        for m in range(slots):
            both = jnp.where(first, *ends(m))
            if m > 0:
                both = pltpu.roll(both, m * 2 * rim, 1)
            result = jnp.where(masks[m], both, result)
        return result

    def rows(m):
        lower = jnp.broadcast_to(nbr_ref[m : m + 1, :LANES], (PACK, LANES))
        upper = jnp.broadcast_to(nbr_ref[m : m + 1, blocks - LANES :], (PACK, LANES))
        return jnp.where(lower < rim, lower, -LANES), jnp.where(upper >= blocks + rim, upper - blocks, -LANES)

    def tables():
        rimrow_ref[...] = merged(rows, jnp.full((PACK, LANES), -LANES, jnp.int32))
        weight_out[...] = weight_ref[...]
        targets = jnp.broadcast_to(dst_ref[...], (LANES, fringe)).T
        for c in range(chunks):
            table_ref[:, c * LANES : (c + 1) * LANES] = onehot(targets == lane[:1] + c * LANES)

    def rim_coupling(at):
        for u in range(VARS):
            for v in range(VARS):
                span = slice(v * CELLS + at, v * CELLS + at + PACK)
                rimcoup_ref[u, span, :] = merged(
                    lambda m: (coup[0, m, u, span, :], coup[chunks - 1, m, u, span, :]),
                    jnp.zeros((PACK, LANES), jnp.bfloat16),
                )

    diag_copy = pltpu.make_async_copy(diag_ref, diag_out, diag_sem)
    waited = []

    def step(at, lanes, resid):
        if not waited:
            diag_copy.wait()
            waited.append(True)
        for u in range(VARS):
            total = None
            for v in range(VARS):
                span = slice(v * CELLS + at, v * CELLS + at + PACK)
                term = diag_out[u, span, lanes].astype(jnp.float32) * resid[v]
                total = term if total is None else total + term
            span = slice(u * CELLS + at, u * CELLS + at + PACK)
            base_ref[span, lanes] = x_ref[span, lanes] + STEP_CFL * total

    stores = []

    def store(c, lanes):
        copy = pltpu.make_async_copy(local.at[:, lanes], local_ref.at[:, lanes], local_sems.at[c])
        copy.start()
        stores.append(copy)

    local_kernel(
        rim, x_ref, nbr_ref, coup_ref, source_ref, local, terms, near, coup, source, sems, source_sem,
        diag_copy.start, tables, rim_coupling, step, store,
    )
    for copy in stores:
        copy.wait()


def arrived(inc_ref, lower_ref, upper_ref, table_ref, weight_ref, rimcoup_ref, rimrow_ref):
    rim = lower_ref.shape[0]
    blocks = table_ref.shape[1]
    rims = jnp.concatenate(
        [lower_ref[...], upper_ref[...], jnp.zeros((LANES - 2 * rim, BW), jnp.float32)], axis=0
    ).T
    high, low = split(rims)
    low = pltpu.roll(low.astype(jnp.float32), 2 * rim, 1)
    rims = (high.astype(jnp.float32) + low).astype(jnp.bfloat16)
    sub = lax.broadcasted_iota(jnp.int32, (LANES, LANES), 0)
    row = rimrow_ref[:1]
    reads = onehot((sub == row) | (sub == row + 2 * rim))
    near = jnp.dot(rims, reads, preferred_element_type=jnp.float32)
    edge = []
    for u in range(VARS):
        total = None
        for v in range(VARS):
            span = slice(v * CELLS, (v + 1) * CELLS)
            term = rimcoup_ref[u, span, :].astype(jnp.float32) * near[span]
            total = term if total is None else total + term
        edge.append(total)
    edge = jnp.concatenate(edge, axis=0)
    shift = LANES // 2
    while shift >= 2 * rim:
        edge = edge + pltpu.roll(edge, shift, 1)
        shift //= 2
    lane = lax.broadcasted_iota(jnp.int32, (BW, LANES), 1)
    rest = inc_ref[:, 4]
    rest = jnp.concatenate([rest[:, :, :CELLS], rest[:, :, CELLS:]], axis=1).reshape(-1, CELLS)
    fringe = [inc_ref[:, 0:2].reshape(-1, LANES).T, inc_ref[:, 2:4].reshape(-1, LANES).T, rest.T]
    total = pick(jnp.concatenate(fringe, axis=0) * weight_ref[...], table_ref[...])
    lower = total[:, :LANES] + jnp.where(lane < rim, edge, 0.0)
    upper = total[:, blocks - LANES :] + jnp.where(lane >= LANES - rim, edge, 0.0)
    return jnp.concatenate([lower, total[:, LANES : blocks - LANES], upper], axis=1)


def precondition(diag_ref, resid_ref, u, at):
    total = None
    for v in range(VARS):
        span = pl.ds(v * CELLS + at, PACK)
        term = diag_ref[u, span, :].astype(jnp.float32) * resid_ref[span, :]
        total = term if total is None else total + term
    return total


def lane_sums(resid):
    square = jnp.sum(resid * resid, axis=0, keepdims=True)
    return sum(square[:, i : i + LANES] for i in range(0, square.shape[1], LANES))


def advance_kernel(
    base_ref, inc_ref, lower_ref, upper_ref, across_ref, weight_ref, rimcoup_ref, rimrow_ref,
    diag_ref, local_ref, src_ref, select_ref,
    next_ref, norm_ref, out_ref, up_ref, down_ref, came, local, local_sem, rows_ref, sem,
):
    fetch = pltpu.make_async_copy(local_ref, local, local_sem)
    fetch.start()
    came[...] = arrived(
        inc_ref, lower_ref, upper_ref, across_ref, weight_ref, rimcoup_ref, rimrow_ref
    )
    for at in range(0, CELLS, PACK):
        for u in range(VARS):
            total = None
            for v in range(VARS):
                span = slice(v * CELLS + at, v * CELLS + at + PACK)
                term = diag_ref[u, span].astype(jnp.float32) * came[span]
                total = term if total is None else total + term
            span = slice(u * CELLS + at, u * CELLS + at + PACK)
            next_ref[span, :] = base_ref[span, :] + STEP_CFL * total
    copy = send_blocks(
        next_ref[...], src_ref[...], select_ref[...], out_ref, up_ref, down_ref, rows_ref, sem
    )
    fetch.wait()
    norm_ref[...] = lane_sums(local[...] + came[...])
    copy.wait()


def residual_kernel(
    local_ref, inc_ref, lower_ref, upper_ref, across_ref, weight_ref, rimcoup_ref, rimrow_ref, norm_ref,
    resid_ref, sums_ref,
):
    resid = local_ref[...] + arrived(
        inc_ref, lower_ref, upper_ref, across_ref, weight_ref, rimcoup_ref, rimrow_ref
    )
    resid_ref[...] = resid
    both = jnp.concatenate([norm_ref[...], lane_sums(resid)], axis=0)
    sums_ref[...] = jnp.broadcast_to(both[None], sums_ref.shape)


def direction_kernel(diag_ref, resid_ref, out_ref, resid_out):
    resid_out[...] = resid_ref[...]

    def cells(part, carry):
        at = pl.multiple_of(part * PACK, PACK)
        for u in range(VARS):
            out_ref[pl.ds(u * CELLS + at, PACK), :] = precondition(diag_ref, resid_ref, u, at)
        return carry

    lax.fori_loop(0, CELLS // PACK, cells, 0)


def finish_kernel(entries, sums_ref, x_ref, update_ref, out_ref):
    sums = jnp.sum(jnp.sum(sums_ref[...], axis=0), axis=1, keepdims=True) / entries + 1e-06
    cfl = STEP_CFL * jnp.sqrt(sums[0:1] / sums[1:2])
    out_ref[...] = x_ref[...] + cfl * update_ref[...]


VMEM = pl.BlockSpec(memory_space=pltpu.VMEM)
SMEM = pl.BlockSpec(memory_space=pltpu.SMEM)


def f32(*shape):
    return jax.ShapeDtypeStruct(shape, jnp.float32)


def i32(*shape):
    return jax.ShapeDtypeStruct(shape, jnp.int32)


def bf16(*shape):
    return jax.ShapeDtypeStruct(shape, jnp.bfloat16)


def call(kernel, in_specs, out_shape, flops, moved, **more):
    many = isinstance(out_shape, (list, tuple))
    return pl.pallas_call(
        kernel,
        in_specs=in_specs,
        out_specs=more.pop("out_specs", [VMEM] * len(out_shape) if many else VMEM),
        out_shape=out_shape,
        compiler_params=pltpu.CompilerParams(vmem_limit_bytes=VMEM_LIMIT),
        cost_estimate=pl.CostEstimate(flops=flops, bytes_accessed=moved, transcendentals=0),
        **more,
    )


def shards(
    psi_init, source, coupling, diag_inv, neighbours, seam_perm, fringe_src, fringe_dst, fringe_weight
):
    blocks = psi_init.shape[0]
    slots = neighbours.shape[1]
    rim = seam_perm.shape[1]
    fringe = fringe_src.shape[1]
    peers = lax.axis_size("blk")
    devices = lax.axis_size("body") * peers
    up = [(i, (i + 1) % peers) for i in range(peers)]
    down = [(j, i) for i, j in up]
    here = functools.partial(pltpu.with_memory_space_constraint, memory_space=pltpu.HBM)
    x = here(psi_init.T)
    source_t = here(source.T)
    coup = here(coupling.transpose(1, 2, 3, 0))
    diag = here(diag_inv.transpose(1, 2, 0))
    nbr = here(neighbours.T)
    state = f32(BW, blocks)
    hbm = pl.BlockSpec(memory_space=pltpu.HBM)
    message = (devices, BW * fringe // devices // (rim // 2 * LANES), rim // 2, LANES)
    sent = [pltpu.HBM(message, jnp.float32), f32(rim, BW), f32(rim, BW)]
    rows_scratch = [pltpu.VMEM(message, jnp.float32), pltpu.SemaphoreType.DMA]
    size = 4 * BW * blocks

    donors = call(
        donors_kernel,
        [VMEM, VMEM, SMEM],
        sent + [i32(1, fringe), bf16(2 * LANES, LANES), state],
        4 * BW * blocks * fringe,
        2 * size,
        out_specs=[hbm] + [VMEM] * 5,
        scratch_shapes=rows_scratch,
    )
    chunks = blocks // LANES
    scratch = [
        pltpu.VMEM((2 * BW, blocks + LANES), jnp.bfloat16),
        [pltpu.VMEM((BW, slots * LANES), jnp.float32)] * chunks,
        pltpu.VMEM((chunks, slots, VARS, BW, LANES), jnp.bfloat16),
        pltpu.VMEM((BW, blocks), jnp.float32),
        pltpu.SemaphoreType.DMA((chunks,)),
        pltpu.SemaphoreType.DMA,
    ]
    local_more = dict(
        flops=4 * BW * 2 * LANES * slots * blocks,
        moved=coup.size * 2 + 4 * size,
        scratch_shapes=scratch,
    )
    first_local = call(
        functools.partial(first_local_kernel, rim),
        [VMEM, VMEM, hbm, hbm, hbm, VMEM, VMEM],
        [
            state,
            pltpu.HBM((BW, blocks), jnp.float32),
            bf16(VARS, BW, LANES),
            i32(PACK, LANES),
            bf16(fringe, blocks),
            f32(1, fringe),
            bf16(VARS, BW, blocks),
        ],
        out_specs=[VMEM, hbm] + [VMEM] * 5,
        input_output_aliases={0: 0},
        **dict(
            local_more,
            scratch_shapes=scratch
            + [
                pltpu.VMEM((BW, blocks), jnp.float32),
                pltpu.SemaphoreType.DMA((chunks,)),
                pltpu.SemaphoreType.DMA,
            ],
        ),
    )
    local = call(functools.partial(local_kernel, rim), [VMEM, VMEM, hbm, hbm], state, **local_more)
    advance = call(
        advance_kernel,
        [VMEM] * 9 + [hbm] + [VMEM] * 2,
        [state, f32(1, LANES)] + sent,
        8 * BW * blocks * fringe,
        diag.size * 2 + 4 * size,
        out_specs=[VMEM, VMEM, hbm, VMEM, VMEM],
        input_output_aliases={0: 0},
        scratch_shapes=[
            pltpu.VMEM((BW, blocks), jnp.float32),
            pltpu.VMEM((BW, blocks), jnp.float32),
            pltpu.SemaphoreType.DMA,
        ]
        + rows_scratch,
    )
    residual = call(
        residual_kernel,
        [VMEM] * 9,
        [state, f32(devices, 2, LANES)],
        4 * BW * blocks * fringe,
        3 * size,
    )
    direction = call(
        direction_kernel, [VMEM] * 2, [state, state], diag.size * 2, diag.size * 2 + 2 * size
    )
    finish = call(
        functools.partial(finish_kernel, float(blocks * devices * BW)),
        [VMEM] * 3,
        state,
        2 * BW * blocks,
        3 * size,
    )

    def exchange(rows, to_up, to_down):
        rows = lax.all_to_all(rows, ("body", "blk"), split_axis=0, concat_axis=0, tiled=True)
        return rows, lax.ppermute(to_up, "blk", up), lax.ppermute(to_down, "blk", down)

    *out, src, select, x_here = donors(x, here(fringe_src), here(seam_perm))
    arrivals = exchange(*out)
    base, part, rimcoup, rimrow, across, weight, diag_here = first_local(
        x_here, nbr, coup, source_t, diag, here(fringe_dst), here(fringe_weight)
    )
    across = (across, weight, rimcoup, rimrow)
    x, norm, *out = advance(base, *arrivals, *across, diag_here, here(part), src, select)
    arrivals = exchange(*out)
    part = local(x, nbr, coup, source_t)
    resid, sums = residual(part, *arrivals, *across, norm)
    sums = lax.all_to_all(sums, ("body", "blk"), split_axis=0, concat_axis=0, tiled=True)
    update, resid = direction(diag, resid)
    x = finish(sums, x, update)
    return (x.T, resid.T)


def solution(mesh):
    return jax.shard_map(
        shards,
        mesh=mesh,
        in_specs=(
            P(("body", "blk"), None),
            P(("body", "blk"), None),
            P(("body", "blk"), None, None, None),
            P(("body", "blk"), None, None),
            P(("body", "blk"), None),
            P("body", None),
            P(("body", "blk"), None),
            P(("body", "blk"), None),
            P(("body", "blk"), None),
        ),
        out_specs=(P(("body", "blk"), None), P(("body", "blk"), None)),
        check_vma=False,
    )
```

```python
import functools
import math

import jax
import jax.numpy as jnp
from jax import lax
from jax.experimental import pallas as pl
from jax.experimental.pallas import tpu as pltpu
from jax.sharding import PartitionSpec as P

CELLS = 64
VARS = 5
BW = 320
STEP_CFL = 0.5
LANES = 128
PACK = 16
VMEM_LIMIT = 32 * 1024 * 1024


def split(x):
    high = x.astype(jnp.bfloat16)
    return high, (x - high.astype(jnp.float32)).astype(jnp.bfloat16)


def onehot(mask):
    return jnp.where(mask, 1.0, 0.0).astype(jnp.bfloat16)


def pick(x, table):
    both = jnp.dot(jnp.concatenate(split(x), axis=0), table, preferred_element_type=jnp.float32)
    return both[: x.shape[0]] + both[x.shape[0] :]


def send_blocks(x_ref, groups, table, select, out_ref, up_ref, down_ref, rows_ref, sem):
    rim = up_ref.shape[0]
    half = rows_ref.shape[2]
    devices = rows_ref.shape[0]
    for tile in range(2):
        rows = pick(groups(2 * tile, 2 * tile + 2), table).T.reshape(devices, 2 * half, LANES)
        rows_ref[:, 2 * tile] = rows[:, :half]
        rows_ref[:, 2 * tile + 1] = rows[:, half:]
    rows = pick(groups(4, 5), table).T.reshape(devices, 2 * half, CELLS)
    rows_ref[:, 4] = jnp.concatenate([rows[:, :half], rows[:, half:]], axis=2)
    copy = pltpu.make_async_copy(rows_ref, out_ref, sem)
    copy.start()
    index = lax.axis_index("blk")
    at_last = index == lax.axis_size("blk") - 1
    at_first = index == 0
    first = lax.broadcasted_iota(jnp.int32, (BW, LANES), 1) < LANES // 2
    ends = split(jnp.where(first, x_ref[:, :LANES], x_ref[:, x_ref.shape[1] - LANES :]))
    rims = jnp.dot(jnp.concatenate(ends, axis=1), select, preferred_element_type=jnp.float32)
    lane = lax.broadcasted_iota(jnp.int32, (1, LANES), 1)
    turn_up = (lane < rim) & at_last
    turn_down = (lane >= rim) & at_first
    angle = 2.0 * math.pi / 3.0
    cosine = jnp.where(turn_up | turn_down, math.cos(angle), 1.0)
    sine = jnp.where(turn_up, math.sin(angle), jnp.where(turn_down, -math.sin(angle), 0.0))
    first = rims[2 * CELLS : 3 * CELLS]
    second = rims[3 * CELLS : 4 * CELLS]
    rims = jnp.concatenate(
        [
            rims[: 2 * CELLS],
            cosine * first - sine * second,
            sine * first + cosine * second,
            rims[4 * CELLS :],
        ],
        axis=0,
    ).T
    up_ref[...] = rims[:rim]
    down_ref[...] = rims[rim : 2 * rim]
    return copy


def donors_kernel(
    x_ref, src_ref, perm_ref,
    out_ref, up_ref, down_ref, table_ref, select_ref, x_out, rows_ref, sem,
):
    rim = up_ref.shape[0]
    index = lax.axis_index("blk")
    at_last = index == lax.axis_size("blk") - 1
    at_first = index == 0
    sub = lax.broadcasted_iota(jnp.int32, (LANES, LANES), 0)
    lane = lax.broadcasted_iota(jnp.int32, (LANES, LANES), 1)
    wanted = lane[:1]
    target = sub[:, :1]
    for j in range(rim):
        partner = perm_ref[0, j]
        wanted = jnp.where((lane[:1] == j) & at_last, partner, wanted)
        target = jnp.where((sub[:, :1] == j) & at_first, partner, target)
    to_up = (sub == wanted + (LANES - rim)) & (lane < rim)
    to_down = (target + rim == lane) & (sub < rim)
    select = onehot(to_up | to_down)
    select = jnp.concatenate([select, select], axis=0)
    rows = lax.broadcasted_iota(jnp.int32, table_ref.shape, 0)
    table = onehot(rows == src_ref[...])
    copy = send_blocks(
        x_ref, lambda a, b: x_ref[a * CELLS : b * CELLS], table, select,
        out_ref, up_ref, down_ref, rows_ref, sem,
    )
    table_ref[...] = table
    select_ref[...] = select
    x_out[...] = x_ref[...]
    copy.wait()


def local_kernel(
    rim, x_ref, nbr_ref, coup_ref, source_ref, out_ref, terms, near, coup, source, sems, source_sem,
    at_start=None, with_ends=None,
):
    slots, blocks = nbr_ref.shape
    chunks = blocks // LANES
    spans = [slice(c * LANES, (c + 1) * LANES) for c in range(chunks)]
    order = [0, chunks - 1, *range(1, chunks - 1)]
    source_copy = pltpu.make_async_copy(source_ref, source, source_sem)
    copies = {}
    for c in order:
        copies[c] = pltpu.make_async_copy(coup_ref.at[:, :, :, spans[c]], coup.at[c], sems.at[c])
        copies[c].start()
        if c == order[0]:
            source_copy.start()
    lane = lax.broadcasted_iota(jnp.int32, (BW, LANES), 1)
    moved = pltpu.roll(x_ref[...], rim, 1)
    head = jnp.where(lane < rim, 0.0, moved[:, :LANES])
    tail = jnp.where(lane < rim, moved[:, :LANES], 0.0)
    terms[:BW], terms[BW:] = split(jnp.concatenate([head, moved[:, LANES:], tail], axis=1))
    rows = lax.broadcasted_iota(jnp.int32, (2 * LANES, LANES), 0)

    pairs = range(0, slots, 2)

    def gather(c, m):
        window = slice(c * LANES, (c + 2) * LANES)
        table = jnp.concatenate(
            [onehot(rows == nbr_ref[i : i + 1, spans[c]] - c * LANES) for i in (m, m + 1)], axis=1
        )
        both = jnp.dot(terms[:, window], table, preferred_element_type=jnp.float32)
        near[c][:, m * LANES : (m + 2) * LANES] = both[:BW] + both[BW:]

    for m in pairs:
        gather(order[0], m)
    if at_start is not None:
        at_start()
    for step, c in enumerate(order):
        copies[c].wait()
        if step == 0:
            source_copy.wait()
        ahead = list(pairs) if step + 1 < chunks else []
        for at in range(0, CELLS, PACK):
            if ahead:
                gather(order[step + 1], ahead.pop(0))
            if with_ends is not None and step in (1, 2) and (at < CELLS // 2) == (step == 1):
                with_ends(at)
            total = [None] * VARS
            for m in range(slots):
                for v in range(VARS):
                    span = slice(v * CELLS + at, v * CELLS + at + PACK)
                    value = near[c][span, m * LANES : (m + 1) * LANES]
                    for u in range(VARS):
                        term = coup[c, m, u, span, :].astype(jnp.float32) * value
                        total[u] = term if total[u] is None else total[u] + term
            for u in range(VARS):
                span = slice(u * CELLS + at, u * CELLS + at + PACK)
                out_ref[span, spans[c]] = source[span, spans[c]] - x_ref[span, spans[c]] + total[u]


def first_local_kernel(
    rim, x_ref, nbr_ref, coup_ref, source_ref, dst_ref, weight_ref,
    out_ref, rimcoup_ref, rimrow_ref, table_ref, weight_out,
    terms, near, coup, source, sems, source_sem,
):
    slots, blocks = nbr_ref.shape
    chunks = blocks // LANES
    fringe = dst_ref.shape[1]
    lane = lax.broadcasted_iota(jnp.int32, (PACK, LANES), 1)
    first = lane < LANES // 2
    masks = [lax.rem(lane + rim + LANES - m * 2 * rim, LANES) < 2 * rim for m in range(slots)]

    def merged(ends, nothing):
        result = nothing
        for m in range(slots):
            both = jnp.where(first, *ends(m))
            if m > 0:
                both = pltpu.roll(both, m * 2 * rim, 1)
            result = jnp.where(masks[m], both, result)
        return result

    def rows(m):
        lower = jnp.broadcast_to(nbr_ref[m : m + 1, :LANES], (PACK, LANES))
        upper = jnp.broadcast_to(nbr_ref[m : m + 1, blocks - LANES :], (PACK, LANES))
        return jnp.where(lower < rim, lower, -LANES), jnp.where(upper >= blocks + rim, upper - blocks, -LANES)

    def tables():
        rimrow_ref[...] = merged(rows, jnp.full((PACK, LANES), -LANES, jnp.int32))
        weight_out[...] = weight_ref[...]
        targets = jnp.broadcast_to(dst_ref[...], (LANES, fringe)).T
        for c in range(chunks):
            table_ref[:, c * LANES : (c + 1) * LANES] = onehot(targets == lane[:1] + c * LANES)

    def rim_coupling(at):
        for u in range(VARS):
            for v in range(VARS):
                span = slice(v * CELLS + at, v * CELLS + at + PACK)
                rimcoup_ref[u, span, :] = merged(
                    lambda m: (coup[0, m, u, span, :], coup[chunks - 1, m, u, span, :]),
                    jnp.zeros((PACK, LANES), jnp.bfloat16),
                )

    local_kernel(
        rim, x_ref, nbr_ref, coup_ref, source_ref, out_ref, terms, near, coup, source, sems, source_sem,
        tables, rim_coupling,
    )


def full_residual(local_ref, inc_ref, lower_ref, upper_ref, table_ref, weight_ref, rimcoup_ref, rimrow_ref):
    rim = lower_ref.shape[0]
    blocks = local_ref.shape[1]
    rims = jnp.concatenate(
        [lower_ref[...], upper_ref[...], jnp.zeros((LANES - 2 * rim, BW), jnp.float32)], axis=0
    ).T
    high, low = split(rims)
    low = pltpu.roll(low.astype(jnp.float32), 2 * rim, 1)
    rims = (high.astype(jnp.float32) + low).astype(jnp.bfloat16)
    sub = lax.broadcasted_iota(jnp.int32, (LANES, LANES), 0)
    row = rimrow_ref[:1]
    reads = onehot((sub == row) | (sub == row + 2 * rim))
    near = jnp.dot(rims, reads, preferred_element_type=jnp.float32)
    edge = []
    for u in range(VARS):
        total = None
        for v in range(VARS):
            span = slice(v * CELLS, (v + 1) * CELLS)
            term = rimcoup_ref[u, span, :].astype(jnp.float32) * near[span]
            total = term if total is None else total + term
        edge.append(total)
    edge = jnp.concatenate(edge, axis=0)
    shift = LANES // 2
    while shift >= 2 * rim:
        edge = edge + pltpu.roll(edge, shift, 1)
        shift //= 2
    lane = lax.broadcasted_iota(jnp.int32, (BW, LANES), 1)
    rest = inc_ref[:, 4]
    rest = jnp.concatenate([rest[:, :, :CELLS], rest[:, :, CELLS:]], axis=1).reshape(-1, CELLS)
    fringe = [inc_ref[:, 0:2].reshape(-1, LANES).T, inc_ref[:, 2:4].reshape(-1, LANES).T, rest.T]
    total = local_ref[...] + pick(jnp.concatenate(fringe, axis=0) * weight_ref[...], table_ref[...])
    lower = total[:, :LANES] + jnp.where(lane < rim, edge, 0.0)
    upper = total[:, blocks - LANES :] + jnp.where(lane >= LANES - rim, edge, 0.0)
    return jnp.concatenate([lower, total[:, LANES : blocks - LANES], upper], axis=1)


def precondition(diag_ref, resid_ref, u, at):
    total = None
    for v in range(VARS):
        span = pl.ds(v * CELLS + at, PACK)
        term = diag_ref[u, span, :].astype(jnp.float32) * resid_ref[span, :]
        total = term if total is None else total + term
    return total


def lane_sums(resid):
    square = jnp.sum(resid * resid, axis=0, keepdims=True)
    return sum(square[:, i : i + LANES] for i in range(0, square.shape[1], LANES))


def advance_kernel(
    local_ref, inc_ref, lower_ref, upper_ref, across_ref, weight_ref, rimcoup_ref, rimrow_ref,
    diag_ref, x_ref, table_ref, select_ref,
    next_ref, norm_ref, out_ref, up_ref, down_ref, resid, diag, diag_sem, rows_ref, sem,
):
    fetch = pltpu.make_async_copy(diag_ref, diag, diag_sem)
    fetch.start()
    resid[...] = full_residual(
        local_ref, inc_ref, lower_ref, upper_ref, across_ref, weight_ref, rimcoup_ref, rimrow_ref
    )
    fetch.wait()

    def groups(a, b):
        for u in range(a, b):
            for at in range(0, CELLS, PACK):
                total = None
                for v in range(VARS):
                    span = slice(v * CELLS + at, v * CELLS + at + PACK)
                    term = diag[u, span].astype(jnp.float32) * resid[span]
                    total = term if total is None else total + term
                span = slice(u * CELLS + at, u * CELLS + at + PACK)
                next_ref[span, :] = x_ref[span, :] + STEP_CFL * total
        return next_ref[a * CELLS : b * CELLS]

    copy = send_blocks(
        next_ref, groups, table_ref[...], select_ref[...], out_ref, up_ref, down_ref, rows_ref, sem
    )
    norm_ref[...] = lane_sums(resid[...])
    copy.wait()


def residual_kernel(
    local_ref, inc_ref, lower_ref, upper_ref, across_ref, weight_ref, rimcoup_ref, rimrow_ref, norm_ref,
    resid_ref, sums_ref,
):
    resid = full_residual(
        local_ref, inc_ref, lower_ref, upper_ref, across_ref, weight_ref, rimcoup_ref, rimrow_ref
    )
    resid_ref[...] = resid
    both = jnp.concatenate([norm_ref[...], lane_sums(resid)], axis=0)
    sums_ref[...] = jnp.broadcast_to(both[None], sums_ref.shape)


def direction_kernel(diag_ref, resid_ref, out_ref, resid_out):
    resid_out[...] = resid_ref[...]

    def cells(part, carry):
        at = pl.multiple_of(part * PACK, PACK)
        for u in range(VARS):
            out_ref[pl.ds(u * CELLS + at, PACK), :] = precondition(diag_ref, resid_ref, u, at)
        return carry

    lax.fori_loop(0, CELLS // PACK, cells, 0)


def finish_kernel(entries, sums_ref, x_ref, update_ref, out_ref):
    sums = jnp.sum(jnp.sum(sums_ref[...], axis=0), axis=1, keepdims=True) / entries + 1e-06
    cfl = STEP_CFL * jnp.sqrt(sums[0:1] / sums[1:2])
    out_ref[...] = x_ref[...] + cfl * update_ref[...]


VMEM = pl.BlockSpec(memory_space=pltpu.VMEM)
SMEM = pl.BlockSpec(memory_space=pltpu.SMEM)


def f32(*shape):
    return jax.ShapeDtypeStruct(shape, jnp.float32)


def bf16(*shape):
    return jax.ShapeDtypeStruct(shape, jnp.bfloat16)


def call(kernel, in_specs, out_shape, flops, moved, **more):
    many = isinstance(out_shape, (list, tuple))
    return pl.pallas_call(
        kernel,
        in_specs=in_specs,
        out_specs=more.pop("out_specs", [VMEM] * len(out_shape) if many else VMEM),
        out_shape=out_shape,
        compiler_params=pltpu.CompilerParams(vmem_limit_bytes=VMEM_LIMIT),
        cost_estimate=pl.CostEstimate(flops=flops, bytes_accessed=moved, transcendentals=0),
        **more,
    )


def shards(
    psi_init, source, coupling, diag_inv, neighbours, seam_perm, fringe_src, fringe_dst, fringe_weight
):
    blocks = psi_init.shape[0]
    slots = neighbours.shape[1]
    rim = seam_perm.shape[1]
    fringe = fringe_src.shape[1]
    peers = lax.axis_size("blk")
    devices = lax.axis_size("body") * peers
    up = [(i, (i + 1) % peers) for i in range(peers)]
    down = [(j, i) for i, j in up]
    here = functools.partial(pltpu.with_memory_space_constraint, memory_space=pltpu.HBM)
    x = here(psi_init.T)
    source_t = here(source.T)
    coup = here(coupling.transpose(1, 2, 3, 0))
    diag = here(diag_inv.transpose(1, 2, 0))
    nbr = here(neighbours.T)
    state = f32(BW, blocks)
    hbm = pl.BlockSpec(memory_space=pltpu.HBM)
    message = (devices, BW * fringe // devices // (rim // 2 * LANES), rim // 2, LANES)
    sent = [f32(*message), f32(rim, BW), f32(rim, BW)]
    rows_scratch = [pltpu.VMEM(message, jnp.float32), pltpu.SemaphoreType.DMA]
    size = 4 * BW * blocks

    donors = call(
        donors_kernel,
        [VMEM, VMEM, SMEM],
        sent + [bf16(blocks, fringe), bf16(2 * LANES, LANES), state],
        4 * BW * blocks * fringe,
        2 * size,
        out_specs=[hbm] + [VMEM] * 5,
        scratch_shapes=rows_scratch,
    )
    chunks = blocks // LANES
    scratch = [
        pltpu.VMEM((2 * BW, blocks + LANES), jnp.bfloat16),
        [pltpu.VMEM((BW, slots * LANES), jnp.float32)] * chunks,
        pltpu.VMEM((chunks, slots, VARS, BW, LANES), jnp.bfloat16),
        pltpu.VMEM((BW, blocks), jnp.float32),
        pltpu.SemaphoreType.DMA((chunks,)),
        pltpu.SemaphoreType.DMA,
    ]
    local_more = dict(
        flops=4 * BW * 2 * LANES * slots * blocks,
        moved=coup.size * 2 + 4 * size,
        scratch_shapes=scratch,
    )
    first_local = call(
        functools.partial(first_local_kernel, rim),
        [VMEM, VMEM, hbm, hbm, VMEM, VMEM],
        [
            state,
            bf16(VARS, BW, LANES),
            jax.ShapeDtypeStruct((PACK, LANES), jnp.int32),
            bf16(fringe, blocks),
            f32(1, fringe),
        ],
        **local_more,
    )
    local = call(functools.partial(local_kernel, rim), [VMEM, VMEM, hbm, hbm], state, **local_more)
    advance = call(
        advance_kernel,
        [VMEM] * 8 + [hbm] + [VMEM] * 3,
        [state, f32(1, LANES)] + sent,
        8 * BW * blocks * fringe,
        diag.size * 2 + 4 * size,
        out_specs=[VMEM, VMEM, hbm, VMEM, VMEM],
        scratch_shapes=[
            pltpu.VMEM((BW, blocks), jnp.float32),
            pltpu.VMEM((VARS, BW, blocks), jnp.bfloat16),
            pltpu.SemaphoreType.DMA,
        ]
        + rows_scratch,
    )
    residual = call(
        residual_kernel,
        [VMEM] * 9,
        [state, f32(devices, 2, LANES)],
        4 * BW * blocks * fringe,
        3 * size,
    )
    direction = call(
        direction_kernel, [VMEM] * 2, [state, state], diag.size * 2, diag.size * 2 + 2 * size
    )
    finish = call(
        functools.partial(finish_kernel, float(blocks * devices * BW)),
        [VMEM] * 3,
        state,
        2 * BW * blocks,
        3 * size,
    )

    def exchange(rows, to_up, to_down):
        rows = lax.all_to_all(rows, ("body", "blk"), split_axis=0, concat_axis=0, tiled=True)
        return rows, lax.ppermute(to_up, "blk", up), lax.ppermute(to_down, "blk", down)

    *out, table, select, x_here = donors(x, here(fringe_src), here(seam_perm))
    arrived = exchange(*out)
    part, rimcoup, rimrow, across, weight = first_local(
        x_here, nbr, coup, source_t, here(fringe_dst), here(fringe_weight)
    )
    across = (across, weight, rimcoup, rimrow)
    x, norm, *out = advance(part, *arrived, *across, diag, x_here, table, select)
    arrived = exchange(*out)
    part = local(x, nbr, coup, source_t)
    resid, sums = residual(part, *arrived, *across, norm)
    sums = lax.all_to_all(sums, ("body", "blk"), split_axis=0, concat_axis=0, tiled=True)
    update, resid = direction(diag, resid)
    x = finish(sums, x, update)
    return (x.T, resid.T)


def solution(mesh):
    return jax.shard_map(
        shards,
        mesh=mesh,
        in_specs=(
            P(("body", "blk"), None),
            P(("body", "blk"), None),
            P(("body", "blk"), None, None, None),
            P(("body", "blk"), None, None),
            P(("body", "blk"), None),
            P("body", None),
            P(("body", "blk"), None),
            P(("body", "blk"), None),
            P(("body", "blk"), None),
        ),
        out_specs=(P(("body", "blk"), None), P(("body", "blk"), None)),
        check_vma=False,
    )
```

```python
import functools
import math

import jax
import jax.numpy as jnp
import numpy as np
from jax import lax
from jax.experimental import pallas as pl
from jax.experimental.pallas import tpu as pltpu
from jax.sharding import PartitionSpec as P

CELLS = 64
VARS = 5
BW = 320
STEP_CFL = 0.5
LANES = 128
PACK = 16
VMEM_LIMIT = 32 * 1024 * 1024


def split(x):
    high = x.astype(jnp.bfloat16)
    return high, (x - high.astype(jnp.float32)).astype(jnp.bfloat16)


def onehot(mask):
    return jnp.where(mask, 1.0, 0.0).astype(jnp.bfloat16)


def pick(x, table):
    both = jnp.dot(jnp.concatenate(split(x), axis=0), table, preferred_element_type=jnp.float32)
    return both[: x.shape[0]] + both[x.shape[0] :]


def send_blocks(order, x, table, select, out_ref, up_ref, down_ref, rows_ref, sem):
    rim = up_ref.shape[0]
    half = rows_ref.shape[2]
    rows = pick(x, table).T.reshape(rows_ref.shape[0], 2 * half, BW)
    rows = jnp.concatenate([rows[r : r + 1] for r in order], axis=0)
    for h in range(2):
        for tile in range(2):
            rows_ref[:, 2 * tile + h] = rows[:, h * half : (h + 1) * half, tile * LANES : (tile + 1) * LANES]
    rest = rows[:, :, 2 * LANES :]
    rows_ref[:, 4] = jnp.concatenate([rest[:, :half], rest[:, half:]], axis=2)
    copy = pltpu.make_async_copy(rows_ref, out_ref, sem)
    copy.start()
    index = lax.axis_index("blk")
    at_last = index == lax.axis_size("blk") - 1
    at_first = index == 0
    first = lax.broadcasted_iota(jnp.int32, (BW, LANES), 1) < LANES // 2
    ends = split(jnp.where(first, x[:, :LANES], x[:, x.shape[1] - LANES :]))
    rims = jnp.dot(jnp.concatenate(ends, axis=1), select, preferred_element_type=jnp.float32)
    lane = lax.broadcasted_iota(jnp.int32, (1, LANES), 1)
    turn_up = (lane < rim) & at_last
    turn_down = (lane >= rim) & at_first
    angle = 2.0 * math.pi / 3.0
    cosine = jnp.where(turn_up | turn_down, math.cos(angle), 1.0)
    sine = jnp.where(turn_up, math.sin(angle), jnp.where(turn_down, -math.sin(angle), 0.0))
    first = rims[2 * CELLS : 3 * CELLS]
    second = rims[3 * CELLS : 4 * CELLS]
    rims = jnp.concatenate(
        [
            rims[: 2 * CELLS],
            cosine * first - sine * second,
            sine * first + cosine * second,
            rims[4 * CELLS :],
        ],
        axis=0,
    ).T
    up_ref[...] = rims[:rim]
    down_ref[...] = rims[rim : 2 * rim]
    return copy


def donors_kernel(
    order, x_ref, src_ref, perm_ref,
    out_ref, up_ref, down_ref, table_ref, select_ref, x_out, rows_ref, sem,
):
    rim = up_ref.shape[0]
    index = lax.axis_index("blk")
    at_last = index == lax.axis_size("blk") - 1
    at_first = index == 0
    sub = lax.broadcasted_iota(jnp.int32, (LANES, LANES), 0)
    lane = lax.broadcasted_iota(jnp.int32, (LANES, LANES), 1)
    wanted = lane[:1]
    target = sub[:, :1]
    for j in range(rim):
        partner = perm_ref[0, j]
        wanted = jnp.where((lane[:1] == j) & at_last, partner, wanted)
        target = jnp.where((sub[:, :1] == j) & at_first, partner, target)
    to_up = (sub == wanted + (LANES - rim)) & (lane < rim)
    to_down = (target + rim == lane) & (sub < rim)
    select = onehot(to_up | to_down)
    select = jnp.concatenate([select, select], axis=0)
    rows = lax.broadcasted_iota(jnp.int32, table_ref.shape, 0)
    table = onehot(rows == src_ref[...])
    copy = send_blocks(
        order, x_ref[...], table, select, out_ref, up_ref, down_ref, rows_ref, sem
    )
    table_ref[...] = table
    select_ref[...] = select
    x_out[...] = x_ref[...]
    copy.wait()


def local_kernel(
    rim, x_ref, nbr_ref, coup_ref, source_ref, out_ref, terms, near, coup, source, sems, source_sem,
    at_start=None, with_ends=None,
):
    slots, blocks = nbr_ref.shape
    chunks = blocks // LANES
    spans = [slice(c * LANES, (c + 1) * LANES) for c in range(chunks)]
    order = [0, chunks - 1, *range(1, chunks - 1)]
    source_copy = pltpu.make_async_copy(source_ref, source, source_sem)
    copies = {}
    for c in order:
        copies[c] = pltpu.make_async_copy(coup_ref.at[:, :, :, spans[c]], coup.at[c], sems.at[c])
        copies[c].start()
        if c == order[0]:
            source_copy.start()
    lane = lax.broadcasted_iota(jnp.int32, (BW, LANES), 1)
    moved = pltpu.roll(x_ref[...], rim, 1)
    head = jnp.where(lane < rim, 0.0, moved[:, :LANES])
    tail = jnp.where(lane < rim, moved[:, :LANES], 0.0)
    terms[:BW], terms[BW:] = split(jnp.concatenate([head, moved[:, LANES:], tail], axis=1))
    rows = lax.broadcasted_iota(jnp.int32, (2 * LANES, LANES), 0)

    pairs = range(0, slots, 2)

    def gather(c, m):
        window = slice(c * LANES, (c + 2) * LANES)
        table = jnp.concatenate(
            [onehot(rows == nbr_ref[i : i + 1, spans[c]] - c * LANES) for i in (m, m + 1)], axis=1
        )
        both = jnp.dot(terms[:, window], table, preferred_element_type=jnp.float32)
        near[c][:, m * LANES : (m + 2) * LANES] = both[:BW] + both[BW:]

    for m in pairs:
        gather(order[0], m)
    if at_start is not None:
        at_start()
    for step, c in enumerate(order):
        copies[c].wait()
        if step == 0:
            source_copy.wait()
        ahead = list(pairs) if step + 1 < chunks else []
        for at in range(0, CELLS, PACK):
            if ahead:
                gather(order[step + 1], ahead.pop(0))
            if with_ends is not None and step in (1, 2) and (at < CELLS // 2) == (step == 1):
                with_ends(at)
            total = [None] * VARS
            for m in range(slots):
                for v in range(VARS):
                    span = slice(v * CELLS + at, v * CELLS + at + PACK)
                    value = near[c][span, m * LANES : (m + 1) * LANES]
                    for u in range(VARS):
                        term = coup[c, m, u, span, :].astype(jnp.float32) * value
                        total[u] = term if total[u] is None else total[u] + term
            for u in range(VARS):
                span = slice(u * CELLS + at, u * CELLS + at + PACK)
                out_ref[span, spans[c]] = source[span, spans[c]] - x_ref[span, spans[c]] + total[u]


def first_local_kernel(
    rim, x_ref, nbr_ref, coup_ref, source_ref, dst_ref, weight_ref,
    out_ref, rimcoup_ref, rimrow_ref, table_ref, weight_out,
    terms, near, coup, source, sems, source_sem,
):
    slots, blocks = nbr_ref.shape
    chunks = blocks // LANES
    fringe = dst_ref.shape[1]
    lane = lax.broadcasted_iota(jnp.int32, (PACK, LANES), 1)
    first = lane < LANES // 2
    masks = [lax.rem(lane + rim + LANES - m * 2 * rim, LANES) < 2 * rim for m in range(slots)]

    def merged(ends, nothing):
        result = nothing
        for m in range(slots):
            both = jnp.where(first, *ends(m))
            if m > 0:
                both = pltpu.roll(both, m * 2 * rim, 1)
            result = jnp.where(masks[m], both, result)
        return result

    def rows(m):
        lower = jnp.broadcast_to(nbr_ref[m : m + 1, :LANES], (PACK, LANES))
        upper = jnp.broadcast_to(nbr_ref[m : m + 1, blocks - LANES :], (PACK, LANES))
        return jnp.where(lower < rim, lower, -LANES), jnp.where(upper >= blocks + rim, upper - blocks, -LANES)

    def tables():
        rimrow_ref[...] = merged(rows, jnp.full((PACK, LANES), -LANES, jnp.int32))
        weight_out[...] = weight_ref[...]
        targets = jnp.broadcast_to(dst_ref[...], (LANES, fringe)).T
        for c in range(chunks):
            table_ref[:, c * LANES : (c + 1) * LANES] = onehot(targets == lane[:1] + c * LANES)

    def rim_coupling(at):
        for u in range(VARS):
            for v in range(VARS):
                span = slice(v * CELLS + at, v * CELLS + at + PACK)
                rimcoup_ref[u, span, :] = merged(
                    lambda m: (coup[0, m, u, span, :], coup[chunks - 1, m, u, span, :]),
                    jnp.zeros((PACK, LANES), jnp.bfloat16),
                )

    local_kernel(
        rim, x_ref, nbr_ref, coup_ref, source_ref, out_ref, terms, near, coup, source, sems, source_sem,
        tables, rim_coupling,
    )


def full_residual(order, local_ref, inc_ref, lower_ref, upper_ref, table_ref, weight_ref, rimcoup_ref, rimrow_ref):
    rim = lower_ref.shape[0]
    blocks = local_ref.shape[1]
    rims = jnp.concatenate(
        [lower_ref[...], upper_ref[...], jnp.zeros((LANES - 2 * rim, BW), jnp.float32)], axis=0
    ).T
    high, low = split(rims)
    low = pltpu.roll(low.astype(jnp.float32), 2 * rim, 1)
    rims = (high.astype(jnp.float32) + low).astype(jnp.bfloat16)
    sub = lax.broadcasted_iota(jnp.int32, (LANES, LANES), 0)
    row = rimrow_ref[:1]
    reads = onehot((sub == row) | (sub == row + 2 * rim))
    near = jnp.dot(rims, reads, preferred_element_type=jnp.float32)
    edge = []
    for u in range(VARS):
        total = None
        for v in range(VARS):
            span = slice(v * CELLS, (v + 1) * CELLS)
            term = rimcoup_ref[u, span, :].astype(jnp.float32) * near[span]
            total = term if total is None else total + term
        edge.append(total)
    edge = jnp.concatenate(edge, axis=0)
    shift = LANES // 2
    while shift >= 2 * rim:
        edge = edge + pltpu.roll(edge, shift, 1)
        shift //= 2
    lane = lax.broadcasted_iota(jnp.int32, (BW, LANES), 1)
    inc = jnp.concatenate([inc_ref[i : i + 1] for i in np.argsort(order).tolist()], axis=0)
    rest = inc[:, 4]
    rest = jnp.concatenate([rest[:, :, :CELLS], rest[:, :, CELLS:]], axis=1).reshape(-1, CELLS)
    fringe = [inc[:, 0:2].reshape(-1, LANES).T, inc[:, 2:4].reshape(-1, LANES).T, rest.T]
    total = local_ref[...] + pick(jnp.concatenate(fringe, axis=0) * weight_ref[...], table_ref[...])
    lower = total[:, :LANES] + jnp.where(lane < rim, edge, 0.0)
    upper = total[:, blocks - LANES :] + jnp.where(lane >= LANES - rim, edge, 0.0)
    return jnp.concatenate([lower, total[:, LANES : blocks - LANES], upper], axis=1)


def precondition(diag_ref, resid_ref, u, at):
    total = None
    for v in range(VARS):
        span = pl.ds(v * CELLS + at, PACK)
        term = diag_ref[u, span, :].astype(jnp.float32) * resid_ref[span, :]
        total = term if total is None else total + term
    return total


def lane_sums(resid):
    square = jnp.sum(resid * resid, axis=0, keepdims=True)
    return sum(square[:, i : i + LANES] for i in range(0, square.shape[1], LANES))


def advance_kernel(
    order, local_ref, inc_ref, lower_ref, upper_ref, across_ref, weight_ref, rimcoup_ref, rimrow_ref,
    diag_ref, x_ref, table_ref, select_ref,
    next_ref, norm_ref, out_ref, up_ref, down_ref, resid, diag, diag_sem, rows_ref, sem,
):
    fetch = pltpu.make_async_copy(diag_ref, diag, diag_sem)
    fetch.start()
    resid[...] = full_residual(
        order, local_ref, inc_ref, lower_ref, upper_ref, across_ref, weight_ref, rimcoup_ref, rimrow_ref
    )
    fetch.wait()
    for u in range(VARS):
        for at in range(0, CELLS, PACK):
            total = None
            for v in range(VARS):
                span = slice(v * CELLS + at, v * CELLS + at + PACK)
                term = diag[u, span].astype(jnp.float32) * resid[span]
                total = term if total is None else total + term
            span = slice(u * CELLS + at, u * CELLS + at + PACK)
            next_ref[span, :] = x_ref[span, :] + STEP_CFL * total
    copy = send_blocks(
        order, next_ref[...], table_ref[...], select_ref[...], out_ref, up_ref, down_ref, rows_ref, sem
    )
    norm_ref[...] = lane_sums(resid[...])
    copy.wait()


def residual_kernel(
    order, local_ref, inc_ref, lower_ref, upper_ref, across_ref, weight_ref, rimcoup_ref, rimrow_ref, norm_ref,
    resid_ref, sums_ref,
):
    resid = full_residual(
        order, local_ref, inc_ref, lower_ref, upper_ref, across_ref, weight_ref, rimcoup_ref, rimrow_ref
    )
    resid_ref[...] = resid
    both = jnp.concatenate([norm_ref[...], lane_sums(resid)], axis=0)
    sums_ref[...] = jnp.broadcast_to(both[None], sums_ref.shape)


def direction_kernel(diag_ref, resid_ref, out_ref, resid_out):
    resid_out[...] = resid_ref[...]

    def cells(part, carry):
        at = pl.multiple_of(part * PACK, PACK)
        for u in range(VARS):
            out_ref[pl.ds(u * CELLS + at, PACK), :] = precondition(diag_ref, resid_ref, u, at)
        return carry

    lax.fori_loop(0, CELLS // PACK, cells, 0)


def finish_kernel(entries, sums_ref, x_ref, update_ref, out_ref):
    sums = jnp.sum(jnp.sum(sums_ref[...], axis=0), axis=1, keepdims=True) / entries + 1e-06
    cfl = STEP_CFL * jnp.sqrt(sums[0:1] / sums[1:2])
    out_ref[...] = x_ref[...] + cfl * update_ref[...]


VMEM = pl.BlockSpec(memory_space=pltpu.VMEM)
SMEM = pl.BlockSpec(memory_space=pltpu.SMEM)


def f32(*shape):
    return jax.ShapeDtypeStruct(shape, jnp.float32)


def bf16(*shape):
    return jax.ShapeDtypeStruct(shape, jnp.bfloat16)


def call(kernel, in_specs, out_shape, flops, moved, **more):
    many = isinstance(out_shape, (list, tuple))
    return pl.pallas_call(
        kernel,
        in_specs=in_specs,
        out_specs=more.pop("out_specs", [VMEM] * len(out_shape) if many else VMEM),
        out_shape=out_shape,
        compiler_params=pltpu.CompilerParams(vmem_limit_bytes=VMEM_LIMIT),
        cost_estimate=pl.CostEstimate(flops=flops, bytes_accessed=moved, transcendentals=0),
        **more,
    )


def message_order(bodies, peers):
    middle = peers // 2
    far_first = sorted(range(peers), key=lambda k: -abs(2 * k + 1 - peers))
    order = [b * peers + k for b in reversed(range(bodies)) for k in far_first]
    order.remove(middle)
    return [middle, *order]


def shards(
    psi_init, source, coupling, diag_inv, neighbours, seam_perm, fringe_src, fringe_dst, fringe_weight
):
    blocks = psi_init.shape[0]
    slots = neighbours.shape[1]
    rim = seam_perm.shape[1]
    fringe = fringe_src.shape[1]
    peers = lax.axis_size("blk")
    devices = lax.axis_size("body") * peers
    order = message_order(devices // peers, peers)
    up = [(i, (i + 1) % peers) for i in range(peers)]
    down = [(j, i) for i, j in up]
    here = functools.partial(pltpu.with_memory_space_constraint, memory_space=pltpu.HBM)
    x = here(psi_init.T)
    source_t = here(source.T)
    coup = here(coupling.transpose(1, 2, 3, 0))
    diag = here(diag_inv.transpose(1, 2, 0))
    nbr = here(neighbours.T)
    state = f32(BW, blocks)
    hbm = pl.BlockSpec(memory_space=pltpu.HBM)
    message = (devices, BW * fringe // devices // (rim // 2 * LANES), rim // 2, LANES)
    sent = [f32(*message), f32(rim, BW), f32(rim, BW)]
    rows_scratch = [pltpu.VMEM(message, jnp.float32), pltpu.SemaphoreType.DMA]
    size = 4 * BW * blocks

    donors = call(
        functools.partial(donors_kernel, order),
        [VMEM, VMEM, SMEM],
        sent + [bf16(blocks, fringe), bf16(2 * LANES, LANES), state],
        4 * BW * blocks * fringe,
        2 * size,
        out_specs=[hbm] + [VMEM] * 5,
        scratch_shapes=rows_scratch,
    )
    chunks = blocks // LANES
    scratch = [
        pltpu.VMEM((2 * BW, blocks + LANES), jnp.bfloat16),
        [pltpu.VMEM((BW, slots * LANES), jnp.float32)] * chunks,
        pltpu.VMEM((chunks, slots, VARS, BW, LANES), jnp.bfloat16),
        pltpu.VMEM((BW, blocks), jnp.float32),
        pltpu.SemaphoreType.DMA((chunks,)),
        pltpu.SemaphoreType.DMA,
    ]
    local_more = dict(
        flops=4 * BW * 2 * LANES * slots * blocks,
        moved=coup.size * 2 + 4 * size,
        scratch_shapes=scratch,
    )
    first_local = call(
        functools.partial(first_local_kernel, rim),
        [VMEM, VMEM, hbm, hbm, VMEM, VMEM],
        [
            state,
            bf16(VARS, BW, LANES),
            jax.ShapeDtypeStruct((PACK, LANES), jnp.int32),
            bf16(fringe, blocks),
            f32(1, fringe),
        ],
        **local_more,
    )
    local = call(functools.partial(local_kernel, rim), [VMEM, VMEM, hbm, hbm], state, **local_more)
    advance = call(
        functools.partial(advance_kernel, order),
        [VMEM] * 8 + [hbm] + [VMEM] * 3,
        [state, f32(1, LANES)] + sent,
        8 * BW * blocks * fringe,
        diag.size * 2 + 4 * size,
        out_specs=[VMEM, VMEM, hbm, VMEM, VMEM],
        scratch_shapes=[
            pltpu.VMEM((BW, blocks), jnp.float32),
            pltpu.VMEM((VARS, BW, blocks), jnp.bfloat16),
            pltpu.SemaphoreType.DMA,
        ]
        + rows_scratch,
    )
    residual = call(
        functools.partial(residual_kernel, order),
        [VMEM] * 9,
        [state, f32(devices, 2, LANES)],
        4 * BW * blocks * fringe,
        3 * size,
    )
    direction = call(
        direction_kernel, [VMEM] * 2, [state, state], diag.size * 2, diag.size * 2 + 2 * size
    )
    finish = call(
        functools.partial(finish_kernel, float(blocks * devices * BW)),
        [VMEM] * 3,
        state,
        2 * BW * blocks,
        3 * size,
    )

    everyone = functools.partial(
        lax.all_to_all,
        axis_name=("body", "blk"),
        split_axis=0,
        concat_axis=0,
        tiled=True,
        axis_index_groups=[order],
    )

    def exchange(rows, to_up, to_down):
        rows = everyone(rows)
        return rows, lax.ppermute(to_up, "blk", up), lax.ppermute(to_down, "blk", down)

    *out, table, select, x_here = donors(x, here(fringe_src), here(seam_perm))
    arrived = exchange(*out)
    part, rimcoup, rimrow, across, weight = first_local(
        x_here, nbr, coup, source_t, here(fringe_dst), here(fringe_weight)
    )
    across = (across, weight, rimcoup, rimrow)
    x, norm, *out = advance(part, *arrived, *across, diag, x_here, table, select)
    arrived = exchange(*out)
    part = local(x, nbr, coup, source_t)
    resid, sums = residual(part, *arrived, *across, norm)
    sums = everyone(sums)
    update, resid = direction(diag, resid)
    x = finish(sums, x, update)
    return (x.T, resid.T)


def solution(mesh):
    return jax.shard_map(
        shards,
        mesh=mesh,
        in_specs=(
            P(("body", "blk"), None),
            P(("body", "blk"), None),
            P(("body", "blk"), None, None, None),
            P(("body", "blk"), None, None),
            P(("body", "blk"), None),
            P("body", None),
            P(("body", "blk"), None),
            P(("body", "blk"), None),
            P(("body", "blk"), None),
        ),
        out_specs=(P(("body", "blk"), None), P(("body", "blk"), None)),
        check_vma=False,
    )
```

```python
import functools
import math

import jax
import jax.numpy as jnp
import numpy as np
from jax import lax
from jax.experimental import pallas as pl
from jax.experimental.pallas import tpu as pltpu
from jax.sharding import PartitionSpec as P

CELLS = 64
VARS = 5
BW = 320
STEP_CFL = 0.5
LANES = 128
PACK = 16
VMEM_LIMIT = 32 * 1024 * 1024


def split(x):
    high = x.astype(jnp.bfloat16)
    return high, (x - high.astype(jnp.float32)).astype(jnp.bfloat16)


def onehot(mask):
    return jnp.where(mask, 1.0, 0.0).astype(jnp.bfloat16)


def pick(x, table):
    both = jnp.dot(jnp.concatenate(split(x), axis=0), table, preferred_element_type=jnp.float32)
    return both[: x.shape[0]] + both[x.shape[0] :]


def send_blocks(order, x, table, select, out_ref, up_ref, down_ref, rows_ref, sem):
    rim = up_ref.shape[0]
    half = rows_ref.shape[2]
    rows = pick(x, table).T.reshape(rows_ref.shape[0], 2 * half, BW)
    rows = jnp.concatenate([rows[r : r + 1] for r in order], axis=0)
    for h in range(2):
        for tile in range(2):
            rows_ref[:, 2 * tile + h] = rows[:, h * half : (h + 1) * half, tile * LANES : (tile + 1) * LANES]
    rest = rows[:, :, 2 * LANES :]
    rows_ref[:, 4] = jnp.concatenate([rest[:, :half], rest[:, half:]], axis=2)
    copy = pltpu.make_async_copy(rows_ref, out_ref, sem)
    copy.start()
    index = lax.axis_index("blk")
    at_last = index == lax.axis_size("blk") - 1
    at_first = index == 0
    first = lax.broadcasted_iota(jnp.int32, (BW, LANES), 1) < LANES // 2
    ends = split(jnp.where(first, x[:, :LANES], x[:, x.shape[1] - LANES :]))
    rims = jnp.dot(jnp.concatenate(ends, axis=1), select, preferred_element_type=jnp.float32)
    lane = lax.broadcasted_iota(jnp.int32, (1, LANES), 1)
    turn_up = (lane < rim) & at_last
    turn_down = (lane >= rim) & at_first
    angle = 2.0 * math.pi / 3.0
    cosine = jnp.where(turn_up | turn_down, math.cos(angle), 1.0)
    sine = jnp.where(turn_up, math.sin(angle), jnp.where(turn_down, -math.sin(angle), 0.0))
    first = rims[2 * CELLS : 3 * CELLS]
    second = rims[3 * CELLS : 4 * CELLS]
    rims = jnp.concatenate(
        [
            rims[: 2 * CELLS],
            cosine * first - sine * second,
            sine * first + cosine * second,
            rims[4 * CELLS :],
        ],
        axis=0,
    ).T
    up_ref[...] = rims[:rim]
    down_ref[...] = rims[rim : 2 * rim]
    return copy


def donors_kernel(
    order, x_ref, src_ref, perm_ref,
    out_ref, up_ref, down_ref, table_ref, select_ref, x_out, rows_ref, sem,
):
    rim = up_ref.shape[0]
    index = lax.axis_index("blk")
    at_last = index == lax.axis_size("blk") - 1
    at_first = index == 0
    sub = lax.broadcasted_iota(jnp.int32, (LANES, LANES), 0)
    lane = lax.broadcasted_iota(jnp.int32, (LANES, LANES), 1)
    wanted = lane[:1]
    target = sub[:, :1]
    for j in range(rim):
        partner = perm_ref[0, j]
        wanted = jnp.where((lane[:1] == j) & at_last, partner, wanted)
        target = jnp.where((sub[:, :1] == j) & at_first, partner, target)
    to_up = (sub == wanted + (LANES - rim)) & (lane < rim)
    to_down = (target + rim == lane) & (sub < rim)
    select = onehot(to_up | to_down)
    select = jnp.concatenate([select, select], axis=0)
    rows = lax.broadcasted_iota(jnp.int32, table_ref.shape, 0)
    table = onehot(rows == src_ref[...])
    copy = send_blocks(
        order, x_ref[...], table, select, out_ref, up_ref, down_ref, rows_ref, sem
    )
    table_ref[...] = table
    select_ref[...] = select
    x_out[...] = x_ref[...]
    copy.wait()


def local_kernel(
    rim, x_ref, nbr_ref, coup_ref, source_ref, out_ref, terms, near, coup, source, sems, source_sem,
    at_start=None, with_ends=None,
):
    slots, blocks = nbr_ref.shape
    chunks = blocks // LANES
    spans = [slice(c * LANES, (c + 1) * LANES) for c in range(chunks)]
    order = [0, chunks - 1, *range(1, chunks - 1)]
    source_copy = pltpu.make_async_copy(source_ref, source, source_sem)
    copies = {}
    for c in order:
        copies[c] = pltpu.make_async_copy(coup_ref.at[:, :, :, spans[c]], coup.at[c], sems.at[c])
        copies[c].start()
        if c == order[0]:
            source_copy.start()
    lane = lax.broadcasted_iota(jnp.int32, (BW, LANES), 1)
    moved = pltpu.roll(x_ref[...], rim, 1)
    head = jnp.where(lane < rim, 0.0, moved[:, :LANES])
    tail = jnp.where(lane < rim, moved[:, :LANES], 0.0)
    terms[:BW], terms[BW:] = split(jnp.concatenate([head, moved[:, LANES:], tail], axis=1))
    rows = lax.broadcasted_iota(jnp.int32, (2 * LANES, LANES), 0)

    pairs = range(0, slots, 2)

    def gather(c, m):
        window = slice(c * LANES, (c + 2) * LANES)
        table = jnp.concatenate(
            [onehot(rows == nbr_ref[i : i + 1, spans[c]] - c * LANES) for i in (m, m + 1)], axis=1
        )
        both = jnp.dot(terms[:, window], table, preferred_element_type=jnp.float32)
        near[c][:, m * LANES : (m + 2) * LANES] = both[:BW] + both[BW:]

    for m in pairs:
        gather(order[0], m)
    if at_start is not None:
        at_start()
    for step, c in enumerate(order):
        copies[c].wait()
        if step == 0:
            source_copy.wait()
        ahead = list(pairs) if step + 1 < chunks else []
        for at in range(0, CELLS, PACK):
            if ahead:
                gather(order[step + 1], ahead.pop(0))
            if with_ends is not None and step in (1, 2) and (at < CELLS // 2) == (step == 1):
                with_ends(at)
            total = [None] * VARS
            for m in range(slots):
                for v in range(VARS):
                    span = slice(v * CELLS + at, v * CELLS + at + PACK)
                    value = near[c][span, m * LANES : (m + 1) * LANES]
                    for u in range(VARS):
                        term = coup[c, m, u, span, :].astype(jnp.float32) * value
                        total[u] = term if total[u] is None else total[u] + term
            for u in range(VARS):
                span = slice(u * CELLS + at, u * CELLS + at + PACK)
                out_ref[span, spans[c]] = source[span, spans[c]] - x_ref[span, spans[c]] + total[u]


def first_local_kernel(
    rim, x_ref, nbr_ref, coup_ref, source_ref, dst_ref, weight_ref,
    out_ref, rimcoup_ref, rimrow_ref, table_ref, weight_out,
    terms, near, coup, source, sems, source_sem,
):
    slots, blocks = nbr_ref.shape
    chunks = blocks // LANES
    fringe = dst_ref.shape[1]
    lane = lax.broadcasted_iota(jnp.int32, (PACK, LANES), 1)
    first = lane < LANES // 2
    masks = [lax.rem(lane + rim + LANES - m * 2 * rim, LANES) < 2 * rim for m in range(slots)]

    def merged(ends, nothing):
        result = nothing
        for m in range(slots):
            both = jnp.where(first, *ends(m))
            if m > 0:
                both = pltpu.roll(both, m * 2 * rim, 1)
            result = jnp.where(masks[m], both, result)
        return result

    def rows(m):
        lower = jnp.broadcast_to(nbr_ref[m : m + 1, :LANES], (PACK, LANES))
        upper = jnp.broadcast_to(nbr_ref[m : m + 1, blocks - LANES :], (PACK, LANES))
        return jnp.where(lower < rim, lower, -LANES), jnp.where(upper >= blocks + rim, upper - blocks, -LANES)

    def tables():
        rimrow_ref[...] = merged(rows, jnp.full((PACK, LANES), -LANES, jnp.int32))
        weight_out[...] = weight_ref[...]
        targets = jnp.broadcast_to(dst_ref[...], (LANES, fringe)).T
        for c in range(chunks):
            table_ref[:, c * LANES : (c + 1) * LANES] = onehot(targets == lane[:1] + c * LANES)

    def rim_coupling(at):
        for u in range(VARS):
            for v in range(VARS):
                span = slice(v * CELLS + at, v * CELLS + at + PACK)
                rimcoup_ref[u, span, :] = merged(
                    lambda m: (coup[0, m, u, span, :], coup[chunks - 1, m, u, span, :]),
                    jnp.zeros((PACK, LANES), jnp.bfloat16),
                )

    local_kernel(
        rim, x_ref, nbr_ref, coup_ref, source_ref, out_ref, terms, near, coup, source, sems, source_sem,
        tables, rim_coupling,
    )


def full_residual(order, local_ref, inc_ref, lower_ref, upper_ref, table_ref, weight_ref, rimcoup_ref, rimrow_ref):
    rim = lower_ref.shape[0]
    blocks = local_ref.shape[1]
    rims = jnp.concatenate(
        [lower_ref[...], upper_ref[...], jnp.zeros((LANES - 2 * rim, BW), jnp.float32)], axis=0
    ).T
    high, low = split(rims)
    low = pltpu.roll(low.astype(jnp.float32), 2 * rim, 1)
    rims = (high.astype(jnp.float32) + low).astype(jnp.bfloat16)
    sub = lax.broadcasted_iota(jnp.int32, (LANES, LANES), 0)
    row = rimrow_ref[:1]
    reads = onehot((sub == row) | (sub == row + 2 * rim))
    near = jnp.dot(rims, reads, preferred_element_type=jnp.float32)
    edge = []
    for u in range(VARS):
        total = None
        for v in range(VARS):
            span = slice(v * CELLS, (v + 1) * CELLS)
            term = rimcoup_ref[u, span, :].astype(jnp.float32) * near[span]
            total = term if total is None else total + term
        edge.append(total)
    edge = jnp.concatenate(edge, axis=0)
    shift = LANES // 2
    while shift >= 2 * rim:
        edge = edge + pltpu.roll(edge, shift, 1)
        shift //= 2
    lane = lax.broadcasted_iota(jnp.int32, (BW, LANES), 1)
    inc = jnp.concatenate([inc_ref[i : i + 1] for i in np.argsort(order).tolist()], axis=0)
    rest = inc[:, 4]
    rest = jnp.concatenate([rest[:, :, :CELLS], rest[:, :, CELLS:]], axis=1).reshape(-1, CELLS)
    fringe = [inc[:, 0:2].reshape(-1, LANES).T, inc[:, 2:4].reshape(-1, LANES).T, rest.T]
    total = local_ref[...] + pick(jnp.concatenate(fringe, axis=0) * weight_ref[...], table_ref[...])
    lower = total[:, :LANES] + jnp.where(lane < rim, edge, 0.0)
    upper = total[:, blocks - LANES :] + jnp.where(lane >= LANES - rim, edge, 0.0)
    return jnp.concatenate([lower, total[:, LANES : blocks - LANES], upper], axis=1)


def precondition(diag_ref, resid_ref, u, at):
    total = None
    for v in range(VARS):
        span = pl.ds(v * CELLS + at, PACK)
        term = diag_ref[u, span, :].astype(jnp.float32) * resid_ref[span, :]
        total = term if total is None else total + term
    return total


def lane_sums(resid):
    square = jnp.sum(resid * resid, axis=0, keepdims=True)
    return sum(square[:, i : i + LANES] for i in range(0, square.shape[1], LANES))


def advance_kernel(
    order, local_ref, inc_ref, lower_ref, upper_ref, across_ref, weight_ref, rimcoup_ref, rimrow_ref,
    diag_ref, x_ref, table_ref, select_ref,
    next_ref, norm_ref, out_ref, up_ref, down_ref, resid, diag, diag_sem, rows_ref, sem,
):
    fetch = pltpu.make_async_copy(diag_ref, diag, diag_sem)
    fetch.start()
    resid[...] = full_residual(
        order, local_ref, inc_ref, lower_ref, upper_ref, across_ref, weight_ref, rimcoup_ref, rimrow_ref
    )
    fetch.wait()
    for u in range(VARS):
        for at in range(0, CELLS, PACK):
            total = None
            for v in range(VARS):
                span = slice(v * CELLS + at, v * CELLS + at + PACK)
                term = diag[u, span].astype(jnp.float32) * resid[span]
                total = term if total is None else total + term
            span = slice(u * CELLS + at, u * CELLS + at + PACK)
            next_ref[span, :] = x_ref[span, :] + STEP_CFL * total
    copy = send_blocks(
        order, next_ref[...], table_ref[...], select_ref[...], out_ref, up_ref, down_ref, rows_ref, sem
    )
    norm_ref[...] = lane_sums(resid[...])
    copy.wait()


def residual_kernel(
    order, local_ref, inc_ref, lower_ref, upper_ref, across_ref, weight_ref, rimcoup_ref, rimrow_ref, norm_ref,
    resid_ref, sums_ref,
):
    resid = full_residual(
        order, local_ref, inc_ref, lower_ref, upper_ref, across_ref, weight_ref, rimcoup_ref, rimrow_ref
    )
    resid_ref[...] = resid
    both = jnp.concatenate([norm_ref[...], lane_sums(resid)], axis=0)
    sums_ref[...] = jnp.broadcast_to(both[None], sums_ref.shape)


def direction_kernel(diag_ref, resid_ref, out_ref, resid_out):
    resid_out[...] = resid_ref[...]

    def cells(part, carry):
        at = pl.multiple_of(part * PACK, PACK)
        for u in range(VARS):
            out_ref[pl.ds(u * CELLS + at, PACK), :] = precondition(diag_ref, resid_ref, u, at)
        return carry

    lax.fori_loop(0, CELLS // PACK, cells, 0)


def finish_kernel(entries, sums_ref, x_ref, update_ref, out_ref):
    sums = jnp.sum(jnp.sum(sums_ref[...], axis=0), axis=1, keepdims=True) / entries + 1e-06
    cfl = STEP_CFL * jnp.sqrt(sums[0:1] / sums[1:2])
    out_ref[...] = x_ref[...] + cfl * update_ref[...]


VMEM = pl.BlockSpec(memory_space=pltpu.VMEM)
SMEM = pl.BlockSpec(memory_space=pltpu.SMEM)


def f32(*shape):
    return jax.ShapeDtypeStruct(shape, jnp.float32)


def bf16(*shape):
    return jax.ShapeDtypeStruct(shape, jnp.bfloat16)


def call(kernel, in_specs, out_shape, flops, moved, **more):
    many = isinstance(out_shape, (list, tuple))
    return pl.pallas_call(
        kernel,
        in_specs=in_specs,
        out_specs=more.pop("out_specs", [VMEM] * len(out_shape) if many else VMEM),
        out_shape=out_shape,
        compiler_params=pltpu.CompilerParams(vmem_limit_bytes=VMEM_LIMIT),
        cost_estimate=pl.CostEstimate(flops=flops, bytes_accessed=moved, transcendentals=0),
        **more,
    )


def message_order(bodies, peers):
    return sorted(range(bodies * peers), key=lambda i: i * 0.6180339887 % 1.0)


def shards(
    psi_init, source, coupling, diag_inv, neighbours, seam_perm, fringe_src, fringe_dst, fringe_weight
):
    blocks = psi_init.shape[0]
    slots = neighbours.shape[1]
    rim = seam_perm.shape[1]
    fringe = fringe_src.shape[1]
    peers = lax.axis_size("blk")
    devices = lax.axis_size("body") * peers
    order = message_order(devices // peers, peers)
    up = [(i, (i + 1) % peers) for i in range(peers)]
    down = [(j, i) for i, j in up]
    here = functools.partial(pltpu.with_memory_space_constraint, memory_space=pltpu.HBM)
    x = here(psi_init.T)
    source_t = here(source.T)
    coup = here(coupling.transpose(1, 2, 3, 0))
    diag = here(diag_inv.transpose(1, 2, 0))
    nbr = here(neighbours.T)
    state = f32(BW, blocks)
    hbm = pl.BlockSpec(memory_space=pltpu.HBM)
    message = (devices, BW * fringe // devices // (rim // 2 * LANES), rim // 2, LANES)
    sent = [f32(*message), f32(rim, BW), f32(rim, BW)]
    rows_scratch = [pltpu.VMEM(message, jnp.float32), pltpu.SemaphoreType.DMA]
    size = 4 * BW * blocks

    donors = call(
        functools.partial(donors_kernel, order),
        [VMEM, VMEM, SMEM],
        sent + [bf16(blocks, fringe), bf16(2 * LANES, LANES), state],
        4 * BW * blocks * fringe,
        2 * size,
        out_specs=[hbm] + [VMEM] * 5,
        scratch_shapes=rows_scratch,
    )
    chunks = blocks // LANES
    scratch = [
        pltpu.VMEM((2 * BW, blocks + LANES), jnp.bfloat16),
        [pltpu.VMEM((BW, slots * LANES), jnp.float32)] * chunks,
        pltpu.VMEM((chunks, slots, VARS, BW, LANES), jnp.bfloat16),
        pltpu.VMEM((BW, blocks), jnp.float32),
        pltpu.SemaphoreType.DMA((chunks,)),
        pltpu.SemaphoreType.DMA,
    ]
    local_more = dict(
        flops=4 * BW * 2 * LANES * slots * blocks,
        moved=coup.size * 2 + 4 * size,
        scratch_shapes=scratch,
    )
    first_local = call(
        functools.partial(first_local_kernel, rim),
        [VMEM, VMEM, hbm, hbm, VMEM, VMEM],
        [
            state,
            bf16(VARS, BW, LANES),
            jax.ShapeDtypeStruct((PACK, LANES), jnp.int32),
            bf16(fringe, blocks),
            f32(1, fringe),
        ],
        **local_more,
    )
    local = call(functools.partial(local_kernel, rim), [VMEM, VMEM, hbm, hbm], state, **local_more)
    advance = call(
        functools.partial(advance_kernel, order),
        [VMEM] * 8 + [hbm] + [VMEM] * 3,
        [state, f32(1, LANES)] + sent,
        8 * BW * blocks * fringe,
        diag.size * 2 + 4 * size,
        out_specs=[VMEM, VMEM, hbm, VMEM, VMEM],
        scratch_shapes=[
            pltpu.VMEM((BW, blocks), jnp.float32),
            pltpu.VMEM((VARS, BW, blocks), jnp.bfloat16),
            pltpu.SemaphoreType.DMA,
        ]
        + rows_scratch,
    )
    residual = call(
        functools.partial(residual_kernel, order),
        [VMEM] * 9,
        [state, f32(devices, 2, LANES)],
        4 * BW * blocks * fringe,
        3 * size,
    )
    direction = call(
        direction_kernel, [VMEM] * 2, [state, state], diag.size * 2, diag.size * 2 + 2 * size
    )
    finish = call(
        functools.partial(finish_kernel, float(blocks * devices * BW)),
        [VMEM] * 3,
        state,
        2 * BW * blocks,
        3 * size,
    )

    everyone = functools.partial(
        lax.all_to_all,
        axis_name=("body", "blk"),
        split_axis=0,
        concat_axis=0,
        tiled=True,
        axis_index_groups=[order],
    )

    def exchange(rows, to_up, to_down):
        rows = everyone(rows)
        return rows, lax.ppermute(to_up, "blk", up), lax.ppermute(to_down, "blk", down)

    *out, table, select, x_here = donors(x, here(fringe_src), here(seam_perm))
    arrived = exchange(*out)
    part, rimcoup, rimrow, across, weight = first_local(
        x_here, nbr, coup, source_t, here(fringe_dst), here(fringe_weight)
    )
    across = (across, weight, rimcoup, rimrow)
    x, norm, *out = advance(part, *arrived, *across, diag, x_here, table, select)
    arrived = exchange(*out)
    part = local(x, nbr, coup, source_t)
    resid, sums = residual(part, *arrived, *across, norm)
    sums = everyone(sums)
    update, resid = direction(diag, resid)
    x = finish(sums, x, update)
    return (x.T, resid.T)


def solution(mesh):
    return jax.shard_map(
        shards,
        mesh=mesh,
        in_specs=(
            P(("body", "blk"), None),
            P(("body", "blk"), None),
            P(("body", "blk"), None, None, None),
            P(("body", "blk"), None, None),
            P(("body", "blk"), None),
            P("body", None),
            P(("body", "blk"), None),
            P(("body", "blk"), None),
            P(("body", "blk"), None),
        ),
        out_specs=(P(("body", "blk"), None), P(("body", "blk"), None)),
        check_vma=False,
    )
```

```python
import functools
import math

import jax
import jax.numpy as jnp
import numpy as np
from jax import lax
from jax.experimental import pallas as pl
from jax.experimental.pallas import tpu as pltpu
from jax.sharding import PartitionSpec as P

CELLS = 64
VARS = 5
BW = 320
STEP_CFL = 0.5
LANES = 128
PACK = 16
VMEM_LIMIT = 32 * 1024 * 1024


def split(x):
    high = x.astype(jnp.bfloat16)
    return high, (x - high.astype(jnp.float32)).astype(jnp.bfloat16)


def onehot(mask):
    return jnp.where(mask, 1.0, 0.0).astype(jnp.bfloat16)


def pick(x, table):
    both = jnp.dot(jnp.concatenate(split(x), axis=0), table, preferred_element_type=jnp.float32)
    return both[: x.shape[0]] + both[x.shape[0] :]


def send_blocks(order, x, table, select, out_ref, up_ref, down_ref, rows_ref, sem):
    rim = up_ref.shape[0]
    half = rows_ref.shape[2]
    rows = pick(x, table).T.reshape(rows_ref.shape[0], 2 * half, BW)
    rows = jnp.concatenate([rows[r : r + 1] for r in order], axis=0)
    for h in range(2):
        for tile in range(2):
            rows_ref[:, 2 * tile + h] = rows[:, h * half : (h + 1) * half, tile * LANES : (tile + 1) * LANES]
    rest = rows[:, :, 2 * LANES :]
    rows_ref[:, 4] = jnp.concatenate([rest[:, :half], rest[:, half:]], axis=2)
    copy = pltpu.make_async_copy(rows_ref, out_ref, sem)
    copy.start()
    index = lax.axis_index("blk")
    at_last = index == lax.axis_size("blk") - 1
    at_first = index == 0
    first = lax.broadcasted_iota(jnp.int32, (BW, LANES), 1) < LANES // 2
    ends = split(jnp.where(first, x[:, :LANES], x[:, x.shape[1] - LANES :]))
    rims = jnp.dot(jnp.concatenate(ends, axis=1), select, preferred_element_type=jnp.float32)
    lane = lax.broadcasted_iota(jnp.int32, (1, LANES), 1)
    turn_up = (lane < rim) & at_last
    turn_down = (lane >= rim) & at_first
    angle = 2.0 * math.pi / 3.0
    cosine = jnp.where(turn_up | turn_down, math.cos(angle), 1.0)
    sine = jnp.where(turn_up, math.sin(angle), jnp.where(turn_down, -math.sin(angle), 0.0))
    first = rims[2 * CELLS : 3 * CELLS]
    second = rims[3 * CELLS : 4 * CELLS]
    rims = jnp.concatenate(
        [
            rims[: 2 * CELLS],
            cosine * first - sine * second,
            sine * first + cosine * second,
            rims[4 * CELLS :],
        ],
        axis=0,
    ).T
    up_ref[...] = rims[:rim]
    down_ref[...] = rims[rim : 2 * rim]
    return copy


def donors_kernel(
    order, x_ref, src_ref, perm_ref,
    out_ref, up_ref, down_ref, table_ref, select_ref, x_out, rows_ref, sem,
):
    rim = up_ref.shape[0]
    index = lax.axis_index("blk")
    at_last = index == lax.axis_size("blk") - 1
    at_first = index == 0
    sub = lax.broadcasted_iota(jnp.int32, (LANES, LANES), 0)
    lane = lax.broadcasted_iota(jnp.int32, (LANES, LANES), 1)
    wanted = lane[:1]
    target = sub[:, :1]
    for j in range(rim):
        partner = perm_ref[0, j]
        wanted = jnp.where((lane[:1] == j) & at_last, partner, wanted)
        target = jnp.where((sub[:, :1] == j) & at_first, partner, target)
    to_up = (sub == wanted + (LANES - rim)) & (lane < rim)
    to_down = (target + rim == lane) & (sub < rim)
    select = onehot(to_up | to_down)
    select = jnp.concatenate([select, select], axis=0)
    rows = lax.broadcasted_iota(jnp.int32, table_ref.shape, 0)
    table = onehot(rows == src_ref[...])
    copy = send_blocks(
        order, x_ref[...], table, select, out_ref, up_ref, down_ref, rows_ref, sem
    )
    table_ref[...] = table
    select_ref[...] = select
    x_out[...] = x_ref[...]
    copy.wait()


def local_kernel(
    rim, x_ref, nbr_ref, coup_ref, source_ref, out_ref, terms, near, coup, source, sems, source_sem,
    at_start=None, with_ends=None,
):
    slots, blocks = nbr_ref.shape
    chunks = blocks // LANES
    spans = [slice(c * LANES, (c + 1) * LANES) for c in range(chunks)]
    order = [0, chunks - 1, *range(1, chunks - 1)]
    source_copy = pltpu.make_async_copy(source_ref, source, source_sem)
    copies = {}
    for c in order:
        copies[c] = pltpu.make_async_copy(coup_ref.at[:, :, :, spans[c]], coup.at[c], sems.at[c])
        copies[c].start()
        if c == order[0]:
            source_copy.start()
    lane = lax.broadcasted_iota(jnp.int32, (BW, LANES), 1)
    moved = pltpu.roll(x_ref[...], rim, 1)
    head = jnp.where(lane < rim, 0.0, moved[:, :LANES])
    tail = jnp.where(lane < rim, moved[:, :LANES], 0.0)
    terms[:BW], terms[BW:] = split(jnp.concatenate([head, moved[:, LANES:], tail], axis=1))
    rows = lax.broadcasted_iota(jnp.int32, (2 * LANES, LANES), 0)

    pairs = range(0, slots, 2)

    def gather(c, m):
        window = slice(c * LANES, (c + 2) * LANES)
        table = jnp.concatenate(
            [onehot(rows == nbr_ref[i : i + 1, spans[c]] - c * LANES) for i in (m, m + 1)], axis=1
        )
        both = jnp.dot(terms[:, window], table, preferred_element_type=jnp.float32)
        near[c][:, m * LANES : (m + 2) * LANES] = both[:BW] + both[BW:]

    for m in pairs:
        gather(order[0], m)
    if at_start is not None:
        at_start()
    for step, c in enumerate(order):
        copies[c].wait()
        if step == 0:
            source_copy.wait()
        ahead = list(pairs) if step + 1 < chunks else []
        for at in range(0, CELLS, PACK):
            if ahead:
                gather(order[step + 1], ahead.pop(0))
            if with_ends is not None and step in (1, 2) and (at < CELLS // 2) == (step == 1):
                with_ends(at)
            total = [None] * VARS
            for m in range(slots):
                for v in range(VARS):
                    span = slice(v * CELLS + at, v * CELLS + at + PACK)
                    value = near[c][span, m * LANES : (m + 1) * LANES]
                    for u in range(VARS):
                        term = coup[c, m, u, span, :].astype(jnp.float32) * value
                        total[u] = term if total[u] is None else total[u] + term
            for u in range(VARS):
                span = slice(u * CELLS + at, u * CELLS + at + PACK)
                out_ref[span, spans[c]] = source[span, spans[c]] - x_ref[span, spans[c]] + total[u]


def first_local_kernel(
    rim, x_ref, nbr_ref, coup_ref, source_ref, dst_ref, weight_ref,
    out_ref, rimcoup_ref, rimrow_ref, table_ref, weight_out,
    terms, near, coup, source, sems, source_sem,
):
    slots, blocks = nbr_ref.shape
    chunks = blocks // LANES
    fringe = dst_ref.shape[1]
    lane = lax.broadcasted_iota(jnp.int32, (PACK, LANES), 1)
    first = lane < LANES // 2
    masks = [lax.rem(lane + rim + LANES - m * 2 * rim, LANES) < 2 * rim for m in range(slots)]

    def merged(ends, nothing):
        result = nothing
        for m in range(slots):
            both = jnp.where(first, *ends(m))
            if m > 0:
                both = pltpu.roll(both, m * 2 * rim, 1)
            result = jnp.where(masks[m], both, result)
        return result

    def rows(m):
        lower = jnp.broadcast_to(nbr_ref[m : m + 1, :LANES], (PACK, LANES))
        upper = jnp.broadcast_to(nbr_ref[m : m + 1, blocks - LANES :], (PACK, LANES))
        return jnp.where(lower < rim, lower, -LANES), jnp.where(upper >= blocks + rim, upper - blocks, -LANES)

    def tables():
        rimrow_ref[...] = merged(rows, jnp.full((PACK, LANES), -LANES, jnp.int32))
        weight_out[...] = weight_ref[...]
        targets = jnp.broadcast_to(dst_ref[...], (LANES, fringe)).T
        for c in range(chunks):
            table_ref[:, c * LANES : (c + 1) * LANES] = onehot(targets == lane[:1] + c * LANES)

    def rim_coupling(at):
        for u in range(VARS):
            for v in range(VARS):
                span = slice(v * CELLS + at, v * CELLS + at + PACK)
                rimcoup_ref[u, span, :] = merged(
                    lambda m: (coup[0, m, u, span, :], coup[chunks - 1, m, u, span, :]),
                    jnp.zeros((PACK, LANES), jnp.bfloat16),
                )

    local_kernel(
        rim, x_ref, nbr_ref, coup_ref, source_ref, out_ref, terms, near, coup, source, sems, source_sem,
        tables, rim_coupling,
    )


def full_residual(order, local_ref, inc_ref, lower_ref, upper_ref, table_ref, weight_ref, rimcoup_ref, rimrow_ref):
    rim = lower_ref.shape[0]
    blocks = local_ref.shape[1]
    rims = jnp.concatenate(
        [lower_ref[...], upper_ref[...], jnp.zeros((LANES - 2 * rim, BW), jnp.float32)], axis=0
    ).T
    high, low = split(rims)
    low = pltpu.roll(low.astype(jnp.float32), 2 * rim, 1)
    rims = (high.astype(jnp.float32) + low).astype(jnp.bfloat16)
    sub = lax.broadcasted_iota(jnp.int32, (LANES, LANES), 0)
    row = rimrow_ref[:1]
    reads = onehot((sub == row) | (sub == row + 2 * rim))
    near = jnp.dot(rims, reads, preferred_element_type=jnp.float32)
    edge = []
    for u in range(VARS):
        total = None
        for v in range(VARS):
            span = slice(v * CELLS, (v + 1) * CELLS)
            term = rimcoup_ref[u, span, :].astype(jnp.float32) * near[span]
            total = term if total is None else total + term
        edge.append(total)
    edge = jnp.concatenate(edge, axis=0)
    shift = LANES // 2
    while shift >= 2 * rim:
        edge = edge + pltpu.roll(edge, shift, 1)
        shift //= 2
    lane = lax.broadcasted_iota(jnp.int32, (BW, LANES), 1)
    inc = jnp.concatenate([inc_ref[i : i + 1] for i in np.argsort(order).tolist()], axis=0)
    rest = inc[:, 4]
    rest = jnp.concatenate([rest[:, :, :CELLS], rest[:, :, CELLS:]], axis=1).reshape(-1, CELLS)
    fringe = [inc[:, 0:2].reshape(-1, LANES).T, inc[:, 2:4].reshape(-1, LANES).T, rest.T]
    total = local_ref[...] + pick(jnp.concatenate(fringe, axis=0) * weight_ref[...], table_ref[...])
    lower = total[:, :LANES] + jnp.where(lane < rim, edge, 0.0)
    upper = total[:, blocks - LANES :] + jnp.where(lane >= LANES - rim, edge, 0.0)
    return jnp.concatenate([lower, total[:, LANES : blocks - LANES], upper], axis=1)


def precondition(diag_ref, resid_ref, u, at):
    total = None
    for v in range(VARS):
        span = pl.ds(v * CELLS + at, PACK)
        term = diag_ref[u, span, :].astype(jnp.float32) * resid_ref[span, :]
        total = term if total is None else total + term
    return total


def lane_sums(resid):
    square = jnp.sum(resid * resid, axis=0, keepdims=True)
    return sum(square[:, i : i + LANES] for i in range(0, square.shape[1], LANES))


def advance_kernel(
    order, local_ref, inc_ref, lower_ref, upper_ref, across_ref, weight_ref, rimcoup_ref, rimrow_ref,
    diag_ref, x_ref, table_ref, select_ref,
    next_ref, norm_ref, out_ref, up_ref, down_ref, resid, diag, diag_sem, rows_ref, sem,
):
    fetch = pltpu.make_async_copy(diag_ref, diag, diag_sem)
    fetch.start()
    resid[...] = full_residual(
        order, local_ref, inc_ref, lower_ref, upper_ref, across_ref, weight_ref, rimcoup_ref, rimrow_ref
    )
    fetch.wait()
    for u in range(VARS):
        for at in range(0, CELLS, PACK):
            total = None
            for v in range(VARS):
                span = slice(v * CELLS + at, v * CELLS + at + PACK)
                term = diag[u, span].astype(jnp.float32) * resid[span]
                total = term if total is None else total + term
            span = slice(u * CELLS + at, u * CELLS + at + PACK)
            next_ref[span, :] = x_ref[span, :] + STEP_CFL * total
    copy = send_blocks(
        order, next_ref[...], table_ref[...], select_ref[...], out_ref, up_ref, down_ref, rows_ref, sem
    )
    norm_ref[...] = lane_sums(resid[...])
    copy.wait()


def residual_kernel(
    order, local_ref, inc_ref, lower_ref, upper_ref, across_ref, weight_ref, rimcoup_ref, rimrow_ref, norm_ref,
    resid_ref, sums_ref,
):
    resid = full_residual(
        order, local_ref, inc_ref, lower_ref, upper_ref, across_ref, weight_ref, rimcoup_ref, rimrow_ref
    )
    resid_ref[...] = resid
    both = jnp.concatenate([norm_ref[...], lane_sums(resid)], axis=0)
    sums_ref[...] = jnp.broadcast_to(both[None], sums_ref.shape)


def direction_kernel(diag_ref, resid_ref, out_ref, resid_out):
    resid_out[...] = resid_ref[...]

    def cells(part, carry):
        at = pl.multiple_of(part * PACK, PACK)
        for u in range(VARS):
            out_ref[pl.ds(u * CELLS + at, PACK), :] = precondition(diag_ref, resid_ref, u, at)
        return carry

    lax.fori_loop(0, CELLS // PACK, cells, 0)


def finish_kernel(entries, sums_ref, x_ref, update_ref, out_ref):
    sums = jnp.sum(jnp.sum(sums_ref[...], axis=0), axis=1, keepdims=True) / entries + 1e-06
    cfl = STEP_CFL * jnp.sqrt(sums[0:1] / sums[1:2])
    out_ref[...] = x_ref[...] + cfl * update_ref[...]


VMEM = pl.BlockSpec(memory_space=pltpu.VMEM)
SMEM = pl.BlockSpec(memory_space=pltpu.SMEM)


def f32(*shape):
    return jax.ShapeDtypeStruct(shape, jnp.float32)


def bf16(*shape):
    return jax.ShapeDtypeStruct(shape, jnp.bfloat16)


def call(kernel, in_specs, out_shape, flops, moved, **more):
    many = isinstance(out_shape, (list, tuple))
    return pl.pallas_call(
        kernel,
        in_specs=in_specs,
        out_specs=more.pop("out_specs", [VMEM] * len(out_shape) if many else VMEM),
        out_shape=out_shape,
        compiler_params=pltpu.CompilerParams(vmem_limit_bytes=VMEM_LIMIT),
        cost_estimate=pl.CostEstimate(flops=flops, bytes_accessed=moved, transcendentals=0),
        **more,
    )


def message_order(bodies, peers):
    middle = peers // 2
    far_first = sorted(range(peers), key=lambda k: -abs(2 * k + 1 - peers))
    order = [b * peers + k for b in range(bodies) for k in far_first]
    order.remove(middle)
    return [middle, *order]


def shards(
    psi_init, source, coupling, diag_inv, neighbours, seam_perm, fringe_src, fringe_dst, fringe_weight
):
    blocks = psi_init.shape[0]
    slots = neighbours.shape[1]
    rim = seam_perm.shape[1]
    fringe = fringe_src.shape[1]
    peers = lax.axis_size("blk")
    devices = lax.axis_size("body") * peers
    order = message_order(devices // peers, peers)
    up = [(i, (i + 1) % peers) for i in range(peers)]
    down = [(j, i) for i, j in up]
    here = functools.partial(pltpu.with_memory_space_constraint, memory_space=pltpu.HBM)
    x = here(psi_init.T)
    source_t = here(source.T)
    coup = here(coupling.transpose(1, 2, 3, 0))
    diag = here(diag_inv.transpose(1, 2, 0))
    nbr = here(neighbours.T)
    state = f32(BW, blocks)
    hbm = pl.BlockSpec(memory_space=pltpu.HBM)
    message = (devices, BW * fringe // devices // (rim // 2 * LANES), rim // 2, LANES)
    sent = [f32(*message), f32(rim, BW), f32(rim, BW)]
    rows_scratch = [pltpu.VMEM(message, jnp.float32), pltpu.SemaphoreType.DMA]
    size = 4 * BW * blocks

    donors = call(
        functools.partial(donors_kernel, order),
        [VMEM, VMEM, SMEM],
        sent + [bf16(blocks, fringe), bf16(2 * LANES, LANES), state],
        4 * BW * blocks * fringe,
        2 * size,
        out_specs=[hbm] + [VMEM] * 5,
        scratch_shapes=rows_scratch,
    )
    chunks = blocks // LANES
    scratch = [
        pltpu.VMEM((2 * BW, blocks + LANES), jnp.bfloat16),
        [pltpu.VMEM((BW, slots * LANES), jnp.float32)] * chunks,
        pltpu.VMEM((chunks, slots, VARS, BW, LANES), jnp.bfloat16),
        pltpu.VMEM((BW, blocks), jnp.float32),
        pltpu.SemaphoreType.DMA((chunks,)),
        pltpu.SemaphoreType.DMA,
    ]
    local_more = dict(
        flops=4 * BW * 2 * LANES * slots * blocks,
        moved=coup.size * 2 + 4 * size,
        scratch_shapes=scratch,
    )
    first_local = call(
        functools.partial(first_local_kernel, rim),
        [VMEM, VMEM, hbm, hbm, VMEM, VMEM],
        [
            state,
            bf16(VARS, BW, LANES),
            jax.ShapeDtypeStruct((PACK, LANES), jnp.int32),
            bf16(fringe, blocks),
            f32(1, fringe),
        ],
        **local_more,
    )
    local = call(functools.partial(local_kernel, rim), [VMEM, VMEM, hbm, hbm], state, **local_more)
    advance = call(
        functools.partial(advance_kernel, order),
        [VMEM] * 8 + [hbm] + [VMEM] * 3,
        [state, f32(1, LANES)] + sent,
        8 * BW * blocks * fringe,
        diag.size * 2 + 4 * size,
        out_specs=[VMEM, VMEM, hbm, VMEM, VMEM],
        scratch_shapes=[
            pltpu.VMEM((BW, blocks), jnp.float32),
            pltpu.VMEM((VARS, BW, blocks), jnp.bfloat16),
            pltpu.SemaphoreType.DMA,
        ]
        + rows_scratch,
    )
    residual = call(
        functools.partial(residual_kernel, order),
        [VMEM] * 9,
        [state, f32(devices, 2, LANES)],
        4 * BW * blocks * fringe,
        3 * size,
    )
    direction = call(
        direction_kernel, [VMEM] * 2, [state, state], diag.size * 2, diag.size * 2 + 2 * size
    )
    finish = call(
        functools.partial(finish_kernel, float(blocks * devices * BW)),
        [VMEM] * 3,
        state,
        2 * BW * blocks,
        3 * size,
    )

    everyone = functools.partial(
        lax.all_to_all,
        axis_name=("body", "blk"),
        split_axis=0,
        concat_axis=0,
        tiled=True,
        axis_index_groups=[order],
    )

    def exchange(rows, to_up, to_down):
        rows = everyone(rows)
        return rows, lax.ppermute(to_up, "blk", up), lax.ppermute(to_down, "blk", down)

    *out, table, select, x_here = donors(x, here(fringe_src), here(seam_perm))
    arrived = exchange(*out)
    part, rimcoup, rimrow, across, weight = first_local(
        x_here, nbr, coup, source_t, here(fringe_dst), here(fringe_weight)
    )
    across = (across, weight, rimcoup, rimrow)
    x, norm, *out = advance(part, *arrived, *across, diag, x_here, table, select)
    arrived = exchange(*out)
    part = local(x, nbr, coup, source_t)
    resid, sums = residual(part, *arrived, *across, norm)
    sums = everyone(sums)
    update, resid = direction(diag, resid)
    x = finish(sums, x, update)
    return (x.T, resid.T)


def solution(mesh):
    return jax.shard_map(
        shards,
        mesh=mesh,
        in_specs=(
            P(("body", "blk"), None),
            P(("body", "blk"), None),
            P(("body", "blk"), None, None, None),
            P(("body", "blk"), None, None),
            P(("body", "blk"), None),
            P("body", None),
            P(("body", "blk"), None),
            P(("body", "blk"), None),
            P(("body", "blk"), None),
        ),
        out_specs=(P(("body", "blk"), None), P(("body", "blk"), None)),
        check_vma=False,
    )
```

```python
import functools
import math

import jax
import jax.numpy as jnp
import numpy as np
from jax import lax
from jax.experimental import pallas as pl
from jax.experimental.pallas import tpu as pltpu
from jax.sharding import PartitionSpec as P

CELLS = 64
VARS = 5
BW = 320
STEP_CFL = 0.5
LANES = 128
PACK = 16
VMEM_LIMIT = 32 * 1024 * 1024


def split(x):
    high = x.astype(jnp.bfloat16)
    return high, (x - high.astype(jnp.float32)).astype(jnp.bfloat16)


def onehot(mask):
    return jnp.where(mask, 1.0, 0.0).astype(jnp.bfloat16)


def pick(x, table):
    both = jnp.dot(jnp.concatenate(split(x), axis=0), table, preferred_element_type=jnp.float32)
    return both[: x.shape[0]] + both[x.shape[0] :]


def send_blocks(order, x, table, select, out_ref, up_ref, down_ref, rows_ref, sem):
    rim = up_ref.shape[0]
    half = rows_ref.shape[2]
    rows = pick(x, table).T.reshape(rows_ref.shape[0], 2 * half, BW)
    rows = jnp.concatenate([rows[r : r + 1] for r in order], axis=0)
    for h in range(2):
        for tile in range(2):
            rows_ref[:, 2 * tile + h] = rows[:, h * half : (h + 1) * half, tile * LANES : (tile + 1) * LANES]
    rest = rows[:, :, 2 * LANES :]
    rows_ref[:, 4] = jnp.concatenate([rest[:, :half], rest[:, half:]], axis=2)
    copy = pltpu.make_async_copy(rows_ref, out_ref, sem)
    copy.start()
    index = lax.axis_index("blk")
    at_last = index == lax.axis_size("blk") - 1
    at_first = index == 0
    first = lax.broadcasted_iota(jnp.int32, (BW, LANES), 1) < LANES // 2
    ends = split(jnp.where(first, x[:, :LANES], x[:, x.shape[1] - LANES :]))
    rims = jnp.dot(jnp.concatenate(ends, axis=1), select, preferred_element_type=jnp.float32)
    lane = lax.broadcasted_iota(jnp.int32, (1, LANES), 1)
    turn_up = (lane < rim) & at_last
    turn_down = (lane >= rim) & at_first
    angle = 2.0 * math.pi / 3.0
    cosine = jnp.where(turn_up | turn_down, math.cos(angle), 1.0)
    sine = jnp.where(turn_up, math.sin(angle), jnp.where(turn_down, -math.sin(angle), 0.0))
    first = rims[2 * CELLS : 3 * CELLS]
    second = rims[3 * CELLS : 4 * CELLS]
    rims = jnp.concatenate(
        [
            rims[: 2 * CELLS],
            cosine * first - sine * second,
            sine * first + cosine * second,
            rims[4 * CELLS :],
        ],
        axis=0,
    ).T
    up_ref[...] = rims[:rim]
    down_ref[...] = rims[rim : 2 * rim]
    return copy


def donors_kernel(
    order, x_ref, src_ref, perm_ref,
    out_ref, up_ref, down_ref, table_ref, select_ref, x_out, rows_ref, sem,
):
    rim = up_ref.shape[0]
    index = lax.axis_index("blk")
    at_last = index == lax.axis_size("blk") - 1
    at_first = index == 0
    sub = lax.broadcasted_iota(jnp.int32, (LANES, LANES), 0)
    lane = lax.broadcasted_iota(jnp.int32, (LANES, LANES), 1)
    wanted = lane[:1]
    target = sub[:, :1]
    for j in range(rim):
        partner = perm_ref[0, j]
        wanted = jnp.where((lane[:1] == j) & at_last, partner, wanted)
        target = jnp.where((sub[:, :1] == j) & at_first, partner, target)
    to_up = (sub == wanted + (LANES - rim)) & (lane < rim)
    to_down = (target + rim == lane) & (sub < rim)
    select = onehot(to_up | to_down)
    select = jnp.concatenate([select, select], axis=0)
    rows = lax.broadcasted_iota(jnp.int32, table_ref.shape, 0)
    table = onehot(rows == src_ref[...])
    copy = send_blocks(
        order, x_ref[...], table, select, out_ref, up_ref, down_ref, rows_ref, sem
    )
    table_ref[...] = table
    select_ref[...] = select
    x_out[...] = x_ref[...]
    copy.wait()


def local_kernel(
    rim, x_ref, nbr_ref, coup_ref, source_ref, out_ref, terms, near, coup, source, sems, source_sem,
    at_start=None, with_ends=None,
):
    slots, blocks = nbr_ref.shape
    chunks = blocks // LANES
    spans = [slice(c * LANES, (c + 1) * LANES) for c in range(chunks)]
    order = [0, chunks - 1, *range(1, chunks - 1)]
    source_copy = pltpu.make_async_copy(source_ref, source, source_sem)
    copies = {}
    for c in order:
        copies[c] = pltpu.make_async_copy(coup_ref.at[:, :, :, spans[c]], coup.at[c], sems.at[c])
        copies[c].start()
        if c == order[0]:
            source_copy.start()
    lane = lax.broadcasted_iota(jnp.int32, (BW, LANES), 1)
    moved = pltpu.roll(x_ref[...], rim, 1)
    head = jnp.where(lane < rim, 0.0, moved[:, :LANES])
    tail = jnp.where(lane < rim, moved[:, :LANES], 0.0)
    terms[:BW], terms[BW:] = split(jnp.concatenate([head, moved[:, LANES:], tail], axis=1))
    rows = lax.broadcasted_iota(jnp.int32, (2 * LANES, LANES), 0)

    pairs = range(0, slots, 2)

    def gather(c, m):
        window = slice(c * LANES, (c + 2) * LANES)
        table = jnp.concatenate(
            [onehot(rows == nbr_ref[i : i + 1, spans[c]] - c * LANES) for i in (m, m + 1)], axis=1
        )
        both = jnp.dot(terms[:, window], table, preferred_element_type=jnp.float32)
        near[c][:, m * LANES : (m + 2) * LANES] = both[:BW] + both[BW:]

    for m in pairs:
        gather(order[0], m)
    if at_start is not None:
        at_start()
    for step, c in enumerate(order):
        copies[c].wait()
        if step == 0:
            source_copy.wait()
        ahead = list(pairs) if step + 1 < chunks else []
        for at in range(0, CELLS, PACK):
            if ahead:
                gather(order[step + 1], ahead.pop(0))
            if with_ends is not None and step in (1, 2) and (at < CELLS // 2) == (step == 1):
                with_ends(at)
            total = [None] * VARS
            for m in range(slots):
                for v in range(VARS):
                    span = slice(v * CELLS + at, v * CELLS + at + PACK)
                    value = near[c][span, m * LANES : (m + 1) * LANES]
                    for u in range(VARS):
                        term = coup[c, m, u, span, :].astype(jnp.float32) * value
                        total[u] = term if total[u] is None else total[u] + term
            for u in range(VARS):
                span = slice(u * CELLS + at, u * CELLS + at + PACK)
                out_ref[span, spans[c]] = source[span, spans[c]] - x_ref[span, spans[c]] + total[u]


def first_local_kernel(
    rim, x_ref, nbr_ref, coup_ref, source_ref, dst_ref, weight_ref,
    out_ref, rimcoup_ref, rimrow_ref, table_ref, weight_out,
    terms, near, coup, source, sems, source_sem,
):
    slots, blocks = nbr_ref.shape
    chunks = blocks // LANES
    fringe = dst_ref.shape[1]
    lane = lax.broadcasted_iota(jnp.int32, (PACK, LANES), 1)
    first = lane < LANES // 2
    masks = [lax.rem(lane + rim + LANES - m * 2 * rim, LANES) < 2 * rim for m in range(slots)]

    def merged(ends, nothing):
        result = nothing
        for m in range(slots):
            both = jnp.where(first, *ends(m))
            if m > 0:
                both = pltpu.roll(both, m * 2 * rim, 1)
            result = jnp.where(masks[m], both, result)
        return result

    def rows(m):
        lower = jnp.broadcast_to(nbr_ref[m : m + 1, :LANES], (PACK, LANES))
        upper = jnp.broadcast_to(nbr_ref[m : m + 1, blocks - LANES :], (PACK, LANES))
        return jnp.where(lower < rim, lower, -LANES), jnp.where(upper >= blocks + rim, upper - blocks, -LANES)

    def tables():
        rimrow_ref[...] = merged(rows, jnp.full((PACK, LANES), -LANES, jnp.int32))
        weight_out[...] = weight_ref[...]
        targets = jnp.broadcast_to(dst_ref[...], (LANES, fringe)).T
        for c in range(chunks):
            table_ref[:, c * LANES : (c + 1) * LANES] = onehot(targets == lane[:1] + c * LANES)

    def rim_coupling(at):
        for u in range(VARS):
            for v in range(VARS):
                span = slice(v * CELLS + at, v * CELLS + at + PACK)
                rimcoup_ref[u, span, :] = merged(
                    lambda m: (coup[0, m, u, span, :], coup[chunks - 1, m, u, span, :]),
                    jnp.zeros((PACK, LANES), jnp.bfloat16),
                )

    local_kernel(
        rim, x_ref, nbr_ref, coup_ref, source_ref, out_ref, terms, near, coup, source, sems, source_sem,
        tables, rim_coupling,
    )


def full_residual(order, local_ref, inc_ref, lower_ref, upper_ref, table_ref, weight_ref, rimcoup_ref, rimrow_ref):
    rim = lower_ref.shape[0]
    blocks = local_ref.shape[1]
    rims = jnp.concatenate(
        [lower_ref[...], upper_ref[...], jnp.zeros((LANES - 2 * rim, BW), jnp.float32)], axis=0
    ).T
    high, low = split(rims)
    low = pltpu.roll(low.astype(jnp.float32), 2 * rim, 1)
    rims = (high.astype(jnp.float32) + low).astype(jnp.bfloat16)
    sub = lax.broadcasted_iota(jnp.int32, (LANES, LANES), 0)
    row = rimrow_ref[:1]
    reads = onehot((sub == row) | (sub == row + 2 * rim))
    near = jnp.dot(rims, reads, preferred_element_type=jnp.float32)
    edge = []
    for u in range(VARS):
        total = None
        for v in range(VARS):
            span = slice(v * CELLS, (v + 1) * CELLS)
            term = rimcoup_ref[u, span, :].astype(jnp.float32) * near[span]
            total = term if total is None else total + term
        edge.append(total)
    edge = jnp.concatenate(edge, axis=0)
    shift = LANES // 2
    while shift >= 2 * rim:
        edge = edge + pltpu.roll(edge, shift, 1)
        shift //= 2
    lane = lax.broadcasted_iota(jnp.int32, (BW, LANES), 1)
    inc = jnp.concatenate([inc_ref[i : i + 1] for i in np.argsort(order).tolist()], axis=0)
    rest = inc[:, 4]
    rest = jnp.concatenate([rest[:, :, :CELLS], rest[:, :, CELLS:]], axis=1).reshape(-1, CELLS)
    fringe = [inc[:, 0:2].reshape(-1, LANES).T, inc[:, 2:4].reshape(-1, LANES).T, rest.T]
    total = local_ref[...] + pick(jnp.concatenate(fringe, axis=0) * weight_ref[...], table_ref[...])
    lower = total[:, :LANES] + jnp.where(lane < rim, edge, 0.0)
    upper = total[:, blocks - LANES :] + jnp.where(lane >= LANES - rim, edge, 0.0)
    return jnp.concatenate([lower, total[:, LANES : blocks - LANES], upper], axis=1)


def precondition(diag_ref, resid_ref, u, at):
    total = None
    for v in range(VARS):
        span = pl.ds(v * CELLS + at, PACK)
        term = diag_ref[u, span, :].astype(jnp.float32) * resid_ref[span, :]
        total = term if total is None else total + term
    return total


def lane_sums(resid):
    square = jnp.sum(resid * resid, axis=0, keepdims=True)
    return sum(square[:, i : i + LANES] for i in range(0, square.shape[1], LANES))


def advance_kernel(
    order, local_ref, inc_ref, lower_ref, upper_ref, across_ref, weight_ref, rimcoup_ref, rimrow_ref,
    diag_ref, x_ref, table_ref, select_ref,
    next_ref, norm_ref, out_ref, up_ref, down_ref, resid, diag, diag_sem, rows_ref, sem,
):
    fetch = pltpu.make_async_copy(diag_ref, diag, diag_sem)
    fetch.start()
    resid[...] = full_residual(
        order, local_ref, inc_ref, lower_ref, upper_ref, across_ref, weight_ref, rimcoup_ref, rimrow_ref
    )
    fetch.wait()
    for u in range(VARS):
        for at in range(0, CELLS, PACK):
            total = None
            for v in range(VARS):
                span = slice(v * CELLS + at, v * CELLS + at + PACK)
                term = diag[u, span].astype(jnp.float32) * resid[span]
                total = term if total is None else total + term
            span = slice(u * CELLS + at, u * CELLS + at + PACK)
            next_ref[span, :] = x_ref[span, :] + STEP_CFL * total
    copy = send_blocks(
        order, next_ref[...], table_ref[...], select_ref[...], out_ref, up_ref, down_ref, rows_ref, sem
    )
    norm_ref[...] = lane_sums(resid[...])
    copy.wait()


def residual_kernel(
    order, local_ref, inc_ref, lower_ref, upper_ref, across_ref, weight_ref, rimcoup_ref, rimrow_ref, norm_ref,
    resid_ref, sums_ref,
):
    resid = full_residual(
        order, local_ref, inc_ref, lower_ref, upper_ref, across_ref, weight_ref, rimcoup_ref, rimrow_ref
    )
    resid_ref[...] = resid
    both = jnp.concatenate([norm_ref[...], lane_sums(resid)], axis=0)
    sums_ref[...] = jnp.broadcast_to(both[None], sums_ref.shape)


def direction_kernel(diag_ref, resid_ref, out_ref, resid_out):
    resid_out[...] = resid_ref[...]

    def cells(part, carry):
        at = pl.multiple_of(part * PACK, PACK)
        for u in range(VARS):
            out_ref[pl.ds(u * CELLS + at, PACK), :] = precondition(diag_ref, resid_ref, u, at)
        return carry

    lax.fori_loop(0, CELLS // PACK, cells, 0)


def finish_kernel(entries, sums_ref, x_ref, update_ref, out_ref):
    sums = jnp.sum(jnp.sum(sums_ref[...], axis=0), axis=1, keepdims=True) / entries + 1e-06
    cfl = STEP_CFL * jnp.sqrt(sums[0:1] / sums[1:2])
    out_ref[...] = x_ref[...] + cfl * update_ref[...]


VMEM = pl.BlockSpec(memory_space=pltpu.VMEM)
SMEM = pl.BlockSpec(memory_space=pltpu.SMEM)


def f32(*shape):
    return jax.ShapeDtypeStruct(shape, jnp.float32)


def bf16(*shape):
    return jax.ShapeDtypeStruct(shape, jnp.bfloat16)


def call(kernel, in_specs, out_shape, flops, moved, **more):
    many = isinstance(out_shape, (list, tuple))
    return pl.pallas_call(
        kernel,
        in_specs=in_specs,
        out_specs=more.pop("out_specs", [VMEM] * len(out_shape) if many else VMEM),
        out_shape=out_shape,
        compiler_params=pltpu.CompilerParams(vmem_limit_bytes=VMEM_LIMIT),
        cost_estimate=pl.CostEstimate(flops=flops, bytes_accessed=moved, transcendentals=0),
        **more,
    )


def message_order(bodies, peers):
    return list(reversed(range(bodies * peers)))


def shards(
    psi_init, source, coupling, diag_inv, neighbours, seam_perm, fringe_src, fringe_dst, fringe_weight
):
    blocks = psi_init.shape[0]
    slots = neighbours.shape[1]
    rim = seam_perm.shape[1]
    fringe = fringe_src.shape[1]
    peers = lax.axis_size("blk")
    devices = lax.axis_size("body") * peers
    order = message_order(devices // peers, peers)
    up = [(i, (i + 1) % peers) for i in range(peers)]
    down = [(j, i) for i, j in up]
    here = functools.partial(pltpu.with_memory_space_constraint, memory_space=pltpu.HBM)
    x = here(psi_init.T)
    source_t = here(source.T)
    coup = here(coupling.transpose(1, 2, 3, 0))
    diag = here(diag_inv.transpose(1, 2, 0))
    nbr = here(neighbours.T)
    state = f32(BW, blocks)
    hbm = pl.BlockSpec(memory_space=pltpu.HBM)
    message = (devices, BW * fringe // devices // (rim // 2 * LANES), rim // 2, LANES)
    sent = [f32(*message), f32(rim, BW), f32(rim, BW)]
    rows_scratch = [pltpu.VMEM(message, jnp.float32), pltpu.SemaphoreType.DMA]
    size = 4 * BW * blocks

    donors = call(
        functools.partial(donors_kernel, order),
        [VMEM, VMEM, SMEM],
        sent + [bf16(blocks, fringe), bf16(2 * LANES, LANES), state],
        4 * BW * blocks * fringe,
        2 * size,
        out_specs=[hbm] + [VMEM] * 5,
        scratch_shapes=rows_scratch,
    )
    chunks = blocks // LANES
    scratch = [
        pltpu.VMEM((2 * BW, blocks + LANES), jnp.bfloat16),
        [pltpu.VMEM((BW, slots * LANES), jnp.float32)] * chunks,
        pltpu.VMEM((chunks, slots, VARS, BW, LANES), jnp.bfloat16),
        pltpu.VMEM((BW, blocks), jnp.float32),
        pltpu.SemaphoreType.DMA((chunks,)),
        pltpu.SemaphoreType.DMA,
    ]
    local_more = dict(
        flops=4 * BW * 2 * LANES * slots * blocks,
        moved=coup.size * 2 + 4 * size,
        scratch_shapes=scratch,
    )
    first_local = call(
        functools.partial(first_local_kernel, rim),
        [VMEM, VMEM, hbm, hbm, VMEM, VMEM],
        [
            state,
            bf16(VARS, BW, LANES),
            jax.ShapeDtypeStruct((PACK, LANES), jnp.int32),
            bf16(fringe, blocks),
            f32(1, fringe),
        ],
        **local_more,
    )
    local = call(functools.partial(local_kernel, rim), [VMEM, VMEM, hbm, hbm], state, **local_more)
    advance = call(
        functools.partial(advance_kernel, order),
        [VMEM] * 8 + [hbm] + [VMEM] * 3,
        [state, f32(1, LANES)] + sent,
        8 * BW * blocks * fringe,
        diag.size * 2 + 4 * size,
        out_specs=[VMEM, VMEM, hbm, VMEM, VMEM],
        scratch_shapes=[
            pltpu.VMEM((BW, blocks), jnp.float32),
            pltpu.VMEM((VARS, BW, blocks), jnp.bfloat16),
            pltpu.SemaphoreType.DMA,
        ]
        + rows_scratch,
    )
    residual = call(
        functools.partial(residual_kernel, order),
        [VMEM] * 9,
        [state, f32(devices, 2, LANES)],
        4 * BW * blocks * fringe,
        3 * size,
    )
    direction = call(
        direction_kernel, [VMEM] * 2, [state, state], diag.size * 2, diag.size * 2 + 2 * size
    )
    finish = call(
        functools.partial(finish_kernel, float(blocks * devices * BW)),
        [VMEM] * 3,
        state,
        2 * BW * blocks,
        3 * size,
    )

    everyone = functools.partial(
        lax.all_to_all,
        axis_name=("body", "blk"),
        split_axis=0,
        concat_axis=0,
        tiled=True,
        axis_index_groups=[order],
    )

    def exchange(rows, to_up, to_down):
        rows = everyone(rows)
        return rows, lax.ppermute(to_up, "blk", up), lax.ppermute(to_down, "blk", down)

    *out, table, select, x_here = donors(x, here(fringe_src), here(seam_perm))
    arrived = exchange(*out)
    part, rimcoup, rimrow, across, weight = first_local(
        x_here, nbr, coup, source_t, here(fringe_dst), here(fringe_weight)
    )
    across = (across, weight, rimcoup, rimrow)
    x, norm, *out = advance(part, *arrived, *across, diag, x_here, table, select)
    arrived = exchange(*out)
    part = local(x, nbr, coup, source_t)
    resid, sums = residual(part, *arrived, *across, norm)
    sums = everyone(sums)
    update, resid = direction(diag, resid)
    x = finish(sums, x, update)
    return (x.T, resid.T)


def solution(mesh):
    return jax.shard_map(
        shards,
        mesh=mesh,
        in_specs=(
            P(("body", "blk"), None),
            P(("body", "blk"), None),
            P(("body", "blk"), None, None, None),
            P(("body", "blk"), None, None),
            P(("body", "blk"), None),
            P("body", None),
            P(("body", "blk"), None),
            P(("body", "blk"), None),
            P(("body", "blk"), None),
        ),
        out_specs=(P(("body", "blk"), None), P(("body", "blk"), None)),
        check_vma=False,
    )
```

```python
import functools
import math

import jax
import jax.numpy as jnp
import numpy as np
from jax import lax
from jax.experimental import pallas as pl
from jax.experimental.pallas import tpu as pltpu
from jax.sharding import PartitionSpec as P

CELLS = 64
VARS = 5
BW = 320
STEP_CFL = 0.5
LANES = 128
PACK = 16
VMEM_LIMIT = 32 * 1024 * 1024


def split(x):
    high = x.astype(jnp.bfloat16)
    return high, (x - high.astype(jnp.float32)).astype(jnp.bfloat16)


def onehot(mask):
    return jnp.where(mask, 1.0, 0.0).astype(jnp.bfloat16)


def pick(x, table):
    both = jnp.dot(jnp.concatenate(split(x), axis=0), table, preferred_element_type=jnp.float32)
    return both[: x.shape[0]] + both[x.shape[0] :]


def send_blocks(order, x, table, select, out_ref, up_ref, down_ref, rows_ref, sem):
    rim = up_ref.shape[0]
    half = rows_ref.shape[2]
    rows = pick(x, table).T.reshape(rows_ref.shape[0], 2 * half, BW)
    rows = jnp.concatenate([rows[r : r + 1] for r in order], axis=0)
    for h in range(2):
        for tile in range(2):
            rows_ref[:, 2 * tile + h] = rows[:, h * half : (h + 1) * half, tile * LANES : (tile + 1) * LANES]
    rest = rows[:, :, 2 * LANES :]
    rows_ref[:, 4] = jnp.concatenate([rest[:, :half], rest[:, half:]], axis=2)
    copy = pltpu.make_async_copy(rows_ref, out_ref, sem)
    copy.start()
    index = lax.axis_index("blk")
    at_last = index == lax.axis_size("blk") - 1
    at_first = index == 0
    first = lax.broadcasted_iota(jnp.int32, (BW, LANES), 1) < LANES // 2
    ends = split(jnp.where(first, x[:, :LANES], x[:, x.shape[1] - LANES :]))
    rims = jnp.dot(jnp.concatenate(ends, axis=1), select, preferred_element_type=jnp.float32)
    lane = lax.broadcasted_iota(jnp.int32, (1, LANES), 1)
    turn_up = (lane < rim) & at_last
    turn_down = (lane >= rim) & at_first
    angle = 2.0 * math.pi / 3.0
    cosine = jnp.where(turn_up | turn_down, math.cos(angle), 1.0)
    sine = jnp.where(turn_up, math.sin(angle), jnp.where(turn_down, -math.sin(angle), 0.0))
    first = rims[2 * CELLS : 3 * CELLS]
    second = rims[3 * CELLS : 4 * CELLS]
    rims = jnp.concatenate(
        [
            rims[: 2 * CELLS],
            cosine * first - sine * second,
            sine * first + cosine * second,
            rims[4 * CELLS :],
        ],
        axis=0,
    ).T
    up_ref[...] = rims[:rim]
    down_ref[...] = rims[rim : 2 * rim]
    return copy


def donors_kernel(
    order, x_ref, src_ref, perm_ref,
    out_ref, up_ref, down_ref, table_ref, select_ref, x_out, rows_ref, sem,
):
    rim = up_ref.shape[0]
    index = lax.axis_index("blk")
    at_last = index == lax.axis_size("blk") - 1
    at_first = index == 0
    sub = lax.broadcasted_iota(jnp.int32, (LANES, LANES), 0)
    lane = lax.broadcasted_iota(jnp.int32, (LANES, LANES), 1)
    wanted = lane[:1]
    target = sub[:, :1]
    for j in range(rim):
        partner = perm_ref[0, j]
        wanted = jnp.where((lane[:1] == j) & at_last, partner, wanted)
        target = jnp.where((sub[:, :1] == j) & at_first, partner, target)
    to_up = (sub == wanted + (LANES - rim)) & (lane < rim)
    to_down = (target + rim == lane) & (sub < rim)
    select = onehot(to_up | to_down)
    select = jnp.concatenate([select, select], axis=0)
    rows = lax.broadcasted_iota(jnp.int32, table_ref.shape, 0)
    table = onehot(rows == src_ref[...])
    copy = send_blocks(
        order, x_ref[...], table, select, out_ref, up_ref, down_ref, rows_ref, sem
    )
    table_ref[...] = table
    select_ref[...] = select
    x_out[...] = x_ref[...]
    copy.wait()


def local_kernel(
    rim, x_ref, nbr_ref, coup_ref, source_ref, out_ref, terms, near, coup, source, sems, source_sem,
    at_start=None, with_ends=None,
):
    slots, blocks = nbr_ref.shape
    chunks = blocks // LANES
    spans = [slice(c * LANES, (c + 1) * LANES) for c in range(chunks)]
    order = [0, chunks - 1, *range(1, chunks - 1)]
    source_copy = pltpu.make_async_copy(source_ref, source, source_sem)
    copies = {}
    for c in order:
        copies[c] = pltpu.make_async_copy(coup_ref.at[:, :, :, spans[c]], coup.at[c], sems.at[c])
        copies[c].start()
        if c == order[0]:
            source_copy.start()
    lane = lax.broadcasted_iota(jnp.int32, (BW, LANES), 1)
    moved = pltpu.roll(x_ref[...], rim, 1)
    head = jnp.where(lane < rim, 0.0, moved[:, :LANES])
    tail = jnp.where(lane < rim, moved[:, :LANES], 0.0)
    terms[:BW], terms[BW:] = split(jnp.concatenate([head, moved[:, LANES:], tail], axis=1))
    rows = lax.broadcasted_iota(jnp.int32, (2 * LANES, LANES), 0)

    pairs = range(0, slots, 2)

    def gather(c, m):
        window = slice(c * LANES, (c + 2) * LANES)
        table = jnp.concatenate(
            [onehot(rows == nbr_ref[i : i + 1, spans[c]] - c * LANES) for i in (m, m + 1)], axis=1
        )
        both = jnp.dot(terms[:, window], table, preferred_element_type=jnp.float32)
        near[c][:, m * LANES : (m + 2) * LANES] = both[:BW] + both[BW:]

    for m in pairs:
        gather(order[0], m)
    if at_start is not None:
        at_start()
    for step, c in enumerate(order):
        copies[c].wait()
        if step == 0:
            source_copy.wait()
        ahead = list(pairs) if step + 1 < chunks else []
        for at in range(0, CELLS, PACK):
            if ahead:
                gather(order[step + 1], ahead.pop(0))
            if with_ends is not None and step in (1, 2) and (at < CELLS // 2) == (step == 1):
                with_ends(at)
            total = [None] * VARS
            for m in range(slots):
                for v in range(VARS):
                    span = slice(v * CELLS + at, v * CELLS + at + PACK)
                    value = near[c][span, m * LANES : (m + 1) * LANES]
                    for u in range(VARS):
                        term = coup[c, m, u, span, :].astype(jnp.float32) * value
                        total[u] = term if total[u] is None else total[u] + term
            for u in range(VARS):
                span = slice(u * CELLS + at, u * CELLS + at + PACK)
                out_ref[span, spans[c]] = source[span, spans[c]] - x_ref[span, spans[c]] + total[u]


def first_local_kernel(
    rim, x_ref, nbr_ref, coup_ref, source_ref, dst_ref, weight_ref,
    out_ref, rimcoup_ref, rimrow_ref, table_ref, weight_out,
    terms, near, coup, source, sems, source_sem,
):
    slots, blocks = nbr_ref.shape
    chunks = blocks // LANES
    fringe = dst_ref.shape[1]
    lane = lax.broadcasted_iota(jnp.int32, (PACK, LANES), 1)
    first = lane < LANES // 2
    masks = [lax.rem(lane + rim + LANES - m * 2 * rim, LANES) < 2 * rim for m in range(slots)]

    def merged(ends, nothing):
        result = nothing
        for m in range(slots):
            both = jnp.where(first, *ends(m))
            if m > 0:
                both = pltpu.roll(both, m * 2 * rim, 1)
            result = jnp.where(masks[m], both, result)
        return result

    def rows(m):
        lower = jnp.broadcast_to(nbr_ref[m : m + 1, :LANES], (PACK, LANES))
        upper = jnp.broadcast_to(nbr_ref[m : m + 1, blocks - LANES :], (PACK, LANES))
        return jnp.where(lower < rim, lower, -LANES), jnp.where(upper >= blocks + rim, upper - blocks, -LANES)

    def tables():
        rimrow_ref[...] = merged(rows, jnp.full((PACK, LANES), -LANES, jnp.int32))
        weight_out[...] = weight_ref[...]
        targets = jnp.broadcast_to(dst_ref[...], (LANES, fringe)).T
        for c in range(chunks):
            table_ref[:, c * LANES : (c + 1) * LANES] = onehot(targets == lane[:1] + c * LANES)

    def rim_coupling(at):
        for u in range(VARS):
            for v in range(VARS):
                span = slice(v * CELLS + at, v * CELLS + at + PACK)
                rimcoup_ref[u, span, :] = merged(
                    lambda m: (coup[0, m, u, span, :], coup[chunks - 1, m, u, span, :]),
                    jnp.zeros((PACK, LANES), jnp.bfloat16),
                )

    local_kernel(
        rim, x_ref, nbr_ref, coup_ref, source_ref, out_ref, terms, near, coup, source, sems, source_sem,
        tables, rim_coupling,
    )


def full_residual(order, local_ref, inc_ref, lower_ref, upper_ref, table_ref, weight_ref, rimcoup_ref, rimrow_ref):
    rim = lower_ref.shape[0]
    blocks = local_ref.shape[1]
    rims = jnp.concatenate(
        [lower_ref[...], upper_ref[...], jnp.zeros((LANES - 2 * rim, BW), jnp.float32)], axis=0
    ).T
    high, low = split(rims)
    low = pltpu.roll(low.astype(jnp.float32), 2 * rim, 1)
    rims = (high.astype(jnp.float32) + low).astype(jnp.bfloat16)
    sub = lax.broadcasted_iota(jnp.int32, (LANES, LANES), 0)
    row = rimrow_ref[:1]
    reads = onehot((sub == row) | (sub == row + 2 * rim))
    near = jnp.dot(rims, reads, preferred_element_type=jnp.float32)
    edge = []
    for u in range(VARS):
        total = None
        for v in range(VARS):
            span = slice(v * CELLS, (v + 1) * CELLS)
            term = rimcoup_ref[u, span, :].astype(jnp.float32) * near[span]
            total = term if total is None else total + term
        edge.append(total)
    edge = jnp.concatenate(edge, axis=0)
    shift = LANES // 2
    while shift >= 2 * rim:
        edge = edge + pltpu.roll(edge, shift, 1)
        shift //= 2
    lane = lax.broadcasted_iota(jnp.int32, (BW, LANES), 1)
    inc = jnp.concatenate([inc_ref[i : i + 1] for i in np.argsort(order).tolist()], axis=0)
    rest = inc[:, 4]
    rest = jnp.concatenate([rest[:, :, :CELLS], rest[:, :, CELLS:]], axis=1).reshape(-1, CELLS)
    fringe = [inc[:, 0:2].reshape(-1, LANES).T, inc[:, 2:4].reshape(-1, LANES).T, rest.T]
    total = local_ref[...] + pick(jnp.concatenate(fringe, axis=0) * weight_ref[...], table_ref[...])
    lower = total[:, :LANES] + jnp.where(lane < rim, edge, 0.0)
    upper = total[:, blocks - LANES :] + jnp.where(lane >= LANES - rim, edge, 0.0)
    return jnp.concatenate([lower, total[:, LANES : blocks - LANES], upper], axis=1)


def precondition(diag_ref, resid_ref, u, at):
    total = None
    for v in range(VARS):
        span = pl.ds(v * CELLS + at, PACK)
        term = diag_ref[u, span, :].astype(jnp.float32) * resid_ref[span, :]
        total = term if total is None else total + term
    return total


def lane_sums(resid):
    square = jnp.sum(resid * resid, axis=0, keepdims=True)
    return sum(square[:, i : i + LANES] for i in range(0, square.shape[1], LANES))


def advance_kernel(
    order, local_ref, inc_ref, lower_ref, upper_ref, across_ref, weight_ref, rimcoup_ref, rimrow_ref,
    diag_ref, x_ref, table_ref, select_ref,
    next_ref, norm_ref, out_ref, up_ref, down_ref, resid, diag, diag_sem, rows_ref, sem,
):
    fetch = pltpu.make_async_copy(diag_ref, diag, diag_sem)
    fetch.start()
    resid[...] = full_residual(
        order, local_ref, inc_ref, lower_ref, upper_ref, across_ref, weight_ref, rimcoup_ref, rimrow_ref
    )
    fetch.wait()
    for u in range(VARS):
        for at in range(0, CELLS, PACK):
            total = None
            for v in range(VARS):
                span = slice(v * CELLS + at, v * CELLS + at + PACK)
                term = diag[u, span].astype(jnp.float32) * resid[span]
                total = term if total is None else total + term
            span = slice(u * CELLS + at, u * CELLS + at + PACK)
            next_ref[span, :] = x_ref[span, :] + STEP_CFL * total
    copy = send_blocks(
        order, next_ref[...], table_ref[...], select_ref[...], out_ref, up_ref, down_ref, rows_ref, sem
    )
    norm_ref[...] = lane_sums(resid[...])
    copy.wait()


def residual_kernel(
    order, local_ref, inc_ref, lower_ref, upper_ref, across_ref, weight_ref, rimcoup_ref, rimrow_ref, norm_ref,
    resid_ref, sums_ref,
):
    resid = full_residual(
        order, local_ref, inc_ref, lower_ref, upper_ref, across_ref, weight_ref, rimcoup_ref, rimrow_ref
    )
    resid_ref[...] = resid
    both = jnp.concatenate([norm_ref[...], lane_sums(resid)], axis=0)
    sums_ref[...] = jnp.broadcast_to(both[None], sums_ref.shape)


def direction_kernel(diag_ref, resid_ref, out_ref, resid_out):
    resid_out[...] = resid_ref[...]

    def cells(part, carry):
        at = pl.multiple_of(part * PACK, PACK)
        for u in range(VARS):
            out_ref[pl.ds(u * CELLS + at, PACK), :] = precondition(diag_ref, resid_ref, u, at)
        return carry

    lax.fori_loop(0, CELLS // PACK, cells, 0)


def finish_kernel(entries, sums_ref, x_ref, update_ref, out_ref):
    sums = jnp.sum(jnp.sum(sums_ref[...], axis=0), axis=1, keepdims=True) / entries + 1e-06
    cfl = STEP_CFL * jnp.sqrt(sums[0:1] / sums[1:2])
    out_ref[...] = x_ref[...] + cfl * update_ref[...]


VMEM = pl.BlockSpec(memory_space=pltpu.VMEM)
SMEM = pl.BlockSpec(memory_space=pltpu.SMEM)


def f32(*shape):
    return jax.ShapeDtypeStruct(shape, jnp.float32)


def bf16(*shape):
    return jax.ShapeDtypeStruct(shape, jnp.bfloat16)


def call(kernel, in_specs, out_shape, flops, moved, **more):
    many = isinstance(out_shape, (list, tuple))
    return pl.pallas_call(
        kernel,
        in_specs=in_specs,
        out_specs=more.pop("out_specs", [VMEM] * len(out_shape) if many else VMEM),
        out_shape=out_shape,
        compiler_params=pltpu.CompilerParams(vmem_limit_bytes=VMEM_LIMIT),
        cost_estimate=pl.CostEstimate(flops=flops, bytes_accessed=moved, transcendentals=0),
        **more,
    )


def message_order(bodies, peers):
    middle = peers // 2
    far_first = sorted(range(peers), key=lambda k: -abs(2 * k + 1 - peers))
    order = [(j + i) % bodies * peers + k for j in reversed(range(bodies)) for i, k in enumerate(far_first)]
    order.remove(middle)
    return [middle, *order]


def shards(
    psi_init, source, coupling, diag_inv, neighbours, seam_perm, fringe_src, fringe_dst, fringe_weight
):
    blocks = psi_init.shape[0]
    slots = neighbours.shape[1]
    rim = seam_perm.shape[1]
    fringe = fringe_src.shape[1]
    peers = lax.axis_size("blk")
    devices = lax.axis_size("body") * peers
    order = message_order(devices // peers, peers)
    up = [(i, (i + 1) % peers) for i in range(peers)]
    down = [(j, i) for i, j in up]
    here = functools.partial(pltpu.with_memory_space_constraint, memory_space=pltpu.HBM)
    x = here(psi_init.T)
    source_t = here(source.T)
    coup = here(coupling.transpose(1, 2, 3, 0))
    diag = here(diag_inv.transpose(1, 2, 0))
    nbr = here(neighbours.T)
    state = f32(BW, blocks)
    hbm = pl.BlockSpec(memory_space=pltpu.HBM)
    message = (devices, BW * fringe // devices // (rim // 2 * LANES), rim // 2, LANES)
    sent = [f32(*message), f32(rim, BW), f32(rim, BW)]
    rows_scratch = [pltpu.VMEM(message, jnp.float32), pltpu.SemaphoreType.DMA]
    size = 4 * BW * blocks

    donors = call(
        functools.partial(donors_kernel, order),
        [VMEM, VMEM, SMEM],
        sent + [bf16(blocks, fringe), bf16(2 * LANES, LANES), state],
        4 * BW * blocks * fringe,
        2 * size,
        out_specs=[hbm] + [VMEM] * 5,
        scratch_shapes=rows_scratch,
    )
    chunks = blocks // LANES
    scratch = [
        pltpu.VMEM((2 * BW, blocks + LANES), jnp.bfloat16),
        [pltpu.VMEM((BW, slots * LANES), jnp.float32)] * chunks,
        pltpu.VMEM((chunks, slots, VARS, BW, LANES), jnp.bfloat16),
        pltpu.VMEM((BW, blocks), jnp.float32),
        pltpu.SemaphoreType.DMA((chunks,)),
        pltpu.SemaphoreType.DMA,
    ]
    local_more = dict(
        flops=4 * BW * 2 * LANES * slots * blocks,
        moved=coup.size * 2 + 4 * size,
        scratch_shapes=scratch,
    )
    first_local = call(
        functools.partial(first_local_kernel, rim),
        [VMEM, VMEM, hbm, hbm, VMEM, VMEM],
        [
            state,
            bf16(VARS, BW, LANES),
            jax.ShapeDtypeStruct((PACK, LANES), jnp.int32),
            bf16(fringe, blocks),
            f32(1, fringe),
        ],
        **local_more,
    )
    local = call(functools.partial(local_kernel, rim), [VMEM, VMEM, hbm, hbm], state, **local_more)
    advance = call(
        functools.partial(advance_kernel, order),
        [VMEM] * 8 + [hbm] + [VMEM] * 3,
        [state, f32(1, LANES)] + sent,
        8 * BW * blocks * fringe,
        diag.size * 2 + 4 * size,
        out_specs=[VMEM, VMEM, hbm, VMEM, VMEM],
        scratch_shapes=[
            pltpu.VMEM((BW, blocks), jnp.float32),
            pltpu.VMEM((VARS, BW, blocks), jnp.bfloat16),
            pltpu.SemaphoreType.DMA,
        ]
        + rows_scratch,
    )
    residual = call(
        functools.partial(residual_kernel, order),
        [VMEM] * 9,
        [state, f32(devices, 2, LANES)],
        4 * BW * blocks * fringe,
        3 * size,
    )
    direction = call(
        direction_kernel, [VMEM] * 2, [state, state], diag.size * 2, diag.size * 2 + 2 * size
    )
    finish = call(
        functools.partial(finish_kernel, float(blocks * devices * BW)),
        [VMEM] * 3,
        state,
        2 * BW * blocks,
        3 * size,
    )

    everyone = functools.partial(
        lax.all_to_all,
        axis_name=("body", "blk"),
        split_axis=0,
        concat_axis=0,
        tiled=True,
        axis_index_groups=[order],
    )

    def exchange(rows, to_up, to_down):
        rows = everyone(rows)
        return rows, lax.ppermute(to_up, "blk", up), lax.ppermute(to_down, "blk", down)

    *out, table, select, x_here = donors(x, here(fringe_src), here(seam_perm))
    arrived = exchange(*out)
    part, rimcoup, rimrow, across, weight = first_local(
        x_here, nbr, coup, source_t, here(fringe_dst), here(fringe_weight)
    )
    across = (across, weight, rimcoup, rimrow)
    x, norm, *out = advance(part, *arrived, *across, diag, x_here, table, select)
    arrived = exchange(*out)
    part = local(x, nbr, coup, source_t)
    resid, sums = residual(part, *arrived, *across, norm)
    sums = everyone(sums)
    update, resid = direction(diag, resid)
    x = finish(sums, x, update)
    return (x.T, resid.T)


def solution(mesh):
    return jax.shard_map(
        shards,
        mesh=mesh,
        in_specs=(
            P(("body", "blk"), None),
            P(("body", "blk"), None),
            P(("body", "blk"), None, None, None),
            P(("body", "blk"), None, None),
            P(("body", "blk"), None),
            P("body", None),
            P(("body", "blk"), None),
            P(("body", "blk"), None),
            P(("body", "blk"), None),
        ),
        out_specs=(P(("body", "blk"), None), P(("body", "blk"), None)),
        check_vma=False,
    )
```
